256 devices in a mesh: gx: 32 (over x, z), gz: 8 (over y, core).
Axes of the slice: x: 4, y: 4, z: 8, core: 2. Of those that a mesh axis runs over, the one named last changes fastest.
Arguments:
- atom_values: bfloat16 [160, 4, 1048576], P(None, None, ('gx', 'gz')), may hold values from -6 to 6
- atom_cell: int32 [1048576], P(('gx', 'gz')), may hold values from 0 to 511
- brick_column: int32 [2048], P(('gx', 'gz')), may hold values from 0 to 5, as said below
Outputs:
- denoised: bfloat16 [160, 4, 1048576], P(None, None, ('gx', 'gz'))
The draws below stay inside these ranges and needn't reach their ends.
Inputs may be any that keep to these rules, and one draw needn't show every extreme that they name: `brick_column`: the 8 bricks of each device come in order: one or two bricks of column 0, then bricks of columns 1 to 4, then one or two bricks of column 5; the first device has two at each end.
All inputs are finite; a program needn't handle non-finite values.
Results may differ from the reference program's by a relative error of at most 0.00115.
Values may be sent and summed in bfloat16 or wider, within the bound.
No kernel may reach another device: no remote copies, remote signals or barrier semaphores. Data moves between devices by JAX's collectives and lax.ppermute only.
A program may use at most 128 MiB of HBM per device.

```python
import jax
import jax.numpy as jnp
from jax import lax

SNAPS = 160
FIELDS = 4
MODES = 8
SWEEPS = 3
CX = 4
CS = 16
NWALL = 32
BRICK_ATOMS = 512
CW = 512
BRICK_DEV = 8
ATOM_DEV = 4096
NX = 128
NZS = 128
ATOMS = 1048576
BRICKS = 2048
N_GZ = 8


def draw_brick_column(key, part):
    device_count = BRICKS // BRICK_DEV
    key_low, key_high, key_mid = jax.random.split(key, 3)
    low_count = jax.random.randint(key_low, (device_count, 1), 1, 3)
    high_count = jax.random.randint(key_high, (device_count, 1), 1, 3)
    first_row = jnp.arange(device_count)[:, None] == 0
    low_count = jnp.where(first_row, 2, low_count)
    high_count = jnp.where(first_row, 2, high_count)
    position = jnp.arange(BRICK_DEV)[None, :]
    middle = jax.random.randint(key_mid, (device_count, BRICK_DEV), 1, CX + 1)
    column = jnp.where(position < low_count, 0, jnp.where(position >= BRICK_DEV - high_count, CX + 1, middle))
    return column.reshape(BRICKS).astype(jnp.int32)


def touch_ends(array, rng, smallest, top_value):
    index_at = [jax.random.randint(jax.random.fold_in(rng, axis), (), 0, length) for axis, length in enumerate(array.shape)]
    main_axis = array.shape.index(max(array.shape))
    next_to = index_at[:main_axis] + [(index_at[main_axis] + 1) % array.shape[main_axis]] + index_at[main_axis + 1:]
    return array.at[tuple(index_at)].set(smallest).at[tuple(next_to)].set(top_value)


def level_of(key, shape, shards, smallest, top_value):
    def one(axis_at, shards_of):
        heights = jax.random.uniform(jax.random.fold_in(jax.random.fold_in(key, 6), axis_at), (shards_of,), jnp.float32, smallest / len(shards), top_value / len(shards))
        return jnp.repeat(jnp.exp(heights), shape[axis_at] // shards_of).reshape((-1,) + (1,) * (len(shape) - axis_at - 1))

    level = one(*shards[0])
    for cut in shards[1:]:
        level = level * one(*cut)
    return level


def gaussian(stream_key, extent, width, most, pieces=(), kind=jnp.bfloat16):
    drawn = width * jax.random.normal(stream_key, extent, jnp.float32)
    if pieces:
        drawn = drawn * level_of(stream_key, extent, pieces, -0.22, 0.18)
    return jnp.clip(drawn, -most, most).astype(kind)


def setup_inputs(seed: int = 0) -> dict:
    key_of = jax.random.split(jax.random.key(seed), 4)
    return {
        "atom_values": gaussian(key_of[0], (SNAPS, FIELDS, ATOMS), 1.0, 6.0, ((2, 256),)),
        "atom_cell": touch_ends(jax.random.randint(key_of[1], (ATOMS,), 0, CW), jax.random.fold_in(key_of[1], 1), 0, CW - 1).astype(jnp.int32),
        "brick_column": draw_brick_column(jax.random.fold_in(key_of[3], 71), 0),
    }


def normalize(basis):
    inner_gram = jnp.dot(basis.T, basis, precision=lax.Precision.HIGHEST)
    factor = jnp.linalg.cholesky(inner_gram)
    return lax.linalg.triangular_solve(factor, basis, left_side=False, lower=True, transpose_a=True)

def build_projector(gram):
    basis = gram[:, :MODES]
    for sweep in range(SWEEPS):
        basis = jnp.dot(gram, basis, precision=lax.Precision.HIGHEST)
        basis = normalize(basis)
    return jnp.dot(basis, basis.T, precision=lax.Precision.HIGHEST)

def reference(atom_values, atom_cell, brick_column):
    atom_ids = jnp.arange(ATOMS, dtype=jnp.int32)
    block_ids = atom_ids // ATOM_DEV
    stream_block = block_ids // N_GZ
    span_block = block_ids % N_GZ
    column = brick_column[atom_ids // BRICK_ATOMS]
    stream_cell = (stream_block * CX + column - 1) % NX
    span_cell = atom_cell // NWALL
    wall_cell = atom_cell % NWALL
    flattened = ((stream_cell * NZS + span_block * CS + span_cell) * NWALL + wall_cell).astype(jnp.int32)
    cell_total = NX * NZS * NWALL

    def bin_snapshot(snapshot):
        return jax.ops.segment_sum(snapshot.astype(jnp.float32).T, flattened, num_segments=cell_total).T
    cells = lax.map(bin_snapshot, atom_values)
    matrix = cells.reshape(SNAPS, FIELDS * cell_total)
    gram = jnp.dot(matrix, matrix.T, precision=lax.Precision.HIGHEST)
    projector = build_projector(gram)

    def rebuild(proj_row):
        row_fields = jnp.dot(proj_row[None, :], matrix, precision=lax.Precision.HIGHEST)
        return row_fields.reshape(FIELDS, cell_total)[:, flattened].astype(jnp.bfloat16)
    return lax.map(rebuild, projector)
```

```python
import jax
import jax.numpy as jnp
from jax import lax
from jax.experimental import pallas as pl
from jax.experimental.pallas import tpu as pltpu
from jax.sharding import PartitionSpec as P

SNAPS = 160
FIELDS = 4
ROWS = SNAPS * FIELDS
MODES = 8
SWEEPS = 3
CX = 4
EXT = CX + 2
CW = 512
PER_BRICK = 512
BRICKS = 8
COEFS = MODES * FIELDS
SPLIT = 128
TAIL = SNAPS - SPLIT
LANES = CW // 128
F32 = jnp.float32
BF16 = jnp.bfloat16
NT = (((1,), (1,)), ((), ()))
TN = (((0,), (0,)), ((), ()))


def params(mib):
    return pltpu.CompilerParams(vmem_limit_bytes=mib * 1024 * 1024)


def dot_nt(a, b):
    return lax.dot_general(a, b, NT, preferred_element_type=F32)


def dot(a, b):
    return jnp.dot(a, b, preferred_element_type=F32)


def exact_dot(a, b):
    return jnp.dot(a, b, precision=lax.Precision.HIGHEST, preferred_element_type=F32)


def cell_hot(cell_ref, brick):
    cells = lax.broadcasted_iota(jnp.int32, (CW, PER_BRICK), 0)
    return (cells == cell_ref[pl.ds(brick, 1), :]).astype(F32).astype(BF16)


def brick_sums(values_ref, cell_ref, brick):
    values = values_ref[...].reshape(ROWS, PER_BRICK)
    return dot_nt(values, cell_hot(cell_ref, brick))


def halves(x):
    head = x.astype(BF16)
    return head, (x - head.astype(F32)).astype(BF16)


def add_lanes(total, sums):
    for t in range(LANES):
        total[t] += sums[:, t * 128 : (t + 1) * 128]


def one_field(total, field):
    rows = pl.ds(field, SNAPS, stride=FIELDS)
    return jnp.concatenate([total[t, rows, :] for t in range(LANES)], axis=1)


def face_brick(step):
    return jnp.where(step < 2, step, step + BRICKS - 4)


def faces_kernel(column_ref, values_ref, cell_ref, low_ref, high_ref, total):
    step = pl.program_id(0)
    brick = face_brick(step)
    column = column_ref[brick]

    @pl.when(step % 2 == 0)
    def _():
        total[...] = jnp.zeros_like(total)

    @pl.when((column == 0) | (column == EXT - 1))
    def _():
        add_lanes(total, brick_sums(values_ref, cell_ref, brick))

    def store(out_ref):
        for f in range(FIELDS):
            out_ref[f * SNAPS : (f + 1) * SNAPS, :] = one_field(total, f).astype(BF16)

    @pl.when(step == 1)
    def _():
        store(low_ref)

    @pl.when(step == 3)
    def _():
        store(high_ref)


def face_sums(values, cells, columns):
    shape = jax.ShapeDtypeStruct((ROWS, CW), BF16)
    whole = pl.BlockSpec((ROWS, CW), lambda i, c: (0, 0))
    return pl.pallas_call(
        faces_kernel,
        grid_spec=pltpu.PrefetchScalarGridSpec(
            num_scalar_prefetch=1,
            grid=(4,),
            in_specs=[
                pl.BlockSpec((SNAPS, FIELDS, PER_BRICK), lambda i, c: (0, 0, face_brick(i))),
                pl.BlockSpec((BRICKS, PER_BRICK), lambda i, c: (0, 0)),
            ],
            out_specs=[whole, whole],
            scratch_shapes=[pltpu.VMEM((LANES, ROWS, 128), F32)],
        ),
        out_shape=[shape, shape],
        compiler_params=params(32),
        name="faces",
    )(columns, values, cells)


def local_kernel(column_ref, values_ref, cell_ref, after_ref, head_ref, rest_ref, gram_ref, total):
    step = pl.program_id(0)

    @pl.when(step == 0)
    def _():
        total[...] = jnp.zeros_like(total)

    add_lanes(total.at[column_ref[step]], brick_sums(values_ref, cell_ref, step))

    @pl.when(step == BRICKS - 1)
    def _():
        same = jnp.zeros((SNAPS, SNAPS), F32)
        mixed = jnp.zeros((SNAPS, SNAPS), F32)
        for k in range(EXT):
            for f in range(FIELDS):
                head, rest = halves(one_field(total.at[k], f))
                head_ref[f * SNAPS : (f + 1) * SNAPS, k * CW : (k + 1) * CW] = head
                rest_ref[f * SNAPS : (f + 1) * SNAPS, k * CW : (k + 1) * CW] = rest
                same += dot_nt(head, head)
                mixed += dot_nt(head, rest)
        gram_ref[...] = same + mixed + mixed.T


def local_sums(values, cells, columns, after):
    half = jax.ShapeDtypeStruct((ROWS, EXT * CW), BF16)
    half_spec = pl.BlockSpec((ROWS, EXT * CW), lambda i, c: (0, 0))
    return pl.pallas_call(
        local_kernel,
        grid_spec=pltpu.PrefetchScalarGridSpec(
            num_scalar_prefetch=1,
            grid=(BRICKS,),
            in_specs=[
                pl.BlockSpec((SNAPS, FIELDS, PER_BRICK), lambda i, c: (0, 0, i)),
                pl.BlockSpec((BRICKS, PER_BRICK), lambda i, c: (0, 0)),
                pl.BlockSpec((16, 128), lambda i, c: (0, 0)),
            ],
            out_specs=[half_spec, half_spec, pl.BlockSpec((SNAPS, SNAPS), lambda i, c: (0, 0))],
            scratch_shapes=[pltpu.VMEM((EXT, LANES, ROWS, 128), F32)],
        ),
        out_shape=[half, half, jax.ShapeDtypeStruct((SNAPS, SNAPS), F32)],
        compiler_params=params(48),
        cost_estimate=pl.CostEstimate(flops=6_000_000_000, bytes_accessed=14_000_000, transcendentals=0),
        name="local",
    )(columns, values, cells, after)


def pack(gram):
    body = gram[:SPLIT, :SPLIT]
    side = gram[:SPLIT, SPLIT:]
    corner = gram[SPLIT:, SPLIT:]
    t = TAIL
    rows = [
        body[:t],
        jnp.concatenate([side[:t], body[t : 2 * t, t:]], axis=1),
        jnp.concatenate([side[t : 2 * t], side[2 * t : 3 * t], body[2 * t : 3 * t, 2 * t :]], axis=1),
        jnp.concatenate([side[3 * t :], corner, corner, body[3 * t :, 3 * t :]], axis=1),
    ]
    return jnp.concatenate(rows, axis=0)


def unpack(packed):
    t = TAIL
    row = lax.broadcasted_iota(jnp.int32, (SPLIT, SPLIT), 0) // t
    col = lax.broadcasted_iota(jnp.int32, (SPLIT, SPLIT), 1) // t
    above = jnp.where(col > row, packed, 0.0)
    body = jnp.where(col == row, packed, 0.0) + above + above.T
    side = jnp.concatenate(
        [packed[t : 2 * t, :t], packed[2 * t : 3 * t, :t], packed[2 * t : 3 * t, t : 2 * t], packed[3 * t :, :t]], axis=0
    )
    corner = packed[3 * t :, t : 2 * t]
    top = jnp.concatenate([body, side], axis=1)
    padded = jnp.concatenate([side, jnp.zeros((SPLIT, SPLIT - t), F32)], axis=1)
    bottom = jnp.concatenate([padded.T[:t], corner], axis=1)
    return jnp.concatenate([top, bottom], axis=0)


def cross_kernel(gram_ref, low_head, low_rest, high_head, high_rest, from_below, from_above, packed_ref):
    cross = jnp.zeros((SNAPS, SNAPS), F32)
    for f in range(FIELDS):
        rows = slice(f * SNAPS, (f + 1) * SNAPS)
        below, above = from_below[rows, :], from_above[rows, :]
        cross += dot_nt(low_head[rows, :], below) + dot_nt(low_rest[rows, :], below)
        cross += dot_nt(high_head[rows, :], above) + dot_nt(high_rest[rows, :], above)
    packed_ref[...] = pack(gram_ref[...] + cross + cross.T)


def packed_gram(gram, head, rest, from_below, from_above):
    first = pl.BlockSpec((ROWS, CW), lambda i: (0, 1))
    last = pl.BlockSpec((ROWS, CW), lambda i: (0, CX))
    face = pl.BlockSpec((ROWS, CW), lambda i: (0, 0))
    return pl.pallas_call(
        cross_kernel,
        grid=(1,),
        in_specs=[pl.BlockSpec((SNAPS, SNAPS), lambda i: (0, 0)), first, first, last, last, face, face],
        out_specs=pl.BlockSpec((SPLIT, SPLIT), lambda i: (0, 0)),
        out_shape=jax.ShapeDtypeStruct((SPLIT, SPLIT), F32),
        compiler_params=params(32),
        name="cross",
    )(gram, head, rest, head, rest, from_below, from_above)


def add_over_devices(x):
    def along(axis, pairs):
        return lambda y: lax.ppermute(y, axis, pairs)

    def y_pairs(move):
        return [(i, move(i // 2) * 2 + i % 2) for i in range(8)]

    def x_pairs(move):
        return [(i, move(i // 8) * 8 + i % 8) for i in range(32)]

    def z_pairs(move):
        return [(i, (i // 8) * 8 + move(i % 8)) for i in range(32)]

    x = x + along("gz", [(i, i ^ 1) for i in range(8)])(x)
    for axis, pairs in (("gz", y_pairs), ("gx", x_pairs)):
        x = x + along(axis, pairs(lambda i: i ^ 1))(x)
        x = x + along(axis, pairs(lambda i: 3 - i))(x)
    above = along("gx", z_pairs(lambda i: (i - 1) % 8))(x)
    below = along("gx", z_pairs(lambda i: (i + 1) % 8))(x)
    two = x + above
    three = two + below
    far_above = along("gx", z_pairs(lambda i: (i - 3) % 8))(three)
    far_below = along("gx", z_pairs(lambda i: (i + 3) % 8))(two)
    return three + far_above + far_below


def orthonormal(basis):
    inner = lax.dot_general(basis, basis, NT, precision=lax.Precision.HIGHEST, preferred_element_type=F32)
    row = lax.broadcasted_iota(jnp.int32, (MODES, 1), 0)
    square = lax.broadcasted_iota(jnp.int32, (MODES, MODES), 0) == lax.broadcasted_iota(jnp.int32, (MODES, MODES), 1)
    for j in range(MODES - 1):
        factor = jnp.where(row > j, inner[:, j : j + 1] / inner[j : j + 1, j : j + 1], 0.0)
        inner = inner - factor * inner[j : j + 1, :]
        basis = basis - factor * basis[j : j + 1, :]
    pivots = jnp.sum(jnp.where(square, inner, 0.0), axis=1, keepdims=True)
    return basis * lax.rsqrt(pivots)


def coefs_kernel(packed_ref, head_ref, rest_ref, basis_ref, own_ref, down_ref, up_ref):
    gram = unpack(packed_ref[...])
    basis = gram[:MODES, :]
    for _ in range(SWEEPS):
        basis = orthonormal(exact_dot(basis, gram))
    basis_ref[...] = basis
    wide = jnp.concatenate([basis] * FIELDS, axis=1)
    tall = jnp.concatenate([wide] * FIELDS, axis=0)
    row_field = lax.broadcasted_iota(jnp.int32, (COEFS, ROWS), 0) // MODES
    col_field = lax.broadcasted_iota(jnp.int32, (COEFS, ROWS), 1) // SNAPS
    head, rest = halves(jnp.where(row_field == col_field, tall, 0.0))
    both = jnp.concatenate([head, rest], axis=0)
    for k in range(EXT):
        columns = slice(k * CW, (k + 1) * CW)
        pair = dot(both, head_ref[:, columns])
        own_ref[:, columns] = pair[:COEFS] + pair[COEFS:] + dot(head, rest_ref[:, columns])
    down_ref[...] = own_ref[:, : 2 * CW]
    up_ref[...] = own_ref[:, CX * CW :]


def coefficients(packed, head, rest):
    side = jax.ShapeDtypeStruct((COEFS, 2 * CW), F32)
    return pl.pallas_call(
        coefs_kernel,
        out_shape=[
            jax.ShapeDtypeStruct((MODES, SNAPS), F32),
            jax.ShapeDtypeStruct((COEFS, EXT * CW), F32),
            side,
            side,
        ],
        compiler_params=params(48),
        name="coefs",
    )(packed, head, rest)


def spread_kernel(basis_ref, spread_ref):
    head, rest = halves(basis_ref[...])
    snap = lax.broadcasted_iota(jnp.int32, (SNAPS, ROWS), 0)
    column = lax.broadcasted_iota(jnp.int32, (SNAPS, ROWS), 1)
    repeat = (snap == column // FIELDS).astype(F32).astype(BF16)
    both = dot(jnp.concatenate([head, rest], axis=0), repeat)
    field = lax.broadcasted_iota(jnp.int32, (COEFS, ROWS), 0) // MODES
    mine = field == lax.broadcasted_iota(jnp.int32, (COEFS, ROWS), 1) % FIELDS
    head = jnp.where(mine, jnp.concatenate([both[:MODES]] * FIELDS, axis=0), 0.0)
    rest = jnp.where(mine, jnp.concatenate([both[MODES:]] * FIELDS, axis=0), 0.0)
    stacked = jnp.concatenate([head, head, rest, jnp.zeros_like(rest)], axis=0)
    spread_ref[...] = stacked.T.astype(BF16)


def spread_matrix(basis):
    return pl.pallas_call(
        spread_kernel,
        out_shape=jax.ShapeDtypeStruct((ROWS, 4 * COEFS), BF16),
        name="spread",
    )(basis)


def atoms_kernel(column_ref, own_ref, below_ref, above_ref, spread_ref, cell_ref, out_ref, whole):
    step = pl.program_id(0)

    @pl.when(step == 0)
    def _():
        for k in range(EXT):
            value = own_ref[:, k * CW : (k + 1) * CW]
            if k < 2:
                value = value + below_ref[:, k * CW : (k + 1) * CW]
            if k >= CX:
                value = value + above_ref[:, (k - CX) * CW : (k - CX + 1) * CW]
            head, rest = halves(value)
            whole[k] = jnp.concatenate([head, rest], axis=0)

    picked = dot(whole[column_ref[step]], cell_hot(cell_ref, step)).astype(BF16)
    stacked = jnp.concatenate([picked, picked[:COEFS], jnp.zeros((COEFS, PER_BRICK), BF16)], axis=0)
    out_ref[...] = dot(spread_ref[...], stacked).astype(BF16).reshape(SNAPS, FIELDS, PER_BRICK)


def atom_fields(columns, own, below, above, spread, cells):
    side = pl.BlockSpec((COEFS, 2 * CW), lambda i, c: (0, 0))
    return pl.pallas_call(
        atoms_kernel,
        grid_spec=pltpu.PrefetchScalarGridSpec(
            num_scalar_prefetch=1,
            grid=(BRICKS,),
            in_specs=[
                pl.BlockSpec((COEFS, EXT * CW), lambda i, c: (0, 0)),
                side,
                side,
                pl.BlockSpec((ROWS, 4 * COEFS), lambda i, c: (0, 0)),
                pl.BlockSpec((BRICKS, PER_BRICK), lambda i, c: (0, 0)),
            ],
            out_specs=pl.BlockSpec((SNAPS, FIELDS, PER_BRICK), lambda i, c: (0, 0, i)),
            scratch_shapes=[pltpu.VMEM((EXT, 2 * COEFS, CW), BF16)],
        ),
        out_shape=jax.ShapeDtypeStruct((SNAPS, FIELDS, BRICKS * PER_BRICK), BF16),
        compiler_params=params(32),
        name="atoms",
    )(columns, own, below, above, spread, cells)


def on_device(atom_values, atom_cell, brick_column):
    cells = atom_cell.reshape(BRICKS, PER_BRICK)
    count = lax.axis_size("gx")
    to_lower = [((i + 1) % count, i) for i in range(count)]
    to_upper = [(i, (i + 1) % count) for i in range(count)]
    low, high = face_sums(atom_values, cells, brick_column)
    from_above = lax.ppermute(low, "gx", to_lower)
    from_below = lax.ppermute(high, "gx", to_upper)
    head, rest, gram = local_sums(atom_values, cells, brick_column, low)
    packed = add_over_devices(packed_gram(gram, head, rest, from_below, from_above))
    basis, own, down, up = coefficients(packed, head, rest)
    above = lax.ppermute(down, "gx", to_lower)
    below = lax.ppermute(up, "gx", to_upper)
    spread = spread_matrix(basis)
    return atom_fields(brick_column, own, below, above, spread, cells)


def solution(mesh):
    in_specs = (P(None, None, ("gx", "gz")), P(("gx", "gz")), P(("gx", "gz")))
    out_specs = P(None, None, ("gx", "gz"))
    return jax.shard_map(on_device, mesh=mesh, in_specs=in_specs, out_specs=out_specs, check_vma=False)
```

```python
import jax
import jax.numpy as jnp
from jax import lax
from jax.experimental import pallas as pl
from jax.experimental.pallas import tpu as pltpu
from jax.sharding import PartitionSpec as P

SNAPS = 160
FIELDS = 4
ROWS = SNAPS * FIELDS
MODES = 8
SWEEPS = 3
CX = 4
EXT = CX + 2
CW = 512
PER_BRICK = 512
BRICKS = 8
COEFS = MODES * FIELDS
SPLIT = 128
TAIL = SNAPS - SPLIT
LANES = CW // 128
F32 = jnp.float32
BF16 = jnp.bfloat16
NT = (((1,), (1,)), ((), ()))
TN = (((0,), (0,)), ((), ()))


def params(mib):
    return pltpu.CompilerParams(vmem_limit_bytes=mib * 1024 * 1024)


def dot_nt(a, b):
    return lax.dot_general(a, b, NT, preferred_element_type=F32)


def dot(a, b):
    return jnp.dot(a, b, preferred_element_type=F32)


def exact_dot(a, b):
    return jnp.dot(a, b, precision=lax.Precision.HIGHEST, preferred_element_type=F32)


def cell_hot(cells, brick, keep=None):
    ids = lax.broadcasted_iota(jnp.int32, (CW, 128), 0)
    tiles = []
    for t in range(LANES):
        row = cells[brick * LANES + t : brick * LANES + t + 1, :]
        if keep is not None:
            row = jnp.where(keep, row, -1)
        tiles.append((ids == row).astype(F32).astype(BF16))
    return jnp.concatenate(tiles, axis=1)


def halves(x):
    head = x.astype(BF16)
    return head, (x - head.astype(F32)).astype(BF16)


def one_field(total, field):
    rows = pl.ds(field, SNAPS, stride=FIELDS)
    return jnp.concatenate([total[t, rows, :] for t in range(LANES)], axis=1)


def brick_copy(values_hbm, held, sems, brick, slot):
    source = values_hbm.at[:, :, pl.ds(brick * PER_BRICK, PER_BRICK)]
    return pltpu.make_async_copy(source, held.at[slot], sems.at[slot])


HBM = pl.BlockSpec(memory_space=pltpu.HBM)
VMEM = pl.BlockSpec(memory_space=pltpu.VMEM)
SMEM = pl.BlockSpec(memory_space=pltpu.SMEM)


def faces_kernel(values_hbm, cells_hbm, column_hbm, low_ref, high_ref, cells_ref, column_ref, held, total, sems, small):
    bricks = (0, 1, BRICKS - 2, BRICKS - 1)
    ids = pltpu.make_async_copy(cells_hbm, cells_ref, small.at[0])
    columns = pltpu.make_async_copy(column_hbm, column_ref, small.at[1])
    ids.start()
    columns.start()
    copies = [brick_copy(values_hbm, held, sems, brick, slot) for slot, brick in enumerate(bricks)]
    for copy in copies:
        copy.start()
    ids.wait()
    columns.wait()
    for face, (first, out_ref, column) in enumerate(((0, low_ref, 0), (2, high_ref, EXT - 1))):
        sums = None
        for slot in (first, first + 1):
            brick = bricks[slot]
            hot = cell_hot(cells_ref, brick, column_ref[:, brick : brick + 1] == column)
            copies[slot].wait()
            part = dot_nt(held[slot].reshape(ROWS, PER_BRICK), hot)
            sums = part if sums is None else sums + part
        for t in range(LANES):
            total[face, t] = sums[:, t * 128 : (t + 1) * 128]
        for f in range(FIELDS):
            out_ref[f * SNAPS : (f + 1) * SNAPS, :] = one_field(total.at[face], f).astype(BF16)


def face_sums(values, cells, columns):
    shape = jax.ShapeDtypeStruct((ROWS, CW), BF16)
    return pl.pallas_call(
        faces_kernel,
        in_specs=[HBM, HBM, HBM],
        out_specs=[VMEM] * 4,
        scratch_shapes=[
            pltpu.VMEM((4, SNAPS, FIELDS, PER_BRICK), BF16),
            pltpu.VMEM((2, LANES, ROWS, 128), F32),
            pltpu.SemaphoreType.DMA((4,)),
            pltpu.SemaphoreType.DMA((2,)),
        ],
        out_shape=[
            shape,
            shape,
            jax.ShapeDtypeStruct((BRICKS * LANES, 128), jnp.int32),
            jax.ShapeDtypeStruct((1, BRICKS), jnp.int32),
        ],
        compiler_params=params(63),
        name="faces",
    )(values, cells, columns)


def local_kernel(column_ref, values_hbm, cells, head_ref, rest_ref, gram_ref, held, total, sems):
    copies = [brick_copy(values_hbm, held, sems, brick, brick) for brick in range(BRICKS)]
    for copy in copies:
        copy.start()
    total[...] = jnp.zeros_like(total)
    for brick in range(BRICKS):
        hot = cell_hot(cells, brick)
        copies[brick].wait()
        sums = dot_nt(held[brick].reshape(ROWS, PER_BRICK), hot)
        column = column_ref[brick]
        for t in range(LANES):
            total[column, t] += sums[:, t * 128 : (t + 1) * 128]
    same = jnp.zeros((SNAPS, SNAPS), F32)
    mixed = jnp.zeros((SNAPS, SNAPS), F32)
    for k in range(EXT):
        for f in range(FIELDS):
            head, rest = halves(one_field(total.at[k], f))
            head_ref[f * SNAPS : (f + 1) * SNAPS, k * CW : (k + 1) * CW] = head
            rest_ref[f * SNAPS : (f + 1) * SNAPS, k * CW : (k + 1) * CW] = rest
            same += dot_nt(head, head)
            mixed += dot_nt(head, rest)
    gram_ref[...] = same + mixed + mixed.T


def local_sums(values, cells, columns):
    half = jax.ShapeDtypeStruct((ROWS, EXT * CW), BF16)
    return pl.pallas_call(
        local_kernel,
        in_specs=[SMEM, HBM, VMEM],
        out_specs=[VMEM, VMEM, VMEM],
        scratch_shapes=[
            pltpu.VMEM((BRICKS, SNAPS, FIELDS, PER_BRICK), BF16),
            pltpu.VMEM((EXT, LANES, ROWS, 128), F32),
            pltpu.SemaphoreType.DMA((BRICKS,)),
        ],
        out_shape=[half, half, jax.ShapeDtypeStruct((SNAPS, SNAPS), F32)],
        compiler_params=params(44),
        cost_estimate=pl.CostEstimate(flops=6_000_000_000, bytes_accessed=14_000_000, transcendentals=0),
        name="local",
    )(columns, values, cells)


def pack(gram):
    body = gram[:SPLIT, :SPLIT]
    side = gram[:SPLIT, SPLIT:]
    corner = gram[SPLIT:, SPLIT:]
    t = TAIL
    rows = [
        body[:t],
        jnp.concatenate([side[:t], body[t : 2 * t, t:]], axis=1),
        jnp.concatenate([side[t : 2 * t], side[2 * t : 3 * t], body[2 * t : 3 * t, 2 * t :]], axis=1),
        jnp.concatenate([side[3 * t :], corner, corner, body[3 * t :, 3 * t :]], axis=1),
    ]
    return jnp.concatenate(rows, axis=0)


def unpack(packed):
    t = TAIL
    row = lax.broadcasted_iota(jnp.int32, (SPLIT, SPLIT), 0) // t
    col = lax.broadcasted_iota(jnp.int32, (SPLIT, SPLIT), 1) // t
    above = jnp.where(col > row, packed, 0.0)
    body = jnp.where(col == row, packed, 0.0) + above + above.T
    side = jnp.concatenate(
        [packed[t : 2 * t, :t], packed[2 * t : 3 * t, :t], packed[2 * t : 3 * t, t : 2 * t], packed[3 * t :, :t]], axis=0
    )
    corner = packed[3 * t :, t : 2 * t]
    top = jnp.concatenate([body, side], axis=1)
    padded = jnp.concatenate([side, jnp.zeros((SPLIT, SPLIT - t), F32)], axis=1)
    bottom = jnp.concatenate([padded.T[:t], corner], axis=1)
    return jnp.concatenate([top, bottom], axis=0)


def cross_kernel(gram_ref, head_ref, rest_ref, from_below, from_above, packed_ref):
    cross = jnp.zeros((SNAPS, SNAPS), F32)
    for f in range(FIELDS):
        rows = slice(f * SNAPS, (f + 1) * SNAPS)
        for column, received in ((1, from_below), (CX, from_above)):
            lanes = slice(column * CW, (column + 1) * CW)
            other = received[rows, :]
            cross += dot_nt(head_ref[rows, lanes], other) + dot_nt(rest_ref[rows, lanes], other)
    packed_ref[...] = pack(gram_ref[...] + cross + cross.T)


def packed_gram(gram, head, rest, from_below, from_above):
    return pl.pallas_call(
        cross_kernel,
        in_specs=[VMEM] * 5,
        out_specs=VMEM,
        out_shape=jax.ShapeDtypeStruct((SPLIT, SPLIT), F32),
        compiler_params=params(16),
        name="cross",
    )(gram, head, rest, from_below, from_above)


def add_over_devices(x):
    places = [(a, z, y, c) for a in range(4) for z in range(8) for y in range(4) for c in range(2)]
    number = {place: i for i, place in enumerate(places)}

    def move(y, target):
        return lax.ppermute(y, ("gx", "gz"), [(number[place], number[target(*place)]) for place in places])

    def pair(i, step):
        return i ^ 1 if step == 0 else 3 - i

    for turn in range(4):
        step = turn % 2

        def target(a, z, y, c):
            return (a, z, pair(y, step), c) if c == turn // 2 else (pair(a, step), z, y, c)

        x = x + move(x, target)

    def swap(y):
        return move(y, lambda a, z, y, c: (a, z, y, 1 - c))

    first = lax.axis_index("gz") % 2 == 0
    x = x + swap(x)
    near = move(x, lambda a, z, y, c: (a, (z + 2 * c - 1) % 8, y, c))
    other = swap(near)
    two = x + other
    three = two + near
    far = move(jnp.where(first, three, two), lambda a, z, y, c: (a, (z + 6 * c - 3) % 8, y, c))
    return three + far + swap(far)


def orthonormal(basis):
    inner = lax.dot_general(basis, basis, NT, precision=lax.Precision.HIGHEST, preferred_element_type=F32)
    row = lax.broadcasted_iota(jnp.int32, (MODES, 1), 0)
    square = lax.broadcasted_iota(jnp.int32, (MODES, MODES), 0) == lax.broadcasted_iota(jnp.int32, (MODES, MODES), 1)
    for j in range(MODES - 1):
        factor = jnp.where(row > j, inner[:, j : j + 1] / inner[j : j + 1, j : j + 1], 0.0)
        inner = inner - factor * inner[j : j + 1, :]
        basis = basis - factor * basis[j : j + 1, :]
    pivots = jnp.sum(jnp.where(square, inner, 0.0), axis=1, keepdims=True)
    return basis * lax.rsqrt(pivots)


def coefs_kernel(packed_ref, head_ref, rest_ref, basis_ref, own_ref, down_ref, up_ref):
    gram = unpack(packed_ref[...])
    basis = gram[:MODES, :]
    for _ in range(SWEEPS):
        basis = orthonormal(exact_dot(basis, gram))
    basis_ref[...] = basis
    wide = jnp.concatenate([basis] * FIELDS, axis=1)
    tall = jnp.concatenate([wide] * FIELDS, axis=0)
    row_field = lax.broadcasted_iota(jnp.int32, (COEFS, ROWS), 0) // MODES
    col_field = lax.broadcasted_iota(jnp.int32, (COEFS, ROWS), 1) // SNAPS
    head, rest = halves(jnp.where(row_field == col_field, tall, 0.0))
    both = jnp.concatenate([head, rest], axis=0)
    for k in range(EXT):
        columns = slice(k * CW, (k + 1) * CW)
        pair = dot(both, head_ref[:, columns])
        own_ref[:, columns] = pair[:COEFS] + pair[COEFS:] + dot(head, rest_ref[:, columns])
    down_ref[...] = own_ref[:, : 2 * CW]
    up_ref[...] = own_ref[:, CX * CW :]


def coefficients(packed, head, rest):
    side = jax.ShapeDtypeStruct((COEFS, 2 * CW), F32)
    return pl.pallas_call(
        coefs_kernel,
        out_shape=[
            jax.ShapeDtypeStruct((MODES, SNAPS), F32),
            jax.ShapeDtypeStruct((COEFS, EXT * CW), F32),
            side,
            side,
        ],
        in_specs=[VMEM] * 3,
        out_specs=[VMEM] * 4,
        compiler_params=params(16),
        name="coefs",
    )(packed, head, rest)


def spread_kernel(basis_ref, spread_ref):
    head, rest = halves(basis_ref[...])
    snap = lax.broadcasted_iota(jnp.int32, (SNAPS, ROWS), 0)
    column = lax.broadcasted_iota(jnp.int32, (SNAPS, ROWS), 1)
    repeat = (snap == column // FIELDS).astype(F32).astype(BF16)
    both = dot(jnp.concatenate([head, rest], axis=0), repeat)
    field = lax.broadcasted_iota(jnp.int32, (COEFS, ROWS), 0) // MODES
    mine = field == lax.broadcasted_iota(jnp.int32, (COEFS, ROWS), 1) % FIELDS
    head = jnp.where(mine, jnp.concatenate([both[:MODES]] * FIELDS, axis=0), 0.0)
    rest = jnp.where(mine, jnp.concatenate([both[MODES:]] * FIELDS, axis=0), 0.0)
    stacked = jnp.concatenate([head, head, rest, jnp.zeros_like(rest)], axis=0)
    spread_ref[...] = stacked.T.astype(BF16)


def spread_matrix(basis):
    return pl.pallas_call(
        spread_kernel,
        in_specs=[VMEM],
        out_specs=VMEM,
        out_shape=jax.ShapeDtypeStruct((ROWS, 4 * COEFS), BF16),
        compiler_params=params(16),
        name="spread",
    )(basis)


def atoms_kernel(own_ref, below_ref, above_ref, spread_ref, cells, column_ref, out_hbm, held, sems):
    whole = []
    for k in range(EXT):
        value = own_ref[:, k * CW : (k + 1) * CW]
        if k < 2:
            value = value + below_ref[:, k * CW : (k + 1) * CW]
        if k >= CX:
            value = value + above_ref[:, (k - CX) * CW : (k - CX + 1) * CW]
        whole.append(jnp.concatenate(halves(value), axis=0))
    blank = jnp.zeros((COEFS, PER_BRICK), BF16)
    copies = []
    for brick in range(BRICKS):
        column = column_ref[:, brick : brick + 1]
        mine = whole[0]
        for k in range(1, EXT):
            mine = jnp.where(column == k, whole[k], mine)
        picked = dot(mine, cell_hot(cells, brick)).astype(BF16)
        stacked = jnp.concatenate([picked, picked[:COEFS], blank], axis=0)
        fields = dot(spread_ref[...], stacked).astype(BF16)
        held[brick] = fields.reshape(SNAPS, FIELDS, PER_BRICK)
        target = out_hbm.at[:, :, pl.ds(brick * PER_BRICK, PER_BRICK)]
        copy = pltpu.make_async_copy(held.at[brick], target, sems.at[brick])
        copy.start()
        copies.append(copy)
    for copy in copies:
        copy.wait()


def atom_fields(columns, own, below, above, spread, cells):
    return pl.pallas_call(
        atoms_kernel,
        in_specs=[VMEM] * 6,
        out_specs=HBM,
        scratch_shapes=[
            pltpu.VMEM((BRICKS, SNAPS, FIELDS, PER_BRICK), BF16),
            pltpu.SemaphoreType.DMA((BRICKS,)),
        ],
        out_shape=jax.ShapeDtypeStruct((SNAPS, FIELDS, BRICKS * PER_BRICK), BF16),
        compiler_params=params(32),
        name="atoms",
    )(own, below, above, spread, cells, columns)


def on_device(atom_values, atom_cell, brick_column):
    count = lax.axis_size("gx")
    to_lower = [((i + 1) % count, i) for i in range(count)]
    to_upper = [(i, (i + 1) % count) for i in range(count)]
    low, high, cells, columns = face_sums(
        atom_values, atom_cell.reshape(BRICKS * LANES, 128), brick_column.reshape(1, BRICKS)
    )
    from_above = lax.ppermute(low, "gx", to_lower)
    from_below = lax.ppermute(high, "gx", to_upper)
    head, rest, gram = local_sums(atom_values, cells, brick_column)
    packed = add_over_devices(packed_gram(gram, head, rest, from_below, from_above))
    basis, own, down, up = coefficients(packed, head, rest)
    above = lax.ppermute(down, "gx", to_lower)
    below = lax.ppermute(up, "gx", to_upper)
    spread = spread_matrix(basis)
    return atom_fields(columns, own, below, above, spread, cells)


def solution(mesh):
    in_specs = (P(None, None, ("gx", "gz")), P(("gx", "gz")), P(("gx", "gz")))
    out_specs = P(None, None, ("gx", "gz"))
    return jax.shard_map(on_device, mesh=mesh, in_specs=in_specs, out_specs=out_specs, check_vma=False)
```

```python
import jax
import jax.numpy as jnp
from jax import lax
from jax.experimental import pallas as pl
from jax.experimental.pallas import tpu as pltpu
from jax.sharding import PartitionSpec as P

SNAPS = 160
FIELDS = 4
ROWS = SNAPS * FIELDS
MODES = 8
SWEEPS = 3
CX = 4
EXT = CX + 2
CW = 512
PER_BRICK = 512
BRICKS = 8
COEFS = MODES * FIELDS
SPLIT = 128
TAIL = SNAPS - SPLIT
LANES = CW // 128
F32 = jnp.float32
BF16 = jnp.bfloat16
NT = (((1,), (1,)), ((), ()))
TN = (((0,), (0,)), ((), ()))


def params(mib):
    return pltpu.CompilerParams(vmem_limit_bytes=mib * 1024 * 1024)


def dot_nt(a, b):
    return lax.dot_general(a, b, NT, preferred_element_type=F32)


def dot(a, b):
    return jnp.dot(a, b, preferred_element_type=F32)


def exact_dot(a, b):
    return jnp.dot(a, b, precision=lax.Precision.HIGHEST, preferred_element_type=F32)


def cell_hot(cells, brick, keep=None):
    ids = lax.broadcasted_iota(jnp.int32, (CW, 128), 0)
    tiles = []
    for t in range(LANES):
        row = cells[brick * LANES + t : brick * LANES + t + 1, :]
        if keep is not None:
            row = jnp.where(keep, row, -1)
        tiles.append((ids == row).astype(F32).astype(BF16))
    return jnp.concatenate(tiles, axis=1)


def halves(x):
    head = x.astype(BF16)
    return head, (x - head.astype(F32)).astype(BF16)


def one_field(total, field):
    rows = pl.ds(field, SNAPS, stride=FIELDS)
    return jnp.concatenate([total[t, rows, :] for t in range(LANES)], axis=1)


def brick_copy(values_hbm, held, sems, brick, slot):
    source = values_hbm.at[:, :, pl.ds(brick * PER_BRICK, PER_BRICK)]
    return pltpu.make_async_copy(source, held.at[slot], sems.at[slot])


HBM = pl.BlockSpec(memory_space=pltpu.HBM)
VMEM = pl.BlockSpec(memory_space=pltpu.VMEM)
SMEM = pl.BlockSpec(memory_space=pltpu.SMEM)


def faces_kernel(values_hbm, cells_hbm, column_hbm, low_hbm, high_hbm, held, total, face, cells, columns, sems, small, out_sems):
    bricks = (0, 1, BRICKS - 2, BRICKS - 1)
    targets = ((0, low_hbm), (EXT - 1, high_hbm))
    inputs = [
        pltpu.make_async_copy(cells_hbm, cells, small.at[0]),
        pltpu.make_async_copy(column_hbm, columns, small.at[1]),
    ]
    copies = [brick_copy(values_hbm, held, sems, brick, slot) for slot, brick in enumerate(bricks)]
    outputs = [pltpu.make_async_copy(face.at[i], out, out_sems.at[i]) for i, (_, out) in enumerate(targets)]
    for copy in inputs + copies:
        copy.start()
    for copy in inputs:
        copy.wait()
    hots = [
        cell_hot(cells, brick, columns[:, brick : brick + 1] == targets[slot // 2][0]) for slot, brick in enumerate(bricks)
    ]
    for i in range(2):
        sums = None
        for slot in (2 * i, 2 * i + 1):
            copies[slot].wait()
            part = dot_nt(held[slot].reshape(ROWS, PER_BRICK), hots[slot])
            sums = part if sums is None else sums + part
        for t in range(LANES):
            total[i, t] = sums[:, t * 128 : (t + 1) * 128]
        for f in range(FIELDS):
            face[i, f * SNAPS : (f + 1) * SNAPS, :] = one_field(total.at[i], f).astype(BF16)
        outputs[i].start()
    for copy in outputs:
        copy.wait()


def face_sums(values, cells, columns):
    shape = jax.ShapeDtypeStruct((ROWS, CW), BF16)
    return pl.pallas_call(
        faces_kernel,
        in_specs=[HBM] * 3,
        out_specs=[HBM] * 2,
        scratch_shapes=[
            pltpu.VMEM((4, SNAPS, FIELDS, PER_BRICK), BF16),
            pltpu.VMEM((2, LANES, ROWS, 128), F32),
            pltpu.VMEM((2, ROWS, CW), BF16),
            pltpu.VMEM((BRICKS * LANES, 128), jnp.int32),
            pltpu.VMEM((1, BRICKS), jnp.int32),
            pltpu.SemaphoreType.DMA((4,)),
            pltpu.SemaphoreType.DMA((2,)),
            pltpu.SemaphoreType.DMA((2,)),
        ],
        out_shape=[shape, shape],
        compiler_params=params(63),
        name="faces",
    )(values, cells, columns)


def local_kernel(column_ref, values_hbm, cells, after, head_hbm, rest_hbm, face_ref, gram_ref, held, total, heads, rests, sems, out_sems):
    copies = [brick_copy(values_hbm, held, sems, brick, brick) for brick in range(BRICKS)]
    for copy in copies:
        copy.start()
    total[...] = jnp.zeros_like(total)
    for brick in range(BRICKS):
        hot = cell_hot(cells, brick)
        copies[brick].wait()
        sums = dot_nt(held[brick].reshape(ROWS, PER_BRICK), hot)
        column = column_ref[brick]
        for t in range(LANES):
            total[column, t] += sums[:, t * 128 : (t + 1) * 128]
    same = jnp.zeros((SNAPS, SNAPS), F32)
    mixed = jnp.zeros((SNAPS, SNAPS), F32)
    outputs = []
    for k in range(EXT):
        for f in range(FIELDS):
            rows = slice(f * SNAPS, (f + 1) * SNAPS)
            head, rest = halves(one_field(total.at[k], f))
            heads[k, rows, :] = head
            rests[k, rows, :] = rest
            if k in (1, CX):
                face_ref[2 * (k // CX), rows, :] = head
                face_ref[2 * (k // CX) + 1, rows, :] = rest
            same += dot_nt(head, head)
            mixed += dot_nt(head, rest)
        for i, (source, target) in enumerate(((heads, head_hbm), (rests, rest_hbm))):
            outputs.append(pltpu.make_async_copy(source.at[k], target.at[k], out_sems.at[i, k]))
            outputs[-1].start()
    gram_ref[...] = same + mixed + mixed.T
    for copy in outputs:
        copy.wait()


def local_sums(values, cells, columns, after):
    half = jax.ShapeDtypeStruct((EXT, ROWS, CW), BF16)
    return pl.pallas_call(
        local_kernel,
        in_specs=[SMEM, HBM, VMEM, HBM],
        out_specs=[HBM, HBM, VMEM, VMEM],
        scratch_shapes=[
            pltpu.VMEM((BRICKS, SNAPS, FIELDS, PER_BRICK), BF16),
            pltpu.VMEM((EXT, LANES, ROWS, 128), F32),
            pltpu.VMEM((EXT, ROWS, CW), BF16),
            pltpu.VMEM((EXT, ROWS, CW), BF16),
            pltpu.SemaphoreType.DMA((BRICKS,)),
            pltpu.SemaphoreType.DMA((2, EXT)),
        ],
        out_shape=[
            half,
            half,
            jax.ShapeDtypeStruct((4, ROWS, CW), BF16),
            jax.ShapeDtypeStruct((SNAPS, SNAPS), F32),
        ],
        compiler_params=params(50),
        cost_estimate=pl.CostEstimate(flops=6_000_000_000, bytes_accessed=14_000_000, transcendentals=0),
        name="local",
    )(columns, values, cells, after)


def pack(gram):
    body = gram[:SPLIT, :SPLIT]
    side = gram[:SPLIT, SPLIT:]
    corner = gram[SPLIT:, SPLIT:]
    t = TAIL
    rows = [
        body[:t],
        jnp.concatenate([side[:t], body[t : 2 * t, t:]], axis=1),
        jnp.concatenate([side[t : 2 * t], side[2 * t : 3 * t], body[2 * t : 3 * t, 2 * t :]], axis=1),
        jnp.concatenate([side[3 * t :], corner, corner, body[3 * t :, 3 * t :]], axis=1),
    ]
    return jnp.concatenate(rows, axis=0)


def unpack(packed):
    t = TAIL
    row = lax.broadcasted_iota(jnp.int32, (SPLIT, SPLIT), 0) // t
    col = lax.broadcasted_iota(jnp.int32, (SPLIT, SPLIT), 1) // t
    above = jnp.where(col > row, packed, 0.0)
    body = jnp.where(col == row, packed, 0.0) + above + above.T
    side = jnp.concatenate(
        [packed[t : 2 * t, :t], packed[2 * t : 3 * t, :t], packed[2 * t : 3 * t, t : 2 * t], packed[3 * t :, :t]], axis=0
    )
    corner = packed[3 * t :, t : 2 * t]
    top = jnp.concatenate([body, side], axis=1)
    padded = jnp.concatenate([side, jnp.zeros((SPLIT, SPLIT - t), F32)], axis=1)
    bottom = jnp.concatenate([padded.T[:t], corner], axis=1)
    return jnp.concatenate([top, bottom], axis=0)


def cross_kernel(gram_ref, face_ref, from_below, from_above, packed_ref):
    cross = jnp.zeros((SNAPS, SNAPS), F32)
    for f in range(FIELDS):
        rows = slice(f * SNAPS, (f + 1) * SNAPS)
        for i, received in enumerate((from_below, from_above)):
            other = received[rows, :]
            cross += dot_nt(face_ref[2 * i, rows, :], other) + dot_nt(face_ref[2 * i + 1, rows, :], other)
    packed_ref[...] = pack(gram_ref[...] + cross + cross.T)


def packed_gram(gram, faces, from_below, from_above):
    return pl.pallas_call(
        cross_kernel,
        in_specs=[VMEM] * 4,
        out_specs=VMEM,
        out_shape=jax.ShapeDtypeStruct((SPLIT, SPLIT), F32),
        compiler_params=params(16),
        name="cross",
    )(gram, faces, from_below, from_above)


def add_over_devices(x):
    axes = ("gx", "gz")
    depth = 8
    planes = [[i * 8 + j for i in range(z, 32, depth) for j in range(8)] for z in range(depth)]
    lines = [list(line) for line in zip(*planes)]
    size = len(planes[0])

    def trade(parts, groups):
        return lax.all_to_all(parts, axes, 0, 0, axis_index_groups=groups, tiled=True)

    shape = (SPLIT // size, SPLIT)
    mine = trade(x.reshape((size,) + shape), planes).sum(0)
    mine = trade(jnp.broadcast_to(mine, (depth,) + shape), lines).sum(0)
    return trade(jnp.broadcast_to(mine, (size,) + shape), planes).reshape(SPLIT, SPLIT)


def orthonormal(basis):
    inner = lax.dot_general(basis, basis, NT, precision=lax.Precision.HIGHEST, preferred_element_type=F32)
    row = lax.broadcasted_iota(jnp.int32, (MODES, 1), 0)
    columns = [jnp.broadcast_to(inner[:, j : j + 1], (MODES, 128)) for j in range(MODES)]
    wide = jnp.concatenate([basis, jnp.zeros((MODES, 256 - SNAPS), F32)], axis=1)
    parts = [wide[:, :128], wide[:, 128:]]
    scale = jnp.zeros((MODES, 128), F32)
    for j in range(MODES):
        pivot = columns[j][j : j + 1, :]
        scale = jnp.where(row == j, lax.rsqrt(pivot), scale)
        factor = jnp.where(row > j, columns[j] * (1.0 / pivot), 0.0)
        for k in range(j + 1, MODES):
            columns[k] = columns[k] - factor * columns[k][j : j + 1, :]
        parts = [part - factor * part[j : j + 1, :] for part in parts]
    return jnp.concatenate([part * scale for part in parts], axis=1)[:, :SNAPS]


def coefs_kernel(packed_ref, head_hbm, rest_hbm, basis_ref, own_ref, down_ref, up_ref, heads, rests, sems):
    copies = [
        pltpu.make_async_copy(head_hbm, heads, sems.at[0]),
        pltpu.make_async_copy(rest_hbm, rests, sems.at[1]),
    ]
    for copy in copies:
        copy.start()
    gram = unpack(packed_ref[...])
    basis = gram[:MODES, :]
    for _ in range(SWEEPS):
        basis = orthonormal(exact_dot(basis, gram))
    basis_ref[...] = basis
    wide = jnp.concatenate([basis] * FIELDS, axis=1)
    tall = jnp.concatenate([wide] * FIELDS, axis=0)
    row_field = lax.broadcasted_iota(jnp.int32, (COEFS, ROWS), 0) // MODES
    col_field = lax.broadcasted_iota(jnp.int32, (COEFS, ROWS), 1) // SNAPS
    head, rest = halves(jnp.where(row_field == col_field, tall, 0.0))
    both = jnp.concatenate([head, rest], axis=0)
    for copy in copies:
        copy.wait()
    for k in range(EXT):
        pair = dot(both, heads[k])
        own = pair[:COEFS] + pair[COEFS:] + dot(head, rests[k])
        own_ref[:, k * CW : (k + 1) * CW] = own
        if k < 2:
            down_ref[:, k * CW : (k + 1) * CW] = own
        if k >= CX:
            up_ref[:, (k - CX) * CW : (k - CX + 1) * CW] = own


def coefficients(packed, head, rest):
    side = jax.ShapeDtypeStruct((COEFS, 2 * CW), F32)
    return pl.pallas_call(
        coefs_kernel,
        in_specs=[VMEM, HBM, HBM],
        out_specs=[VMEM] * 4,
        scratch_shapes=[
            pltpu.VMEM((EXT, ROWS, CW), BF16),
            pltpu.VMEM((EXT, ROWS, CW), BF16),
            pltpu.SemaphoreType.DMA((2,)),
        ],
        out_shape=[
            jax.ShapeDtypeStruct((MODES, SNAPS), F32),
            jax.ShapeDtypeStruct((COEFS, EXT * CW), F32),
            side,
            side,
        ],
        compiler_params=params(52),
        name="coefs",
    )(packed, head, rest)


def prepare_kernel(basis_ref, cells, spread_ref, hots_ref):
    head, rest = halves(basis_ref[...])
    snap = lax.broadcasted_iota(jnp.int32, (SNAPS, ROWS), 0)
    column = lax.broadcasted_iota(jnp.int32, (SNAPS, ROWS), 1)
    repeat = (snap == column // FIELDS).astype(F32).astype(BF16)
    both = dot(jnp.concatenate([head, rest], axis=0), repeat)
    field = lax.broadcasted_iota(jnp.int32, (COEFS, ROWS), 0) // MODES
    mine = field == lax.broadcasted_iota(jnp.int32, (COEFS, ROWS), 1) % FIELDS
    head = jnp.where(mine, jnp.concatenate([both[:MODES]] * FIELDS, axis=0), 0.0)
    rest = jnp.where(mine, jnp.concatenate([both[MODES:]] * FIELDS, axis=0), 0.0)
    stacked = jnp.concatenate([head, head, rest, jnp.zeros_like(rest)], axis=0)
    spread_ref[...] = stacked.T.astype(BF16)
    for brick in range(BRICKS):
        hots_ref[brick] = cell_hot(cells, brick)


def prepare(basis, cells):
    return pl.pallas_call(
        prepare_kernel,
        in_specs=[VMEM, VMEM],
        out_specs=[VMEM, VMEM],
        out_shape=[
            jax.ShapeDtypeStruct((ROWS, 4 * COEFS), BF16),
            jax.ShapeDtypeStruct((BRICKS, CW, PER_BRICK), BF16),
        ],
        compiler_params=params(16),
        name="prepare",
    )(basis, cells)


def atoms_kernel(own_ref, below_ref, above_ref, spread_ref, hots_ref, column_ref, out_hbm, held, sems):
    whole = []
    for k in range(EXT):
        value = own_ref[:, k * CW : (k + 1) * CW]
        if k < 2:
            value = value + below_ref[:, k * CW : (k + 1) * CW]
        if k >= CX:
            value = value + above_ref[:, (k - CX) * CW : (k - CX + 1) * CW]
        whole.append(jnp.concatenate(halves(value), axis=0))
    blank = jnp.zeros((COEFS, PER_BRICK), BF16)
    copies = []
    for brick in range(BRICKS):
        column = column_ref[:, brick : brick + 1]
        mine = whole[0]
        for k in range(1, EXT):
            mine = jnp.where(column == k, whole[k], mine)
        picked = dot(mine, hots_ref[brick]).astype(BF16)
        stacked = jnp.concatenate([picked, picked[:COEFS], blank], axis=0)
        fields = dot(spread_ref[...], stacked).astype(BF16)
        held[brick] = fields.reshape(SNAPS, FIELDS, PER_BRICK)
        target = out_hbm.at[:, :, pl.ds(brick * PER_BRICK, PER_BRICK)]
        copy = pltpu.make_async_copy(held.at[brick], target, sems.at[brick])
        copy.start()
        copies.append(copy)
    for copy in copies:
        copy.wait()


def atom_fields(columns, own, below, above, spread, hots):
    return pl.pallas_call(
        atoms_kernel,
        in_specs=[VMEM] * 6,
        out_specs=HBM,
        scratch_shapes=[
            pltpu.VMEM((BRICKS, SNAPS, FIELDS, PER_BRICK), BF16),
            pltpu.SemaphoreType.DMA((BRICKS,)),
        ],
        out_shape=jax.ShapeDtypeStruct((SNAPS, FIELDS, BRICKS * PER_BRICK), BF16),
        compiler_params=params(32),
        name="atoms",
    )(own, below, above, spread, hots, columns)


def on_device(atom_values, atom_cell, brick_column):
    count = lax.axis_size("gx")
    to_lower = [((i + 1) % count, i) for i in range(count)]
    to_upper = [(i, (i + 1) % count) for i in range(count)]
    cells = atom_cell.reshape(BRICKS * LANES, 128)
    columns = brick_column.reshape(1, BRICKS)
    low, high = face_sums(atom_values, cells, columns)
    from_above = lax.ppermute(low, "gx", to_lower)
    from_below = lax.ppermute(high, "gx", to_upper)
    head, rest, faces, gram = local_sums(atom_values, cells, brick_column, low)
    packed = add_over_devices(packed_gram(gram, faces, from_below, from_above))
    basis, own, down, up = coefficients(packed, head, rest)
    above = lax.ppermute(down, "gx", to_lower)
    below = lax.ppermute(up, "gx", to_upper)
    spread, hots = prepare(basis, cells)
    return atom_fields(columns, own, below, above, spread, hots)


def solution(mesh):
    in_specs = (P(None, None, ("gx", "gz")), P(("gx", "gz")), P(("gx", "gz")))
    out_specs = P(None, None, ("gx", "gz"))
    return jax.shard_map(on_device, mesh=mesh, in_specs=in_specs, out_specs=out_specs, check_vma=False)
```

```python
import math

import jax
import jax.numpy as jnp
from jax import lax
from jax.experimental import pallas as pl
from jax.experimental.pallas import tpu as pltpu
from jax.sharding import PartitionSpec as P

SNAPS = 160
FIELDS = 4
ROWS = SNAPS * FIELDS
MODES = 8
SWEEPS = 3
CX = 4
EXT = CX + 2
CW = 512
PER_BRICK = 512
BRICKS = 8
COEFS = MODES * FIELDS
WIRE = ROWS + 16
TOP = 32767.0
STEPS = 8 / math.log(2)
SPLIT = 128
TAIL = SNAPS - SPLIT
LANES = CW // 128
F32 = jnp.float32
BF16 = jnp.bfloat16
NT = (((1,), (1,)), ((), ()))
TN = (((0,), (0,)), ((), ()))


def params(mib):
    return pltpu.CompilerParams(vmem_limit_bytes=mib * 1024 * 1024)


def dot_nt(a, b):
    return lax.dot_general(a, b, NT, preferred_element_type=F32)


def dot(a, b):
    return jnp.dot(a, b, preferred_element_type=F32)


def exact_dot(a, b):
    return jnp.dot(a, b, precision=lax.Precision.HIGHEST, preferred_element_type=F32)


def cell_hot(cells, brick, keep=None):
    ids = lax.broadcasted_iota(jnp.int32, (CW, 128), 0)
    tiles = []
    for t in range(LANES):
        row = cells[brick * LANES + t : brick * LANES + t + 1, :]
        if keep is not None:
            row = jnp.where(keep, row, -1)
        tiles.append((ids == row).astype(F32).astype(BF16))
    return jnp.concatenate(tiles, axis=1)


def halves(x):
    head = x.astype(BF16)
    return head, (x - head.astype(F32)).astype(BF16)


def one_field(total, field):
    rows = pl.ds(field, SNAPS, stride=FIELDS)
    return jnp.concatenate([total[t, rows, :] for t in range(LANES)], axis=1)


def brick_copy(values_hbm, held, sems, brick, slot):
    source = values_hbm.at[:, :, pl.ds(brick * PER_BRICK, PER_BRICK)]
    return pltpu.make_async_copy(source, held.at[slot], sems.at[slot])


def encode(total, out_ref):
    for t in range(LANES):
        lanes = slice(t * 128, (t + 1) * 128)
        most = jnp.max(jnp.abs(total[t]), axis=0, keepdims=True)
        code = jnp.ceil(jnp.log(jnp.maximum(most, 1e-30)) * STEPS)
        scale = jnp.exp(code * (-1 / STEPS)) * TOP
        for f in range(FIELDS):
            steps = jnp.round(total[t, pl.ds(f, SNAPS, stride=FIELDS), :] * scale)
            out_ref[f * SNAPS : (f + 1) * SNAPS, lanes] = jnp.clip(steps, -TOP, TOP).astype(jnp.int32).astype(jnp.int16)
        out_ref[ROWS:, lanes] = jnp.broadcast_to(code, (WIRE - ROWS, 128)).astype(jnp.int32).astype(jnp.int16)


def wire_steps(wire, rows):
    return wire[rows, :].astype(jnp.int32).astype(F32)


def wire_scale(wire):
    return jnp.exp(wire_steps(wire, slice(ROWS, WIRE))[:1] * (1 / STEPS)) * (1 / TOP)


HBM = pl.BlockSpec(memory_space=pltpu.HBM)
VMEM = pl.BlockSpec(memory_space=pltpu.VMEM)
SMEM = pl.BlockSpec(memory_space=pltpu.SMEM)


def faces_kernel(values_hbm, cells_hbm, column_hbm, low_hbm, high_hbm, held, total, face, cells, columns, sems, small, out_sems):
    bricks = (0, 1, BRICKS - 2, BRICKS - 1)
    targets = ((0, low_hbm), (EXT - 1, high_hbm))
    inputs = [
        pltpu.make_async_copy(cells_hbm, cells, small.at[0]),
        pltpu.make_async_copy(column_hbm, columns, small.at[1]),
    ]
    copies = [brick_copy(values_hbm, held, sems, brick, slot) for slot, brick in enumerate(bricks)]
    outputs = [pltpu.make_async_copy(face.at[i], out, out_sems.at[i]) for i, (_, out) in enumerate(targets)]
    for copy in inputs + copies:
        copy.start()
    for copy in inputs:
        copy.wait()
    hots = [
        cell_hot(cells, brick, columns[:, brick : brick + 1] == targets[slot // 2][0]) for slot, brick in enumerate(bricks)
    ]
    for i in range(2):
        sums = None
        for slot in (2 * i, 2 * i + 1):
            copies[slot].wait()
            part = dot_nt(held[slot].reshape(ROWS, PER_BRICK), hots[slot])
            sums = part if sums is None else sums + part
        for t in range(LANES):
            total[i, t] = sums[:, t * 128 : (t + 1) * 128]
        encode(total.at[i], face.at[i])
        outputs[i].start()
    for copy in outputs:
        copy.wait()


def face_sums(values, cells, columns):
    shape = jax.ShapeDtypeStruct((WIRE, CW), jnp.int16)
    return pl.pallas_call(
        faces_kernel,
        in_specs=[HBM] * 3,
        out_specs=[HBM] * 2,
        scratch_shapes=[
            pltpu.VMEM((4, SNAPS, FIELDS, PER_BRICK), BF16),
            pltpu.VMEM((2, LANES, ROWS, 128), F32),
            pltpu.VMEM((2, WIRE, CW), jnp.int16),
            pltpu.VMEM((BRICKS * LANES, 128), jnp.int32),
            pltpu.VMEM((1, BRICKS), jnp.int32),
            pltpu.SemaphoreType.DMA((4,)),
            pltpu.SemaphoreType.DMA((2,)),
            pltpu.SemaphoreType.DMA((2,)),
        ],
        out_shape=[shape, shape],
        compiler_params=params(63),
        name="faces",
    )(values, cells, columns)


def local_kernel(
    column_ref, values_hbm, cells, after, head_hbm, rest_hbm, hots_hbm, face_ref, gram_ref, down_ref, up_ref,
    held, total, heads, rests, hots, sems, out_sems, hot_sems
):
    copies = [brick_copy(values_hbm, held, sems, brick, brick) for brick in range(BRICKS)]
    for copy in copies:
        copy.start()
    outputs = []
    total[...] = jnp.zeros_like(total)
    for brick in range(BRICKS):
        hot = cell_hot(cells, brick)
        hots[brick] = hot
        outputs.append(pltpu.make_async_copy(hots.at[brick], hots_hbm.at[brick], hot_sems.at[brick]))
        outputs[-1].start()
        copies[brick].wait()
        sums = dot_nt(held[brick].reshape(ROWS, PER_BRICK), hot)
        column = column_ref[brick]
        for t in range(LANES):
            total[column, t] += sums[:, t * 128 : (t + 1) * 128]
    encode(total.at[1], down_ref)
    encode(total.at[CX], up_ref)
    same = jnp.zeros((SNAPS, SNAPS), F32)
    mixed = jnp.zeros((SNAPS, SNAPS), F32)
    for k in range(EXT):
        for f in range(FIELDS):
            rows = slice(f * SNAPS, (f + 1) * SNAPS)
            head, rest = halves(one_field(total.at[k], f))
            heads[k, rows, :] = head
            rests[k, rows, :] = rest
            if k in (1, CX):
                face_ref[2 * (k // CX), rows, :] = head
                face_ref[2 * (k // CX) + 1, rows, :] = rest
            same += dot_nt(head, head)
            mixed += dot_nt(head, rest)
        for i, (source, target) in enumerate(((heads, head_hbm), (rests, rest_hbm))):
            outputs.append(pltpu.make_async_copy(source.at[k], target.at[k], out_sems.at[i, k]))
            outputs[-1].start()
    gram_ref[...] = same + mixed + mixed.T
    for copy in outputs:
        copy.wait()


def local_sums(values, cells, columns, after):
    half = jax.ShapeDtypeStruct((EXT, ROWS, CW), BF16)
    wire = jax.ShapeDtypeStruct((WIRE, CW), jnp.int16)
    return pl.pallas_call(
        local_kernel,
        in_specs=[SMEM, HBM, VMEM, HBM],
        out_specs=[HBM] * 3 + [VMEM] * 4,
        scratch_shapes=[
            pltpu.VMEM((BRICKS, SNAPS, FIELDS, PER_BRICK), BF16),
            pltpu.VMEM((EXT, LANES, ROWS, 128), F32),
            pltpu.VMEM((EXT, ROWS, CW), BF16),
            pltpu.VMEM((EXT, ROWS, CW), BF16),
            pltpu.VMEM((BRICKS, CW, PER_BRICK), BF16),
            pltpu.SemaphoreType.DMA((BRICKS,)),
            pltpu.SemaphoreType.DMA((2, EXT)),
            pltpu.SemaphoreType.DMA((BRICKS,)),
        ],
        out_shape=[
            half,
            half,
            jax.ShapeDtypeStruct((BRICKS, CW, PER_BRICK), BF16),
            jax.ShapeDtypeStruct((4, ROWS, CW), BF16),
            jax.ShapeDtypeStruct((SNAPS, SNAPS), F32),
            wire,
            wire,
        ],
        compiler_params=params(48),
        cost_estimate=pl.CostEstimate(flops=6_000_000_000, bytes_accessed=14_000_000, transcendentals=0),
        name="local",
    )(columns, values, cells, after)


def pack(gram):
    body = gram[:SPLIT, :SPLIT]
    side = gram[:SPLIT, SPLIT:]
    corner = gram[SPLIT:, SPLIT:]
    t = TAIL
    rows = [
        body[:t],
        jnp.concatenate([side[:t], body[t : 2 * t, t:]], axis=1),
        jnp.concatenate([side[t : 2 * t], side[2 * t : 3 * t], body[2 * t : 3 * t, 2 * t :]], axis=1),
        jnp.concatenate([side[3 * t :], corner, corner, body[3 * t :, 3 * t :]], axis=1),
    ]
    return jnp.concatenate(rows, axis=0)


def unpack(packed):
    t = TAIL
    row = lax.broadcasted_iota(jnp.int32, (SPLIT, SPLIT), 0) // t
    col = lax.broadcasted_iota(jnp.int32, (SPLIT, SPLIT), 1) // t
    above = jnp.where(col > row, packed, 0.0)
    body = jnp.where(col == row, packed, 0.0) + above + above.T
    side = jnp.concatenate(
        [packed[t : 2 * t, :t], packed[2 * t : 3 * t, :t], packed[2 * t : 3 * t, t : 2 * t], packed[3 * t :, :t]], axis=0
    )
    corner = packed[3 * t :, t : 2 * t]
    top = jnp.concatenate([body, side], axis=1)
    padded = jnp.concatenate([side, jnp.zeros((SPLIT, SPLIT - t), F32)], axis=1)
    bottom = jnp.concatenate([padded.T[:t], corner], axis=1)
    return jnp.concatenate([top, bottom], axis=0)


def cross_kernel(gram_ref, face_ref, from_below, from_above, packed_ref):
    cross = jnp.zeros((SNAPS, SNAPS), F32)
    for i, received in enumerate((from_below, from_above)):
        scale = wire_scale(received)
        for f in range(FIELDS):
            rows = slice(f * SNAPS, (f + 1) * SNAPS)
            head, rest = halves(wire_steps(received, rows) * scale)
            own = face_ref[2 * i, rows, :]
            cross += dot_nt(own, head) + dot_nt(own, rest) + dot_nt(face_ref[2 * i + 1, rows, :], head)
    packed_ref[...] = pack(gram_ref[...] + cross + cross.T)


def packed_gram(gram, faces, from_below, from_above):
    return pl.pallas_call(
        cross_kernel,
        in_specs=[VMEM] * 4,
        out_specs=VMEM,
        out_shape=jax.ShapeDtypeStruct((SPLIT, SPLIT), F32),
        compiler_params=params(16),
        name="cross",
    )(gram, faces, from_below, from_above)


def add_over_devices(x):
    axes = ("gx", "gz")
    depth = 8
    planes = [[i * 8 + j for i in range(z, 32, depth) for j in range(8)] for z in range(depth)]
    lines = [list(line) for line in zip(*planes)]
    size = len(planes[0])

    def trade(parts, groups):
        return lax.all_to_all(parts, axes, 0, 0, axis_index_groups=groups, tiled=True)

    shape = (SPLIT // size, SPLIT)
    mine = trade(x.reshape((size,) + shape), planes).sum(0)
    mine = trade(jnp.broadcast_to(mine, (depth,) + shape), lines).sum(0)
    return trade(jnp.broadcast_to(mine, (size,) + shape), planes).reshape(SPLIT, SPLIT)


def orthonormal(basis):
    inner = lax.dot_general(basis, basis, NT, precision=lax.Precision.HIGHEST, preferred_element_type=F32)
    row = lax.broadcasted_iota(jnp.int32, (MODES, 1), 0)
    columns = [jnp.broadcast_to(inner[:, j : j + 1], (MODES, 128)) for j in range(MODES)]
    wide = jnp.concatenate([basis, jnp.zeros((MODES, 256 - SNAPS), F32)], axis=1)
    parts = [wide[:, :128], wide[:, 128:]]
    scale = jnp.zeros((MODES, 128), F32)
    for j in range(MODES):
        pivot = columns[j][j : j + 1, :]
        scale = jnp.where(row == j, lax.rsqrt(pivot), scale)
        factor = jnp.where(row > j, columns[j] * (1.0 / pivot), 0.0)
        for k in range(j + 1, MODES):
            columns[k] = columns[k] - factor * columns[k][j : j + 1, :]
        parts = [part - factor * part[j : j + 1, :] for part in parts]
    return jnp.concatenate([part * scale for part in parts], axis=1)[:, :SNAPS]


def spread_matrix(basis):
    snap = lax.broadcasted_iota(jnp.int32, (SNAPS, ROWS), 0)
    column = lax.broadcasted_iota(jnp.int32, (SNAPS, ROWS), 1)
    repeat = (snap == column // FIELDS).astype(F32).astype(BF16)
    both = dot(jnp.concatenate(halves(basis), axis=0), repeat)
    field = lax.broadcasted_iota(jnp.int32, (COEFS, ROWS), 0) // MODES
    mine = field == lax.broadcasted_iota(jnp.int32, (COEFS, ROWS), 1) % FIELDS
    head = jnp.where(mine, jnp.concatenate([both[:MODES]] * FIELDS, axis=0), 0.0)
    rest = jnp.where(mine, jnp.concatenate([both[MODES:]] * FIELDS, axis=0), 0.0)
    return jnp.concatenate([head, head, rest, jnp.zeros_like(rest)], axis=0).T.astype(BF16)


def output_kernel(
    packed_ref, column_hbm, head_hbm, rest_hbm, hots_hbm, *refs
):
    wires_hbm, out_hbm = refs[:4], refs[4]
    heads, rests, hots, wires, columns, held, sems, hot_sems, out_sems = refs[5:]
    sources = (head_hbm, rest_hbm) + wires_hbm + (column_hbm,)
    places = (heads, rests) + tuple(wires.at[i] for i in range(4)) + (columns,)
    copies = [pltpu.make_async_copy(a, b, sems.at[i]) for i, (a, b) in enumerate(zip(sources, places))]
    hot_copies = [pltpu.make_async_copy(hots_hbm.at[i], hots.at[i], hot_sems.at[i]) for i in range(BRICKS)]
    for copy in copies + hot_copies:
        copy.start()
    gram = unpack(packed_ref[...])
    basis = gram[:MODES, :]
    for _ in range(SWEEPS):
        basis = orthonormal(exact_dot(basis, gram))
    wide = jnp.concatenate([basis] * FIELDS, axis=1)
    tall = jnp.concatenate([wide] * FIELDS, axis=0)
    row_field = lax.broadcasted_iota(jnp.int32, (COEFS, ROWS), 0) // MODES
    col_field = lax.broadcasted_iota(jnp.int32, (COEFS, ROWS), 1) // SNAPS
    head, rest = halves(jnp.where(row_field == col_field, tall, 0.0))
    both = jnp.concatenate([head, rest], axis=0)
    spread = spread_matrix(basis)

    def coefficients(heads_of, rests_of):
        pair = dot(both, heads_of)
        return pair[:COEFS] + pair[COEFS:] + dot(head, rests_of)

    for copy in copies:
        copy.wait()
    whole = []
    for k in range(EXT):
        value = coefficients(heads[k], rests[k])
        if k in (0, 1, CX, CX + 1):
            wire = wires.at[(0, 1, 0, 0, 2, 3)[k]]
            value += coefficients(*halves(wire_steps(wire, slice(0, ROWS)))) * wire_scale(wire)
        whole.append(jnp.concatenate(halves(value), axis=0))
    blank = jnp.zeros((COEFS, PER_BRICK), BF16)
    outputs = []
    for brick in range(BRICKS):
        column = columns[:, brick : brick + 1]
        mine = whole[0]
        for k in range(1, EXT):
            mine = jnp.where(column == k, whole[k], mine)
        hot_copies[brick].wait()
        picked = dot(mine, hots[brick]).astype(BF16)
        stacked = jnp.concatenate([picked, picked[:COEFS], blank], axis=0)
        held[brick] = dot(spread, stacked).astype(BF16).reshape(SNAPS, FIELDS, PER_BRICK)
        target = out_hbm.at[:, :, pl.ds(brick * PER_BRICK, PER_BRICK)]
        outputs.append(pltpu.make_async_copy(held.at[brick], target, out_sems.at[brick]))
        outputs[-1].start()
    for copy in outputs:
        copy.wait()


def atom_fields(packed, columns, head, rest, hots, wires):
    return pl.pallas_call(
        output_kernel,
        in_specs=[VMEM] + [HBM] * 8,
        out_specs=HBM,
        scratch_shapes=[
            pltpu.VMEM((EXT, ROWS, CW), BF16),
            pltpu.VMEM((EXT, ROWS, CW), BF16),
            pltpu.VMEM((BRICKS, CW, PER_BRICK), BF16),
            pltpu.VMEM((4, WIRE, CW), jnp.int16),
            pltpu.VMEM((1, BRICKS), jnp.int32),
            pltpu.VMEM((BRICKS, SNAPS, FIELDS, PER_BRICK), BF16),
            pltpu.SemaphoreType.DMA((7,)),
            pltpu.SemaphoreType.DMA((BRICKS,)),
            pltpu.SemaphoreType.DMA((BRICKS,)),
        ],
        out_shape=jax.ShapeDtypeStruct((SNAPS, FIELDS, BRICKS * PER_BRICK), BF16),
        compiler_params=params(51),
        name="output",
    )(packed, columns, head, rest, hots, *wires)


def on_device(atom_values, atom_cell, brick_column):
    count = lax.axis_size("gx")
    to_lower = [((i + 1) % count, i) for i in range(count)]
    to_upper = [(i, (i + 1) % count) for i in range(count)]
    cells = atom_cell.reshape(BRICKS * LANES, 128)
    columns = brick_column.reshape(1, BRICKS)
    low, high = face_sums(atom_values, cells, columns)
    from_above = lax.ppermute(low, "gx", to_lower)
    from_below = lax.ppermute(high, "gx", to_upper)
    head, rest, hots, faces, gram, down, up = local_sums(atom_values, cells, brick_column, low)
    second_above = lax.ppermute(down, "gx", to_lower)
    second_below = lax.ppermute(up, "gx", to_upper)
    packed = add_over_devices(packed_gram(gram, faces, from_below, from_above))
    wires = (second_below, from_below, from_above, second_above)
    return atom_fields(packed, columns, head, rest, hots, wires)


def solution(mesh):
    in_specs = (P(None, None, ("gx", "gz")), P(("gx", "gz")), P(("gx", "gz")))
    out_specs = P(None, None, ("gx", "gz"))
    return jax.shard_map(on_device, mesh=mesh, in_specs=in_specs, out_specs=out_specs, check_vma=False)
```

```python
import math

import jax
import jax.numpy as jnp
from jax import lax
from jax.experimental import pallas as pl
from jax.experimental.pallas import tpu as pltpu
from jax.sharding import PartitionSpec as P

SNAPS = 160
FIELDS = 4
ROWS = SNAPS * FIELDS
MODES = 8
SWEEPS = 3
CX = 4
EXT = CX + 2
CW = 512
PER_BRICK = 512
BRICKS = 8
COEFS = MODES * FIELDS
WIRE = ROWS + 16
TOP = 32767.0
STEPS = 8 / math.log(2)
SPLIT = 128
TAIL = SNAPS - SPLIT
LANES = CW // 128
F32 = jnp.float32
BF16 = jnp.bfloat16
NT = (((1,), (1,)), ((), ()))
TN = (((0,), (0,)), ((), ()))


def params(mib):
    return pltpu.CompilerParams(vmem_limit_bytes=mib * 1024 * 1024)


def dot_nt(a, b):
    return lax.dot_general(a, b, NT, preferred_element_type=F32)


def dot(a, b):
    return jnp.dot(a, b, preferred_element_type=F32)


def exact_dot(a, b):
    return jnp.dot(a, b, precision=lax.Precision.HIGHEST, preferred_element_type=F32)


def cell_hot(cells, brick, keep=None):
    ids = lax.broadcasted_iota(jnp.int32, (CW, 128), 0)
    tiles = []
    for t in range(LANES):
        row = cells[brick * LANES + t : brick * LANES + t + 1, :]
        if keep is not None:
            row = jnp.where(keep, row, -1)
        tiles.append((ids == row).astype(F32).astype(BF16))
    return jnp.concatenate(tiles, axis=1)


def halves(x):
    head = x.astype(BF16)
    return head, (x - head.astype(F32)).astype(BF16)


def one_field(total, field):
    rows = pl.ds(field, SNAPS, stride=FIELDS)
    return jnp.concatenate([total[t, rows, :] for t in range(LANES)], axis=1)


def brick_copy(values_hbm, held, sems, brick, slot):
    source = values_hbm.at[:, :, pl.ds(brick * PER_BRICK, PER_BRICK)]
    return pltpu.make_async_copy(source, held.at[slot], sems.at[slot])


def encode(total, out_ref):
    for t in range(LANES):
        lanes = slice(t * 128, (t + 1) * 128)
        most = jnp.max(jnp.abs(total[t]), axis=0, keepdims=True)
        code = jnp.ceil(jnp.log(jnp.maximum(most, 1e-30)) * STEPS)
        scale = jnp.exp(code * (-1 / STEPS)) * TOP
        for f in range(FIELDS):
            steps = jnp.round(total[t, pl.ds(f, SNAPS, stride=FIELDS), :] * scale)
            out_ref[f * SNAPS : (f + 1) * SNAPS, lanes] = jnp.clip(steps, -TOP, TOP).astype(jnp.int32).astype(jnp.int16)
        out_ref[ROWS:, lanes] = jnp.broadcast_to(code, (WIRE - ROWS, 128)).astype(jnp.int32).astype(jnp.int16)


def wire_steps(wire, rows):
    return wire[rows, :].astype(jnp.int32).astype(F32)


def wire_scale(wire):
    return jnp.exp(wire_steps(wire, slice(ROWS, WIRE))[:1] * (1 / STEPS)) * (1 / TOP)


HBM = pl.BlockSpec(memory_space=pltpu.HBM)
VMEM = pl.BlockSpec(memory_space=pltpu.VMEM)
SMEM = pl.BlockSpec(memory_space=pltpu.SMEM)


def faces_kernel(
    values_hbm, cells_hbm, column_hbm, low_hbm, high_hbm, passed_hbm, held, total, face, cells, columns, sems, small, out_sems
):
    bricks = (0, 1, BRICKS - 2, BRICKS - 1)
    targets = ((0, low_hbm), (EXT - 1, high_hbm))
    inputs = [
        pltpu.make_async_copy(cells_hbm, cells, small.at[0]),
        pltpu.make_async_copy(column_hbm, columns, small.at[1]),
    ]
    copies = [brick_copy(values_hbm, held, sems, brick, slot) for slot, brick in enumerate(bricks)]
    outputs = [pltpu.make_async_copy(face.at[i], out, out_sems.at[i]) for i, (_, out) in enumerate(targets)]
    for copy in inputs + copies:
        copy.start()
    for copy in inputs:
        copy.wait()
    outputs.append(pltpu.make_async_copy(cells, passed_hbm, out_sems.at[2]))
    outputs[2].start()
    hots = [
        cell_hot(cells, brick, columns[:, brick : brick + 1] == targets[slot // 2][0]) for slot, brick in enumerate(bricks)
    ]
    for i in range(2):
        sums = None
        for slot in (2 * i, 2 * i + 1):
            copies[slot].wait()
            part = dot_nt(held[slot].reshape(ROWS, PER_BRICK), hots[slot])
            sums = part if sums is None else sums + part
        for t in range(LANES):
            total[i, t] = sums[:, t * 128 : (t + 1) * 128]
        encode(total.at[i], face.at[i])
        outputs[i].start()
    for copy in outputs:
        copy.wait()


def face_sums(values, cells, columns):
    shape = jax.ShapeDtypeStruct((WIRE, CW), jnp.int16)
    return pl.pallas_call(
        faces_kernel,
        in_specs=[HBM] * 3,
        out_specs=[HBM] * 3,
        scratch_shapes=[
            pltpu.VMEM((4, SNAPS, FIELDS, PER_BRICK), BF16),
            pltpu.VMEM((2, LANES, ROWS, 128), F32),
            pltpu.VMEM((2, WIRE, CW), jnp.int16),
            pltpu.VMEM((BRICKS * LANES, 128), jnp.int32),
            pltpu.VMEM((1, BRICKS), jnp.int32),
            pltpu.SemaphoreType.DMA((4,)),
            pltpu.SemaphoreType.DMA((2,)),
            pltpu.SemaphoreType.DMA((3,)),
        ],
        out_shape=[shape, shape, jax.ShapeDtypeStruct((BRICKS * LANES, 128), jnp.int32)],
        compiler_params=params(63),
        name="faces",
    )(values, cells, columns)


def local_kernel(
    column_ref, values_hbm, cells_hbm, head_hbm, rest_hbm, hots_hbm, face_ref, gram_ref,
    cells, held, total, heads, rests, hots, sems, out_sems, hot_sems, small
):
    ids = pltpu.make_async_copy(cells_hbm, cells, small)
    ids.start()
    copies = [brick_copy(values_hbm, held, sems, brick, brick) for brick in range(BRICKS)]
    for copy in copies:
        copy.start()
    outputs = []
    total[...] = jnp.zeros_like(total)
    ids.wait()
    for brick in range(BRICKS):
        hot = cell_hot(cells, brick)
        hots[brick] = hot
        outputs.append(pltpu.make_async_copy(hots.at[brick], hots_hbm.at[brick], hot_sems.at[brick]))
        outputs[-1].start()
        copies[brick].wait()
        sums = dot_nt(held[brick].reshape(ROWS, PER_BRICK), hot)
        column = column_ref[brick]
        for t in range(LANES):
            total[column, t] += sums[:, t * 128 : (t + 1) * 128]
    same = jnp.zeros((SNAPS, SNAPS), F32)
    mixed = jnp.zeros((SNAPS, SNAPS), F32)
    for k in range(EXT):
        for f in range(FIELDS):
            rows = slice(f * SNAPS, (f + 1) * SNAPS)
            head, rest = halves(one_field(total.at[k], f))
            heads[k, rows, :] = head
            rests[k, rows, :] = rest
            if k in (1, CX):
                face_ref[2 * (k // CX), rows, :] = head
                face_ref[2 * (k // CX) + 1, rows, :] = rest
            same += dot_nt(head, head)
            mixed += dot_nt(head, rest)
        for i, (source, target) in enumerate(((heads, head_hbm), (rests, rest_hbm))):
            outputs.append(pltpu.make_async_copy(source.at[k], target.at[k], out_sems.at[i, k]))
            outputs[-1].start()
    gram_ref[...] = same + mixed + mixed.T
    for copy in outputs:
        copy.wait()


def local_sums(values, cells, columns):
    half = jax.ShapeDtypeStruct((EXT, ROWS, CW), BF16)
    return pl.pallas_call(
        local_kernel,
        in_specs=[SMEM, HBM, HBM],
        out_specs=[HBM] * 3 + [VMEM] * 2,
        scratch_shapes=[
            pltpu.VMEM((BRICKS * LANES, 128), jnp.int32),
            pltpu.VMEM((BRICKS, SNAPS, FIELDS, PER_BRICK), BF16),
            pltpu.VMEM((EXT, LANES, ROWS, 128), F32),
            pltpu.VMEM((EXT, ROWS, CW), BF16),
            pltpu.VMEM((EXT, ROWS, CW), BF16),
            pltpu.VMEM((BRICKS, CW, PER_BRICK), BF16),
            pltpu.SemaphoreType.DMA((BRICKS,)),
            pltpu.SemaphoreType.DMA((2, EXT)),
            pltpu.SemaphoreType.DMA((BRICKS,)),
            pltpu.SemaphoreType.DMA,
        ],
        out_shape=[
            half,
            half,
            jax.ShapeDtypeStruct((BRICKS, CW, PER_BRICK), BF16),
            jax.ShapeDtypeStruct((4, ROWS, CW), BF16),
            jax.ShapeDtypeStruct((SNAPS, SNAPS), F32),
        ],
        compiler_params=params(48),
        cost_estimate=pl.CostEstimate(flops=6_000_000_000, bytes_accessed=14_000_000, transcendentals=0),
        name="local",
    )(columns, values, cells)


def pack(gram):
    body = gram[:SPLIT, :SPLIT]
    side = gram[:SPLIT, SPLIT:]
    corner = gram[SPLIT:, SPLIT:]
    t = TAIL
    rows = [
        body[:t],
        jnp.concatenate([side[:t], body[t : 2 * t, t:]], axis=1),
        jnp.concatenate([side[t : 2 * t], side[2 * t : 3 * t], body[2 * t : 3 * t, 2 * t :]], axis=1),
        jnp.concatenate([side[3 * t :], corner, corner, body[3 * t :, 3 * t :]], axis=1),
    ]
    return jnp.concatenate(rows, axis=0)


def unpack(packed):
    t = TAIL
    row = lax.broadcasted_iota(jnp.int32, (SPLIT, SPLIT), 0) // t
    col = lax.broadcasted_iota(jnp.int32, (SPLIT, SPLIT), 1) // t
    above = jnp.where(col > row, packed, 0.0)
    body = jnp.where(col == row, packed, 0.0) + above + above.T
    side = jnp.concatenate(
        [packed[t : 2 * t, :t], packed[2 * t : 3 * t, :t], packed[2 * t : 3 * t, t : 2 * t], packed[3 * t :, :t]], axis=0
    )
    corner = packed[3 * t :, t : 2 * t]
    top = jnp.concatenate([body, side], axis=1)
    padded = jnp.concatenate([side, jnp.zeros((SPLIT, SPLIT - t), F32)], axis=1)
    bottom = jnp.concatenate([padded.T[:t], corner], axis=1)
    return jnp.concatenate([top, bottom], axis=0)


def cross_kernel(gram_ref, face_ref, from_below, from_above, packed_ref):
    cross = jnp.zeros((SNAPS, SNAPS), F32)
    for i, received in enumerate((from_below, from_above)):
        scale = wire_scale(received)
        for f in range(FIELDS):
            rows = slice(f * SNAPS, (f + 1) * SNAPS)
            head, rest = halves(wire_steps(received, rows) * scale)
            own = face_ref[2 * i, rows, :]
            cross += dot_nt(own, head) + dot_nt(own, rest) + dot_nt(face_ref[2 * i + 1, rows, :], head)
    packed_ref[...] = pack(gram_ref[...] + cross + cross.T)


def packed_gram(gram, faces, from_below, from_above):
    return pl.pallas_call(
        cross_kernel,
        in_specs=[VMEM] * 4,
        out_specs=VMEM,
        out_shape=jax.ShapeDtypeStruct((SPLIT, SPLIT), F32),
        compiler_params=params(16),
        name="cross",
    )(gram, faces, from_below, from_above)


def add_over_devices(x):
    axes = ("gx", "gz")
    depth = 8
    planes = [[i * 8 + j for i in range(z, 32, depth) for j in range(8)] for z in range(depth)]
    lines = [list(line) for line in zip(*planes)]
    size = len(planes[0])

    def trade(parts, groups):
        return lax.all_to_all(parts, axes, 0, 0, axis_index_groups=groups, tiled=True)

    shape = (SPLIT // size, SPLIT)
    mine = trade(x.reshape((size,) + shape), planes).sum(0)
    mine = trade(jnp.broadcast_to(mine, (depth,) + shape), lines).sum(0)
    return trade(jnp.broadcast_to(mine, (size,) + shape), planes).reshape(SPLIT, SPLIT)


def orthonormal(basis):
    inner = lax.dot_general(basis, basis, NT, precision=lax.Precision.HIGHEST, preferred_element_type=F32)
    row = lax.broadcasted_iota(jnp.int32, (MODES, 1), 0)
    columns = [jnp.broadcast_to(inner[:, j : j + 1], (MODES, 128)) for j in range(MODES)]
    wide = jnp.concatenate([basis, jnp.zeros((MODES, 256 - SNAPS), F32)], axis=1)
    parts = [wide[:, :128], wide[:, 128:]]
    scale = jnp.zeros((MODES, 128), F32)
    for j in range(MODES):
        pivot = columns[j][j : j + 1, :]
        scale = jnp.where(row == j, lax.rsqrt(pivot), scale)
        factor = jnp.where(row > j, columns[j] * (1.0 / pivot), 0.0)
        for k in range(j + 1, MODES):
            columns[k] = columns[k] - factor * columns[k][j : j + 1, :]
        parts = [part - factor * part[j : j + 1, :] for part in parts]
    return jnp.concatenate([part * scale for part in parts], axis=1)[:, :SNAPS]


def spread_matrix(basis):
    snap = lax.broadcasted_iota(jnp.int32, (SNAPS, ROWS), 0)
    column = lax.broadcasted_iota(jnp.int32, (SNAPS, ROWS), 1)
    repeat = (snap == column // FIELDS).astype(F32).astype(BF16)
    both = dot(jnp.concatenate(halves(basis), axis=0), repeat)
    field = lax.broadcasted_iota(jnp.int32, (COEFS, ROWS), 0) // MODES
    mine = field == lax.broadcasted_iota(jnp.int32, (COEFS, ROWS), 1) % FIELDS
    head = jnp.where(mine, jnp.concatenate([both[:MODES]] * FIELDS, axis=0), 0.0)
    rest = jnp.where(mine, jnp.concatenate([both[MODES:]] * FIELDS, axis=0), 0.0)
    return jnp.concatenate([head, head, rest, jnp.zeros_like(rest)], axis=0).T.astype(BF16)


def start(copies):
    for copy in copies:
        copy.start()
    return copies


def wait(copies):
    for copy in copies:
        copy.wait()


def by_field(basis):
    tall = jnp.concatenate([jnp.concatenate([basis] * FIELDS, axis=1)] * FIELDS, axis=0)
    row_field = lax.broadcasted_iota(jnp.int32, (COEFS, ROWS), 0) // MODES
    col_field = lax.broadcasted_iota(jnp.int32, (COEFS, ROWS), 1) // SNAPS
    return jnp.concatenate(halves(jnp.where(row_field == col_field, tall, 0.0)), axis=0)


def coefficients(both, head, rest):
    pair = dot(both, head)
    return pair[:COEFS] + pair[COEFS:] + dot(both[:COEFS], rest)


def basis_kernel(packed_ref, head_hbm, rest_hbm, basis_ref, down_ref, up_ref, heads, rests, sems):
    copies = []
    for i, k in enumerate((1, CX)):
        copies.append(pltpu.make_async_copy(head_hbm.at[k], heads.at[i], sems.at[0, i]))
        copies.append(pltpu.make_async_copy(rest_hbm.at[k], rests.at[i], sems.at[1, i]))
    start(copies)
    gram = unpack(packed_ref[...])
    basis = gram[:MODES, :]
    for _ in range(SWEEPS):
        basis = orthonormal(exact_dot(basis, gram))
    basis_ref[...] = basis
    both = by_field(basis)
    wait(copies)
    down_ref[...] = coefficients(both, heads[0], rests[0])
    up_ref[...] = coefficients(both, heads[1], rests[1])


def basis_and_faces(packed, head, rest):
    side = jax.ShapeDtypeStruct((COEFS, CW), F32)
    return pl.pallas_call(
        basis_kernel,
        in_specs=[VMEM, HBM, HBM],
        out_specs=[VMEM] * 3,
        scratch_shapes=[
            pltpu.VMEM((2, ROWS, CW), BF16),
            pltpu.VMEM((2, ROWS, CW), BF16),
            pltpu.SemaphoreType.DMA((2, 2)),
        ],
        out_shape=[jax.ShapeDtypeStruct((MODES, SNAPS), F32), side, side],
        compiler_params=params(52),
        name="basis",
    )(packed, head, rest)


def column_of(columns, brick, whole):
    mine = whole[0]
    for k in range(1, EXT):
        mine = jnp.where(columns[:, brick : brick + 1] == k, whole[k], mine)
    return mine


def write_brick(brick, column, hot, spread, held, out_hbm, sem):
    picked = dot(column, hot).astype(BF16)
    blank = jnp.zeros((COEFS, PER_BRICK), BF16)
    stacked = jnp.concatenate([picked, picked[:COEFS], blank], axis=0)
    held[...] = dot(spread, stacked).astype(BF16).reshape(SNAPS, FIELDS, PER_BRICK)
    copy = pltpu.make_async_copy(held, out_hbm.at[:, :, pl.ds(brick * PER_BRICK, PER_BRICK)], sem)
    copy.start()
    return copy


INNER = range(2, BRICKS - 2)
OUTER = (0, 1, BRICKS - 2, BRICKS - 1)


def inner_kernel(
    basis_ref, down_ref, up_ref, from_below, from_above, column_hbm, head_hbm, rest_hbm, hots_hbm,
    out_hbm, whole_ref, ends_ref, spread_ref, edge_hots, passed_ref,
    heads, rests, hots, held, sems, hot_sems, edge_sems, small, out_sems
):
    own = (2, 3, 0, EXT - 1)
    columns = pltpu.make_async_copy(column_hbm, passed_ref, small)
    columns.start()
    copies = []
    for i, k in enumerate(own):
        copies.append(pltpu.make_async_copy(head_hbm.at[k], heads.at[i], sems.at[0, i]))
        copies.append(pltpu.make_async_copy(rest_hbm.at[k], rests.at[i], sems.at[1, i]))
    start(copies)
    hot_copies = start([pltpu.make_async_copy(hots_hbm.at[b], hots.at[i], hot_sems.at[i]) for i, b in enumerate(INNER)])
    edge_copies = start([pltpu.make_async_copy(hots_hbm.at[b], edge_hots.at[i], edge_sems.at[i]) for i, b in enumerate(OUTER)])
    both = by_field(basis_ref[...])
    spread_ref[...] = spread_matrix(basis_ref[...])
    whole = [jnp.zeros((2 * COEFS, CW), BF16)] * EXT
    for k, mine, wire in ((1, down_ref, from_below), (CX, up_ref, from_above)):
        other = coefficients(both, *halves(wire_steps(wire, slice(0, ROWS))))
        whole[k] = jnp.concatenate(halves(mine[...] + other * wire_scale(wire)), axis=0)
    wait(copies)
    for i, k in enumerate(own):
        value = coefficients(both, heads[i], rests[i])
        if i < 2:
            whole[k] = jnp.concatenate(halves(value), axis=0)
        else:
            ends_ref[i - 2] = value
    for k in range(EXT):
        whole_ref[k] = whole[k]
    columns.wait()
    outputs = []
    for i, brick in enumerate(INNER):
        hot_copies[i].wait()
        column = column_of(passed_ref, brick, whole)
        outputs.append(write_brick(brick, column, hots[i], spread_ref[...], held.at[i], out_hbm, out_sems.at[i]))
    wait(edge_copies)
    wait(outputs)


def inner_fields(basis, down, up, from_below, from_above, columns, head, rest, hots):
    return pl.pallas_call(
        inner_kernel,
        in_specs=[VMEM] * 5 + [HBM] * 4,
        out_specs=[HBM] + [VMEM] * 5,
        scratch_shapes=[
            pltpu.VMEM((4, ROWS, CW), BF16),
            pltpu.VMEM((4, ROWS, CW), BF16),
            pltpu.VMEM((4, CW, PER_BRICK), BF16),
            pltpu.VMEM((4, SNAPS, FIELDS, PER_BRICK), BF16),
            pltpu.SemaphoreType.DMA((2, 4)),
            pltpu.SemaphoreType.DMA((4,)),
            pltpu.SemaphoreType.DMA((4,)),
            pltpu.SemaphoreType.DMA,
            pltpu.SemaphoreType.DMA((4,)),
        ],
        out_shape=[
            jax.ShapeDtypeStruct((SNAPS, FIELDS, BRICKS * PER_BRICK), BF16),
            jax.ShapeDtypeStruct((EXT, 2 * COEFS, CW), BF16),
            jax.ShapeDtypeStruct((2, COEFS, CW), F32),
            jax.ShapeDtypeStruct((ROWS, 4 * COEFS), BF16),
            jax.ShapeDtypeStruct((4, CW, PER_BRICK), BF16),
            jax.ShapeDtypeStruct((1, BRICKS), jnp.int32),
        ],
        compiler_params=params(48),
        cost_estimate=pl.CostEstimate(flops=4_000_000_000, bytes_accessed=14_000_000, transcendentals=0),
        name="inner",
    )(basis, down, up, from_below, from_above, columns, head, rest, hots)


def outer_kernel(filled_hbm, whole_ref, ends_ref, below, above, spread_ref, hots, columns, out_hbm, held, out_sems):
    del filled_hbm
    whole = [whole_ref[k] for k in range(EXT)]
    for k, received in ((0, below), (EXT - 1, above)):
        whole[k] = jnp.concatenate(halves(ends_ref[k // CX] + received[...]), axis=0)
    outputs = []
    for i, brick in enumerate(OUTER):
        column = column_of(columns, brick, whole)
        outputs.append(write_brick(brick, column, hots[i], spread_ref[...], held.at[i], out_hbm, out_sems.at[i]))
    wait(outputs)


def outer_fields(filled, whole, ends, below, above, spread, hots, columns):
    return pl.pallas_call(
        outer_kernel,
        in_specs=[HBM] + [VMEM] * 7,
        out_specs=HBM,
        scratch_shapes=[
            pltpu.VMEM((4, SNAPS, FIELDS, PER_BRICK), BF16),
            pltpu.SemaphoreType.DMA((4,)),
        ],
        out_shape=jax.ShapeDtypeStruct(filled.shape, BF16),
        input_output_aliases={0: 0},
        compiler_params=params(32),
        name="outer",
    )(filled, whole, ends, below, above, spread, hots, columns)


def on_device(atom_values, atom_cell, brick_column):
    count = lax.axis_size("gx")
    to_lower = [((i + 1) % count, i) for i in range(count)]
    to_upper = [(i, (i + 1) % count) for i in range(count)]
    cells = atom_cell.reshape(BRICKS * LANES, 128)
    columns = brick_column.reshape(1, BRICKS)
    low, high, passed = face_sums(atom_values, cells, columns)
    from_above = lax.ppermute(low, "gx", to_lower)
    from_below = lax.ppermute(high, "gx", to_upper)
    head, rest, hots, faces, gram = local_sums(atom_values, passed, brick_column)
    packed = add_over_devices(packed_gram(gram, faces, from_below, from_above))
    basis, down, up = basis_and_faces(packed, head, rest)
    above = lax.ppermute(down, "gx", to_lower)
    below = lax.ppermute(up, "gx", to_upper)
    filled, whole, ends, spread, edge_hots, columns = inner_fields(
        basis, down, up, from_below, from_above, columns, head, rest, hots
    )
    return outer_fields(filled, whole, ends, below, above, spread, edge_hots, columns)


def solution(mesh):
    in_specs = (P(None, None, ("gx", "gz")), P(("gx", "gz")), P(("gx", "gz")))
    out_specs = P(None, None, ("gx", "gz"))
    return jax.shard_map(on_device, mesh=mesh, in_specs=in_specs, out_specs=out_specs, check_vma=False)
```

```python
import math

import jax
import jax.numpy as jnp
from jax import lax
from jax.experimental import pallas as pl
from jax.experimental.pallas import tpu as pltpu
from jax.sharding import PartitionSpec as P

SNAPS = 160
FIELDS = 4
ROWS = SNAPS * FIELDS
MODES = 8
SWEEPS = 3
CX = 4
EXT = CX + 2
CW = 512
PER_BRICK = 512
BRICKS = 8
COEFS = MODES * FIELDS
WIRE = ROWS + 16
TOP = 32767.0
STEPS = 8 / math.log(2)
SPLIT = 128
TAIL = SNAPS - SPLIT
LANES = CW // 128
F32 = jnp.float32
BF16 = jnp.bfloat16
NT = (((1,), (1,)), ((), ()))
TN = (((0,), (0,)), ((), ()))


def params(mib):
    return pltpu.CompilerParams(vmem_limit_bytes=mib * 1024 * 1024)


def dot_nt(a, b):
    return lax.dot_general(a, b, NT, preferred_element_type=F32)


def dot(a, b):
    return jnp.dot(a, b, preferred_element_type=F32)


def exact_dot(a, b):
    return jnp.dot(a, b, precision=lax.Precision.HIGHEST, preferred_element_type=F32)


def cell_hot(cells, brick, keep=None):
    ids = lax.broadcasted_iota(jnp.int32, (CW, 128), 0)
    tiles = []
    for t in range(LANES):
        row = cells[brick * LANES + t : brick * LANES + t + 1, :]
        if keep is not None:
            row = jnp.where(keep, row, -1)
        tiles.append((ids == row).astype(F32).astype(BF16))
    return jnp.concatenate(tiles, axis=1)


def halves(x):
    head = x.astype(BF16)
    return head, (x - head.astype(F32)).astype(BF16)


def one_field(total, field):
    rows = pl.ds(field, SNAPS, stride=FIELDS)
    return jnp.concatenate([total[t, rows, :] for t in range(LANES)], axis=1)


def brick_copy(values_hbm, held, sems, brick, slot):
    source = values_hbm.at[:, :, pl.ds(brick * PER_BRICK, PER_BRICK)]
    return pltpu.make_async_copy(source, held.at[slot], sems.at[slot])


def encode(total, out_ref):
    for t in range(LANES):
        lanes = slice(t * 128, (t + 1) * 128)
        most = jnp.max(jnp.abs(total[t]), axis=0, keepdims=True)
        code = jnp.ceil(jnp.log(jnp.maximum(most, 1e-30)) * STEPS)
        scale = jnp.exp(code * (-1 / STEPS)) * TOP
        for f in range(FIELDS):
            steps = jnp.round(total[t, pl.ds(f, SNAPS, stride=FIELDS), :] * scale)
            out_ref[f * SNAPS : (f + 1) * SNAPS, lanes] = jnp.clip(steps, -TOP, TOP).astype(jnp.int32).astype(jnp.int16)
        out_ref[ROWS:, lanes] = jnp.broadcast_to(code, (WIRE - ROWS, 128)).astype(jnp.int32).astype(jnp.int16)


def wire_steps(wire, rows):
    return wire[rows, :].astype(jnp.int32).astype(F32)


def wire_scale(wire):
    return jnp.exp(wire_steps(wire, slice(ROWS, WIRE))[:1] * (1 / STEPS)) * (1 / TOP)


HBM = pl.BlockSpec(memory_space=pltpu.HBM)
VMEM = pl.BlockSpec(memory_space=pltpu.VMEM)
SMEM = pl.BlockSpec(memory_space=pltpu.SMEM)


def faces_kernel(
    values_hbm, cells_hbm, column_hbm, low_hbm, high_hbm, passed_hbm, held, total, face, cells, columns, sems, small, out_sems
):
    bricks = (0, 1, BRICKS - 2, BRICKS - 1)
    targets = ((0, low_hbm), (EXT - 1, high_hbm))
    inputs = [
        pltpu.make_async_copy(cells_hbm, cells, small.at[0]),
        pltpu.make_async_copy(column_hbm, columns, small.at[1]),
    ]
    copies = [brick_copy(values_hbm, held, sems, brick, slot) for slot, brick in enumerate(bricks)]
    outputs = [pltpu.make_async_copy(face.at[i], out, out_sems.at[i]) for i, (_, out) in enumerate(targets)]
    for copy in inputs + copies:
        copy.start()
    for copy in inputs:
        copy.wait()
    outputs.append(pltpu.make_async_copy(cells, passed_hbm, out_sems.at[2]))
    outputs[2].start()
    hots = [
        cell_hot(cells, brick, columns[:, brick : brick + 1] == targets[slot // 2][0]) for slot, brick in enumerate(bricks)
    ]
    for i in range(2):
        sums = None
        for slot in (2 * i, 2 * i + 1):
            copies[slot].wait()
            part = dot_nt(held[slot].reshape(ROWS, PER_BRICK), hots[slot])
            sums = part if sums is None else sums + part
        for t in range(LANES):
            total[i, t] = sums[:, t * 128 : (t + 1) * 128]
        encode(total.at[i], face.at[i])
        outputs[i].start()
    for copy in outputs:
        copy.wait()


def face_sums(values, cells, columns):
    shape = jax.ShapeDtypeStruct((WIRE, CW), jnp.int16)
    return pl.pallas_call(
        faces_kernel,
        in_specs=[HBM] * 3,
        out_specs=[HBM] * 3,
        scratch_shapes=[
            pltpu.VMEM((4, SNAPS, FIELDS, PER_BRICK), BF16),
            pltpu.VMEM((2, LANES, ROWS, 128), F32),
            pltpu.VMEM((2, WIRE, CW), jnp.int16),
            pltpu.VMEM((BRICKS * LANES, 128), jnp.int32),
            pltpu.VMEM((1, BRICKS), jnp.int32),
            pltpu.SemaphoreType.DMA((4,)),
            pltpu.SemaphoreType.DMA((2,)),
            pltpu.SemaphoreType.DMA((3,)),
        ],
        out_shape=[shape, shape, jax.ShapeDtypeStruct((BRICKS * LANES, 128), jnp.int32)],
        compiler_params=params(63),
        name="faces",
    )(values, cells, columns)


def local_kernel(
    column_ref, values_hbm, cells_hbm, heads, rests, hots, gram_ref, cells, held, total, sems, small
):
    ids = pltpu.make_async_copy(cells_hbm, cells, small)
    ids.start()
    copies = [brick_copy(values_hbm, held, sems, brick, brick) for brick in range(BRICKS)]
    for copy in copies:
        copy.start()
    total[...] = jnp.zeros_like(total)
    ids.wait()
    for brick in range(BRICKS):
        hot = cell_hot(cells, brick)
        hots[brick] = hot
        copies[brick].wait()
        sums = dot_nt(held[brick].reshape(ROWS, PER_BRICK), hot)
        column = column_ref[brick]
        for t in range(LANES):
            total[column, t] += sums[:, t * 128 : (t + 1) * 128]
    same = jnp.zeros((SNAPS, SNAPS), F32)
    mixed = jnp.zeros((SNAPS, SNAPS), F32)
    for k in range(EXT):
        for f in range(FIELDS):
            rows = slice(f * SNAPS, (f + 1) * SNAPS)
            head, rest = halves(one_field(total.at[k], f))
            heads[k, rows, :] = head
            rests[k, rows, :] = rest
            same += dot_nt(head, head)
            mixed += dot_nt(head, rest)
    gram_ref[...] = same + mixed + mixed.T


def local_sums(values, cells, columns):
    half = jax.ShapeDtypeStruct((EXT, ROWS, CW), BF16)
    return pl.pallas_call(
        local_kernel,
        in_specs=[SMEM, HBM, HBM],
        out_specs=[VMEM] * 4,
        scratch_shapes=[
            pltpu.VMEM((BRICKS * LANES, 128), jnp.int32),
            pltpu.VMEM((BRICKS, SNAPS, FIELDS, PER_BRICK), BF16),
            pltpu.VMEM((EXT, LANES, ROWS, 128), F32),
            pltpu.SemaphoreType.DMA((BRICKS,)),
            pltpu.SemaphoreType.DMA,
        ],
        out_shape=[
            half,
            half,
            jax.ShapeDtypeStruct((BRICKS, CW, PER_BRICK), BF16),
            jax.ShapeDtypeStruct((SNAPS, SNAPS), F32),
        ],
        compiler_params=params(42),
        cost_estimate=pl.CostEstimate(flops=6_000_000_000, bytes_accessed=14_000_000, transcendentals=0),
        name="local",
    )(columns, values, cells)


def pack(gram):
    body = gram[:SPLIT, :SPLIT]
    side = gram[:SPLIT, SPLIT:]
    corner = gram[SPLIT:, SPLIT:]
    t = TAIL
    rows = [
        body[:t],
        jnp.concatenate([side[:t], body[t : 2 * t, t:]], axis=1),
        jnp.concatenate([side[t : 2 * t], side[2 * t : 3 * t], body[2 * t : 3 * t, 2 * t :]], axis=1),
        jnp.concatenate([side[3 * t :], corner, corner, body[3 * t :, 3 * t :]], axis=1),
    ]
    return jnp.concatenate(rows, axis=0)


def unpack(packed):
    t = TAIL
    row = lax.broadcasted_iota(jnp.int32, (SPLIT, SPLIT), 0) // t
    col = lax.broadcasted_iota(jnp.int32, (SPLIT, SPLIT), 1) // t
    above = jnp.where(col > row, packed, 0.0)
    body = jnp.where(col == row, packed, 0.0) + above + above.T
    side = jnp.concatenate(
        [packed[t : 2 * t, :t], packed[2 * t : 3 * t, :t], packed[2 * t : 3 * t, t : 2 * t], packed[3 * t :, :t]], axis=0
    )
    corner = packed[3 * t :, t : 2 * t]
    top = jnp.concatenate([body, side], axis=1)
    padded = jnp.concatenate([side, jnp.zeros((SPLIT, SPLIT - t), F32)], axis=1)
    bottom = jnp.concatenate([padded.T[:t], corner], axis=1)
    return jnp.concatenate([top, bottom], axis=0)


def cross_kernel(gram_ref, heads, rests, from_below, from_above, packed_ref):
    cross = jnp.zeros((SNAPS, SNAPS), F32)
    for k, received in ((1, from_below), (CX, from_above)):
        scale = wire_scale(received)
        for f in range(FIELDS):
            rows = slice(f * SNAPS, (f + 1) * SNAPS)
            head, rest = halves(wire_steps(received, rows) * scale)
            own = heads[k, rows, :]
            cross += dot_nt(own, head) + dot_nt(own, rest) + dot_nt(rests[k, rows, :], head)
    packed_ref[...] = pack(gram_ref[...] + cross + cross.T)


def packed_gram(gram, heads, rests, from_below, from_above):
    return pl.pallas_call(
        cross_kernel,
        in_specs=[VMEM] * 5,
        out_specs=VMEM,
        out_shape=jax.ShapeDtypeStruct((SPLIT, SPLIT), F32),
        compiler_params=params(16),
        name="cross",
    )(gram, heads, rests, from_below, from_above)


def sum_kernel(parts, out_ref):
    out_ref[...] = jnp.broadcast_to(parts[...].sum(0), out_ref.shape)


def summed_copies(parts, copies):
    return pl.pallas_call(
        sum_kernel,
        in_specs=[VMEM],
        out_specs=VMEM,
        out_shape=jax.ShapeDtypeStruct((copies,) + parts.shape[1:], F32),
        compiler_params=params(2),
        name="sum",
    )(parts)


def add_over_devices(x):
    axes = ("gx", "gz")
    depth = 8
    planes = [[i * 8 + j for i in range(z, 32, depth) for j in range(8)] for z in range(depth)]
    lines = [list(line) for line in zip(*planes)]
    size = len(planes[0])

    def trade(parts, groups):
        return lax.all_to_all(parts, axes, 0, 0, axis_index_groups=groups, tiled=True)

    shape = (SPLIT // size, SPLIT)
    mine = summed_copies(trade(x.reshape((size,) + shape), planes), depth)
    mine = summed_copies(trade(mine, lines), size)
    return trade(mine, planes).reshape(SPLIT, SPLIT)


def orthonormal(basis):
    inner = lax.dot_general(basis, basis, NT, precision=lax.Precision.HIGHEST, preferred_element_type=F32)
    row = lax.broadcasted_iota(jnp.int32, (MODES, 1), 0)
    columns = [jnp.broadcast_to(inner[:, j : j + 1], (MODES, 128)) for j in range(MODES)]
    wide = jnp.concatenate([basis, jnp.zeros((MODES, 256 - SNAPS), F32)], axis=1)
    parts = [wide[:, :128], wide[:, 128:]]
    scale = jnp.zeros((MODES, 128), F32)
    for j in range(MODES):
        pivot = columns[j][j : j + 1, :]
        scale = jnp.where(row == j, lax.rsqrt(pivot), scale)
        factor = jnp.where(row > j, columns[j] * (1.0 / pivot), 0.0)
        for k in range(j + 1, MODES):
            columns[k] = columns[k] - factor * columns[k][j : j + 1, :]
        parts = [part - factor * part[j : j + 1, :] for part in parts]
    return jnp.concatenate([part * scale for part in parts], axis=1)[:, :SNAPS]


def spread_matrix(basis):
    snap = lax.broadcasted_iota(jnp.int32, (SNAPS, ROWS), 0)
    column = lax.broadcasted_iota(jnp.int32, (SNAPS, ROWS), 1)
    repeat = (snap == column // FIELDS).astype(F32).astype(BF16)
    both = dot(jnp.concatenate(halves(basis), axis=0), repeat)
    field = lax.broadcasted_iota(jnp.int32, (COEFS, ROWS), 0) // MODES
    mine = field == lax.broadcasted_iota(jnp.int32, (COEFS, ROWS), 1) % FIELDS
    head = jnp.where(mine, jnp.concatenate([both[:MODES]] * FIELDS, axis=0), 0.0)
    rest = jnp.where(mine, jnp.concatenate([both[MODES:]] * FIELDS, axis=0), 0.0)
    return jnp.concatenate([head, head, rest, jnp.zeros_like(rest)], axis=0).T.astype(BF16)


def start(copies):
    for copy in copies:
        copy.start()
    return copies


def wait(copies):
    for copy in copies:
        copy.wait()


def by_field(basis):
    tall = jnp.concatenate([jnp.concatenate([basis] * FIELDS, axis=1)] * FIELDS, axis=0)
    row_field = lax.broadcasted_iota(jnp.int32, (COEFS, ROWS), 0) // MODES
    col_field = lax.broadcasted_iota(jnp.int32, (COEFS, ROWS), 1) // SNAPS
    return jnp.concatenate(halves(jnp.where(row_field == col_field, tall, 0.0)), axis=0)


def coefficients(both, head, rest):
    pair = dot(both, head)
    return pair[:COEFS] + pair[COEFS:] + dot(both[:COEFS], rest)


def basis_kernel(packed_ref, heads, rests, basis_ref, down_ref, up_ref):
    gram = unpack(packed_ref[...])
    basis = gram[:MODES, :]
    for _ in range(SWEEPS):
        basis = orthonormal(exact_dot(basis, gram))
    basis_ref[...] = basis
    both = by_field(basis)
    down_ref[...] = coefficients(both, heads[1], rests[1])
    up_ref[...] = coefficients(both, heads[CX], rests[CX])


def basis_and_faces(packed, heads, rests):
    side = jax.ShapeDtypeStruct((COEFS, CW), F32)
    return pl.pallas_call(
        basis_kernel,
        in_specs=[VMEM] * 3,
        out_specs=[VMEM] * 3,
        out_shape=[jax.ShapeDtypeStruct((MODES, SNAPS), F32), side, side],
        compiler_params=params(16),
        name="basis",
    )(packed, heads, rests)


def column_of(columns, brick, whole):
    mine = whole[0]
    for k in range(1, EXT):
        mine = jnp.where(columns[:, brick : brick + 1] == k, whole[k], mine)
    return mine


def write_brick(brick, column, hot, spread, held, out_hbm, sem):
    picked = dot(column, hot).astype(BF16)
    blank = jnp.zeros((COEFS, PER_BRICK), BF16)
    stacked = jnp.concatenate([picked, picked[:COEFS], blank], axis=0)
    held[...] = dot(spread, stacked).astype(BF16).reshape(SNAPS, FIELDS, PER_BRICK)
    copy = pltpu.make_async_copy(held, out_hbm.at[:, :, pl.ds(brick * PER_BRICK, PER_BRICK)], sem)
    copy.start()
    return copy


INNER = range(2, BRICKS - 2)
OUTER = (0, 1, BRICKS - 2, BRICKS - 1)


def inner_kernel(
    basis_ref, down_ref, up_ref, from_below, from_above, columns, heads, rests, hots,
    out_hbm, whole_ref, ends_ref, spread_ref, held, out_sems
):
    both = by_field(basis_ref[...])
    spread_ref[...] = spread_matrix(basis_ref[...])
    whole = [jnp.zeros((2 * COEFS, CW), BF16)] * EXT
    for k, mine, wire in ((1, down_ref, from_below), (CX, up_ref, from_above)):
        other = coefficients(both, *halves(wire_steps(wire, slice(0, ROWS))))
        whole[k] = jnp.concatenate(halves(mine[...] + other * wire_scale(wire)), axis=0)
    for k in (2, 3):
        whole[k] = jnp.concatenate(halves(coefficients(both, heads[k], rests[k])), axis=0)
    outputs = []
    for i, brick in enumerate(INNER):
        column = column_of(columns, brick, whole)
        outputs.append(write_brick(brick, column, hots[brick], spread_ref[...], held.at[i], out_hbm, out_sems.at[i]))
    for k in range(EXT):
        whole_ref[k] = whole[k]
    for i, k in enumerate((0, EXT - 1)):
        ends_ref[i] = coefficients(both, heads[k], rests[k])
    wait(outputs)


def inner_fields(basis, down, up, from_below, from_above, columns, heads, rests, hots):
    return pl.pallas_call(
        inner_kernel,
        in_specs=[VMEM] * 9,
        out_specs=[HBM] + [VMEM] * 3,
        scratch_shapes=[
            pltpu.VMEM((4, SNAPS, FIELDS, PER_BRICK), BF16),
            pltpu.SemaphoreType.DMA((4,)),
        ],
        out_shape=[
            jax.ShapeDtypeStruct((SNAPS, FIELDS, BRICKS * PER_BRICK), BF16),
            jax.ShapeDtypeStruct((EXT, 2 * COEFS, CW), BF16),
            jax.ShapeDtypeStruct((2, COEFS, CW), F32),
            jax.ShapeDtypeStruct((ROWS, 4 * COEFS), BF16),
        ],
        compiler_params=params(24),
        cost_estimate=pl.CostEstimate(flops=4_000_000_000, bytes_accessed=14_000_000, transcendentals=0),
        name="inner",
    )(basis, down, up, from_below, from_above, columns, heads, rests, hots)


def outer_kernel(filled_hbm, whole_ref, ends_ref, below, above, spread_ref, hots, columns, out_hbm, held, out_sems):
    del filled_hbm
    whole = [whole_ref[k] for k in range(EXT)]
    for k, received in ((0, below), (EXT - 1, above)):
        whole[k] = jnp.concatenate(halves(ends_ref[k // CX] + received[...]), axis=0)
    outputs = []
    for i, brick in enumerate(OUTER):
        column = column_of(columns, brick, whole)
        outputs.append(write_brick(brick, column, hots[brick], spread_ref[...], held.at[i], out_hbm, out_sems.at[i]))
    wait(outputs)


def outer_fields(filled, whole, ends, below, above, spread, hots, columns):
    return pl.pallas_call(
        outer_kernel,
        in_specs=[HBM] + [VMEM] * 7,
        out_specs=HBM,
        scratch_shapes=[
            pltpu.VMEM((4, SNAPS, FIELDS, PER_BRICK), BF16),
            pltpu.SemaphoreType.DMA((4,)),
        ],
        out_shape=jax.ShapeDtypeStruct(filled.shape, BF16),
        input_output_aliases={0: 0},
        compiler_params=params(32),
        name="outer",
    )(filled, whole, ends, below, above, spread, hots, columns)


def on_device(atom_values, atom_cell, brick_column):
    count = lax.axis_size("gx")
    to_lower = [((i + 1) % count, i) for i in range(count)]
    to_upper = [(i, (i + 1) % count) for i in range(count)]
    cells = atom_cell.reshape(BRICKS * LANES, 128)
    columns = brick_column.reshape(1, BRICKS)
    low, high, passed = face_sums(atom_values, cells, columns)
    from_above = lax.ppermute(low, "gx", to_lower)
    from_below = lax.ppermute(high, "gx", to_upper)
    heads, rests, hots, gram = local_sums(atom_values, passed, brick_column)
    packed = add_over_devices(packed_gram(gram, heads, rests, from_below, from_above))
    basis, down, up = basis_and_faces(packed, heads, rests)
    above = lax.ppermute(down, "gx", to_lower)
    below = lax.ppermute(up, "gx", to_upper)
    filled, whole, ends, spread = inner_fields(basis, down, up, from_below, from_above, columns, heads, rests, hots)
    return outer_fields(filled, whole, ends, below, above, spread, hots, columns)


def solution(mesh):
    in_specs = (P(None, None, ("gx", "gz")), P(("gx", "gz")), P(("gx", "gz")))
    out_specs = P(None, None, ("gx", "gz"))
    return jax.shard_map(on_device, mesh=mesh, in_specs=in_specs, out_specs=out_specs, check_vma=False)
```

```python
import math

import jax
import jax.numpy as jnp
from jax import lax
from jax.experimental import pallas as pl
from jax.experimental.pallas import tpu as pltpu
from jax.sharding import PartitionSpec as P

SNAPS = 160
FIELDS = 4
ROWS = SNAPS * FIELDS
MODES = 8
SWEEPS = 3
CX = 4
EXT = CX + 2
CW = 512
PER_BRICK = 512
BRICKS = 8
COEFS = MODES * FIELDS
WIRE = ROWS + 16
TOP = 32767.0
STEPS = 8 / math.log(2)
SPLIT = 128
TAIL = SNAPS - SPLIT
LANES = CW // 128
F32 = jnp.float32
BF16 = jnp.bfloat16
NT = (((1,), (1,)), ((), ()))
TN = (((0,), (0,)), ((), ()))


def params(mib):
    return pltpu.CompilerParams(vmem_limit_bytes=mib * 1024 * 1024)


def dot_nt(a, b):
    return lax.dot_general(a, b, NT, preferred_element_type=F32)


def dot(a, b):
    return jnp.dot(a, b, preferred_element_type=F32)


def exact_dot(a, b):
    return jnp.dot(a, b, precision=lax.Precision.HIGHEST, preferred_element_type=F32)


def cell_hot(cells, brick, keep=None):
    ids = lax.broadcasted_iota(jnp.int32, (CW, 128), 0)
    tiles = []
    for t in range(LANES):
        row = cells[brick * LANES + t : brick * LANES + t + 1, :]
        if keep is not None:
            row = jnp.where(keep, row, -1)
        tiles.append((ids == row).astype(F32).astype(BF16))
    return jnp.concatenate(tiles, axis=1)


def halves(x):
    head = x.astype(BF16)
    return head, (x - head.astype(F32)).astype(BF16)


def one_field(total, field):
    rows = pl.ds(field, SNAPS, stride=FIELDS)
    return jnp.concatenate([total[t, rows, :] for t in range(LANES)], axis=1)


def brick_copy(values_hbm, held, sems, brick, slot):
    source = values_hbm.at[:, :, pl.ds(brick * PER_BRICK, PER_BRICK)]
    return pltpu.make_async_copy(source, held.at[slot], sems.at[slot])


def encode(total, out_ref):
    for t in range(LANES):
        lanes = slice(t * 128, (t + 1) * 128)
        most = jnp.max(jnp.abs(total[t]), axis=0, keepdims=True)
        code = jnp.ceil(jnp.log(jnp.maximum(most, 1e-30)) * STEPS)
        scale = jnp.exp(code * (-1 / STEPS)) * TOP
        for f in range(FIELDS):
            steps = jnp.round(total[t, pl.ds(f, SNAPS, stride=FIELDS), :] * scale)
            out_ref[f * SNAPS : (f + 1) * SNAPS, lanes] = jnp.clip(steps, -TOP, TOP).astype(jnp.int32).astype(jnp.int16)
        out_ref[ROWS:, lanes] = jnp.broadcast_to(code, (WIRE - ROWS, 128)).astype(jnp.int32).astype(jnp.int16)


def wire_steps(wire, rows):
    return wire[rows, :].astype(jnp.int32).astype(F32)


def wire_scale(wire):
    return jnp.exp(wire_steps(wire, slice(ROWS, WIRE))[:1] * (1 / STEPS)) * (1 / TOP)


HBM = pl.BlockSpec(memory_space=pltpu.HBM)
VMEM = pl.BlockSpec(memory_space=pltpu.VMEM)
SMEM = pl.BlockSpec(memory_space=pltpu.SMEM)


def faces_kernel(values_hbm, cells_hbm, column_hbm, low_ref, high_ref, cells, total, held, columns, sems, small):
    bricks = (0, 1, BRICKS - 2, BRICKS - 1)
    targets = ((0, low_ref), (EXT - 1, high_ref))
    inputs = [
        pltpu.make_async_copy(cells_hbm, cells, small.at[0]),
        pltpu.make_async_copy(column_hbm, columns, small.at[1]),
    ]
    copies = [brick_copy(values_hbm, held, sems, brick, slot) for slot, brick in enumerate(bricks)]
    for copy in inputs + copies:
        copy.start()
    for copy in inputs:
        copy.wait()
    hots = [
        cell_hot(cells, brick, columns[:, brick : brick + 1] == targets[slot // 2][0]) for slot, brick in enumerate(bricks)
    ]
    for i in range(2):
        sums = None
        for slot in (2 * i, 2 * i + 1):
            copies[slot].wait()
            part = dot_nt(held[slot].reshape(ROWS, PER_BRICK), hots[slot])
            sums = part if sums is None else sums + part
        for t in range(LANES):
            total[i, t] = sums[:, t * 128 : (t + 1) * 128]
        encode(total.at[i], targets[i][1])


def face_sums(values, cells, columns):
    shape = jax.ShapeDtypeStruct((WIRE, CW), jnp.int16)
    return pl.pallas_call(
        faces_kernel,
        in_specs=[HBM] * 3,
        out_specs=[VMEM] * 4,
        scratch_shapes=[
            pltpu.VMEM((4, SNAPS, FIELDS, PER_BRICK), BF16),
            pltpu.VMEM((1, BRICKS), jnp.int32),
            pltpu.SemaphoreType.DMA((4,)),
            pltpu.SemaphoreType.DMA((2,)),
        ],
        out_shape=[
            shape,
            shape,
            jax.ShapeDtypeStruct((BRICKS * LANES, 128), jnp.int32),
            jax.ShapeDtypeStruct((2, LANES, ROWS, 128), F32),
        ],
        compiler_params=params(50),
        name="faces",
    )(values, cells, columns)


def local_kernel(column_ref, values_hbm, cells, faces, heads, rests, hots, gram_ref, held, total, sems):
    copies = [brick_copy(values_hbm, held, sems, brick, brick - 1) for brick in range(1, BRICKS - 1)]
    for copy in copies:
        copy.start()
    total[...] = jnp.zeros_like(total)
    for brick in range(BRICKS):
        hot = cell_hot(cells, brick)
        hots[brick] = hot
        if brick in (0, BRICKS - 1):
            continue
        copies[brick - 1].wait()
        sums = dot_nt(held[brick - 1].reshape(ROWS, PER_BRICK), hot)
        column = column_ref[brick]
        place = jnp.where(column == EXT - 1, 0, column)
        for t in range(LANES):
            total[place, t] += sums[:, t * 128 : (t + 1) * 128]
    same = jnp.zeros((SNAPS, SNAPS), F32)
    mixed = jnp.zeros((SNAPS, SNAPS), F32)
    for k in range(EXT):
        source = faces.at[k // CX] if k in (0, EXT - 1) else total.at[k]
        for f in range(FIELDS):
            rows = slice(f * SNAPS, (f + 1) * SNAPS)
            head, rest = halves(one_field(source, f))
            heads[k, rows, :] = head
            rests[k, rows, :] = rest
            same += dot_nt(head, head)
            mixed += dot_nt(head, rest)
    gram_ref[...] = same + mixed + mixed.T


def local_sums(values, cells, columns, faces):
    half = jax.ShapeDtypeStruct((EXT, ROWS, CW), BF16)
    return pl.pallas_call(
        local_kernel,
        in_specs=[SMEM, HBM, VMEM, VMEM],
        out_specs=[VMEM] * 4,
        scratch_shapes=[
            pltpu.VMEM((BRICKS - 2, SNAPS, FIELDS, PER_BRICK), BF16),
            pltpu.VMEM((CX + 1, LANES, ROWS, 128), F32),
            pltpu.SemaphoreType.DMA((BRICKS - 2,)),
        ],
        out_shape=[
            half,
            half,
            jax.ShapeDtypeStruct((BRICKS, CW, PER_BRICK), BF16),
            jax.ShapeDtypeStruct((SNAPS, SNAPS), F32),
        ],
        compiler_params=params(39),
        cost_estimate=pl.CostEstimate(flops=6_000_000_000, bytes_accessed=14_000_000, transcendentals=0),
        name="local",
    )(columns, values, cells, faces)


def pack(gram):
    body = gram[:SPLIT, :SPLIT]
    side = gram[:SPLIT, SPLIT:]
    corner = gram[SPLIT:, SPLIT:]
    t = TAIL
    rows = [
        body[:t],
        jnp.concatenate([side[:t], body[t : 2 * t, t:]], axis=1),
        jnp.concatenate([side[t : 2 * t], side[2 * t : 3 * t], body[2 * t : 3 * t, 2 * t :]], axis=1),
        jnp.concatenate([side[3 * t :], corner, corner, body[3 * t :, 3 * t :]], axis=1),
    ]
    return jnp.concatenate(rows, axis=0)


def unpack(packed):
    t = TAIL
    row = lax.broadcasted_iota(jnp.int32, (SPLIT, SPLIT), 0) // t
    col = lax.broadcasted_iota(jnp.int32, (SPLIT, SPLIT), 1) // t
    above = jnp.where(col > row, packed, 0.0)
    body = jnp.where(col == row, packed, 0.0) + above + above.T
    side = jnp.concatenate(
        [packed[t : 2 * t, :t], packed[2 * t : 3 * t, :t], packed[2 * t : 3 * t, t : 2 * t], packed[3 * t :, :t]], axis=0
    )
    corner = packed[3 * t :, t : 2 * t]
    top = jnp.concatenate([body, side], axis=1)
    padded = jnp.concatenate([side, jnp.zeros((SPLIT, SPLIT - t), F32)], axis=1)
    bottom = jnp.concatenate([padded.T[:t], corner], axis=1)
    return jnp.concatenate([top, bottom], axis=0)


def cross_kernel(gram_ref, heads, rests, from_below, from_above, mine_ref, other_ref):
    cross = jnp.zeros((SNAPS, SNAPS), F32)
    for k, received in ((1, from_below), (CX, from_above)):
        scale = wire_scale(received)
        for f in range(FIELDS):
            rows = slice(f * SNAPS, (f + 1) * SNAPS)
            head, rest = halves(wire_steps(received, rows) * scale)
            own = heads[k, rows, :]
            cross += dot_nt(own, head) + dot_nt(own, rest) + dot_nt(rests[k, rows, :], head)
    packed = pack(gram_ref[...] + cross + cross.T)
    first = on_first_core()
    mine_ref[...] = jnp.where(first, packed[: SPLIT // 2], packed[SPLIT // 2 :])
    other_ref[...] = jnp.where(first, packed[SPLIT // 2 :], packed[: SPLIT // 2])


def packed_gram(gram, heads, rests, from_below, from_above):
    return pl.pallas_call(
        cross_kernel,
        in_specs=[VMEM] * 5,
        out_specs=[VMEM] * 2,
        out_shape=[jax.ShapeDtypeStruct((SPLIT // 2, SPLIT), F32)] * 2,
        compiler_params=params(16),
        name="cross",
    )(gram, heads, rests, from_below, from_above)


def on_first_core():
    return lax.rem(lax.axis_index("gz"), 2) == 0


def tree_sum(terms):
    while len(terms) > 1:
        terms = [a + b for a, b in zip(terms[::2], terms[1::2])]
    return terms[0]


def terms_kernel(*refs):
    out_ref = refs[-1]
    out_ref[...] = jnp.broadcast_to(tree_sum([ref[...] for ref in refs[:-1]]), out_ref.shape)


def parts_kernel(parts, out_ref):
    out_ref[...] = tree_sum([parts[i] for i in range(parts.shape[0])])


def small_sum(kernel, terms, shape):
    return pl.pallas_call(
        kernel,
        in_specs=[VMEM] * len(terms),
        out_specs=VMEM,
        out_shape=jax.ShapeDtypeStruct(shape, F32),
        compiler_params=params(4),
        name="sum",
    )(*terms)


def add_over_devices(mine, other):
    axes = ("gx", "gz")
    depth = 8
    places = [(a, z, y, c) for a in range(4) for z in range(depth) for y in range(4) for c in range(2)]
    number = {place: i for i, place in enumerate(places)}
    lines = [[number[a, z, y, c] for z in range(depth)] for a in range(4) for y in range(4) for c in range(2)]

    def move(x, target):
        return lax.ppermute(x, axes, [(number[place], number[target(*place)]) for place in places])

    def swap(x):
        return move(x, lambda a, z, y, c: (a, z, y, 1 - c))

    shape = mine.shape
    mine = small_sum(terms_kernel, [mine, swap(other)], shape)
    others = [move(mine, lambda a, z, y, c, k=k: (a ^ k, z, y, c)) for k in (1, 2, 3)]
    mine = small_sum(terms_kernel, [mine] + others, shape)
    others = [move(mine, lambda a, z, y, c, k=k: (a, z, y ^ k, c)) for k in (1, 2, 3)]
    copies = small_sum(terms_kernel, [mine] + others, (depth,) + shape)
    parts = lax.all_to_all(copies, axes, 0, 0, axis_index_groups=lines, tiled=True)
    mine = small_sum(parts_kernel, [parts], shape)
    return mine, swap(mine)


def orthonormal(basis):
    inner = lax.dot_general(basis, basis, NT, precision=lax.Precision.HIGHEST, preferred_element_type=F32)
    row = lax.broadcasted_iota(jnp.int32, (MODES, 1), 0)
    columns = [jnp.broadcast_to(inner[:, j : j + 1], (MODES, 128)) for j in range(MODES)]
    wide = jnp.concatenate([basis, jnp.zeros((MODES, 256 - SNAPS), F32)], axis=1)
    parts = [wide[:, :128], wide[:, 128:]]
    scale = jnp.zeros((MODES, 128), F32)
    for j in range(MODES):
        pivot = columns[j][j : j + 1, :]
        scale = jnp.where(row == j, lax.rsqrt(pivot), scale)
        factor = jnp.where(row > j, columns[j] * (1.0 / pivot), 0.0)
        for k in range(j + 1, MODES):
            columns[k] = columns[k] - factor * columns[k][j : j + 1, :]
        parts = [part - factor * part[j : j + 1, :] for part in parts]
    return jnp.concatenate([part * scale for part in parts], axis=1)[:, :SNAPS]


def spread_matrix(basis):
    snap = lax.broadcasted_iota(jnp.int32, (SNAPS, ROWS), 0)
    column = lax.broadcasted_iota(jnp.int32, (SNAPS, ROWS), 1)
    repeat = (snap == column // FIELDS).astype(F32).astype(BF16)
    both = dot(jnp.concatenate(halves(basis), axis=0), repeat)
    field = lax.broadcasted_iota(jnp.int32, (COEFS, ROWS), 0) // MODES
    mine = field == lax.broadcasted_iota(jnp.int32, (COEFS, ROWS), 1) % FIELDS
    head = jnp.where(mine, jnp.concatenate([both[:MODES]] * FIELDS, axis=0), 0.0)
    rest = jnp.where(mine, jnp.concatenate([both[MODES:]] * FIELDS, axis=0), 0.0)
    return jnp.concatenate([head, head, rest, jnp.zeros_like(rest)], axis=0).T.astype(BF16)


def start(copies):
    for copy in copies:
        copy.start()
    return copies


def wait(copies):
    for copy in copies:
        copy.wait()


def by_field(basis):
    tall = jnp.concatenate([jnp.concatenate([basis] * FIELDS, axis=1)] * FIELDS, axis=0)
    row_field = lax.broadcasted_iota(jnp.int32, (COEFS, ROWS), 0) // MODES
    col_field = lax.broadcasted_iota(jnp.int32, (COEFS, ROWS), 1) // SNAPS
    return jnp.concatenate(halves(jnp.where(row_field == col_field, tall, 0.0)), axis=0)


def coefficients(both, head, rest):
    pair = dot(both, head)
    return pair[:COEFS] + pair[COEFS:] + dot(both[:COEFS], rest)


def basis_kernel(mine_ref, other_ref, heads, rests, basis_ref, down_ref, up_ref):
    first = on_first_core()
    mine, other = mine_ref[...], other_ref[...]
    gram = unpack(jnp.concatenate([jnp.where(first, mine, other), jnp.where(first, other, mine)], axis=0))
    basis = gram[:MODES, :]
    for _ in range(SWEEPS):
        basis = orthonormal(exact_dot(basis, gram))
    basis_ref[...] = basis
    both = by_field(basis)
    down_ref[...] = coefficients(both, heads[1], rests[1])
    up_ref[...] = coefficients(both, heads[CX], rests[CX])


def basis_and_faces(mine, other, heads, rests):
    side = jax.ShapeDtypeStruct((COEFS, CW), F32)
    return pl.pallas_call(
        basis_kernel,
        in_specs=[VMEM] * 4,
        out_specs=[VMEM] * 3,
        out_shape=[jax.ShapeDtypeStruct((MODES, SNAPS), F32), side, side],
        compiler_params=params(16),
        name="basis",
    )(mine, other, heads, rests)


def column_of(columns, brick, whole):
    mine = whole[0]
    for k in range(1, EXT):
        mine = jnp.where(columns[:, brick : brick + 1] == k, whole[k], mine)
    return mine


def write_brick(brick, column, hot, spread, held, out_hbm, sem):
    picked = dot(column, hot).astype(BF16)
    blank = jnp.zeros((COEFS, PER_BRICK), BF16)
    stacked = jnp.concatenate([picked, picked[:COEFS], blank], axis=0)
    held[...] = dot(spread, stacked).astype(BF16).reshape(SNAPS, FIELDS, PER_BRICK)
    copy = pltpu.make_async_copy(held, out_hbm.at[:, :, pl.ds(brick * PER_BRICK, PER_BRICK)], sem)
    copy.start()
    return copy


INNER = range(2, BRICKS - 2)
OUTER = (0, 1, BRICKS - 2, BRICKS - 1)


def inner_kernel(
    basis_ref, down_ref, up_ref, from_below, from_above, columns, heads, rests, hots,
    out_hbm, whole_ref, ends_ref, spread_ref, held, out_sems
):
    both = by_field(basis_ref[...])
    spread_ref[...] = spread_matrix(basis_ref[...])
    whole = [jnp.zeros((2 * COEFS, CW), BF16)] * EXT
    for k, mine, wire in ((1, down_ref, from_below), (CX, up_ref, from_above)):
        other = coefficients(both, *halves(wire_steps(wire, slice(0, ROWS))))
        whole[k] = jnp.concatenate(halves(mine[...] + other * wire_scale(wire)), axis=0)
    for k in (2, 3):
        whole[k] = jnp.concatenate(halves(coefficients(both, heads[k], rests[k])), axis=0)
    outputs = []
    for i, brick in enumerate(INNER):
        column = column_of(columns, brick, whole)
        outputs.append(write_brick(brick, column, hots[brick], spread_ref[...], held.at[i], out_hbm, out_sems.at[i]))
    for k in range(EXT):
        whole_ref[k] = whole[k]
    for i, k in enumerate((0, EXT - 1)):
        ends_ref[i] = coefficients(both, heads[k], rests[k])
    wait(outputs)


def inner_fields(basis, down, up, from_below, from_above, columns, heads, rests, hots):
    return pl.pallas_call(
        inner_kernel,
        in_specs=[VMEM] * 9,
        out_specs=[HBM] + [VMEM] * 3,
        scratch_shapes=[
            pltpu.VMEM((4, SNAPS, FIELDS, PER_BRICK), BF16),
            pltpu.SemaphoreType.DMA((4,)),
        ],
        out_shape=[
            jax.ShapeDtypeStruct((SNAPS, FIELDS, BRICKS * PER_BRICK), BF16),
            jax.ShapeDtypeStruct((EXT, 2 * COEFS, CW), BF16),
            jax.ShapeDtypeStruct((2, COEFS, CW), F32),
            jax.ShapeDtypeStruct((ROWS, 4 * COEFS), BF16),
        ],
        compiler_params=params(24),
        cost_estimate=pl.CostEstimate(flops=4_000_000_000, bytes_accessed=14_000_000, transcendentals=0),
        name="inner",
    )(basis, down, up, from_below, from_above, columns, heads, rests, hots)


def outer_kernel(filled_hbm, whole_ref, ends_ref, below, above, spread_ref, hots, columns, out_hbm, held, out_sems):
    del filled_hbm
    whole = [whole_ref[k] for k in range(EXT)]
    for k, received in ((0, below), (EXT - 1, above)):
        whole[k] = jnp.concatenate(halves(ends_ref[k // CX] + received[...]), axis=0)
    outputs = []
    for i, brick in enumerate(OUTER):
        column = column_of(columns, brick, whole)
        outputs.append(write_brick(brick, column, hots[brick], spread_ref[...], held.at[i], out_hbm, out_sems.at[i]))
    wait(outputs)


def outer_fields(filled, whole, ends, below, above, spread, hots, columns):
    return pl.pallas_call(
        outer_kernel,
        in_specs=[HBM] + [VMEM] * 7,
        out_specs=HBM,
        scratch_shapes=[
            pltpu.VMEM((4, SNAPS, FIELDS, PER_BRICK), BF16),
            pltpu.SemaphoreType.DMA((4,)),
        ],
        out_shape=jax.ShapeDtypeStruct(filled.shape, BF16),
        input_output_aliases={0: 0},
        compiler_params=params(32),
        name="outer",
    )(filled, whole, ends, below, above, spread, hots, columns)


def on_device(atom_values, atom_cell, brick_column):
    count = lax.axis_size("gx")
    to_lower = [((i + 1) % count, i) for i in range(count)]
    to_upper = [(i, (i + 1) % count) for i in range(count)]
    cells = atom_cell.reshape(BRICKS * LANES, 128)
    columns = brick_column.reshape(1, BRICKS)
    low, high, passed, totals = face_sums(atom_values, cells, columns)
    from_above = lax.ppermute(low, "gx", to_lower)
    from_below = lax.ppermute(high, "gx", to_upper)
    heads, rests, hots, gram = local_sums(atom_values, passed, brick_column, totals)
    mine, other = add_over_devices(*packed_gram(gram, heads, rests, from_below, from_above))
    basis, down, up = basis_and_faces(mine, other, heads, rests)
    above = lax.ppermute(down, "gx", to_lower)
    below = lax.ppermute(up, "gx", to_upper)
    filled, whole, ends, spread = inner_fields(basis, down, up, from_below, from_above, columns, heads, rests, hots)
    return outer_fields(filled, whole, ends, below, above, spread, hots, columns)


def solution(mesh):
    in_specs = (P(None, None, ("gx", "gz")), P(("gx", "gz")), P(("gx", "gz")))
    out_specs = P(None, None, ("gx", "gz"))
    return jax.shard_map(on_device, mesh=mesh, in_specs=in_specs, out_specs=out_specs, check_vma=False)
```

```python
import functools
import math

import jax
import jax.numpy as jnp
from jax import lax
from jax.experimental import pallas as pl
from jax.experimental.pallas import tpu as pltpu
from jax.sharding import PartitionSpec as P

SNAPS = 160
FIELDS = 4
ROWS = SNAPS * FIELDS
MODES = 8
SWEEPS = 3
CX = 4
EXT = CX + 2
CW = 512
PER_BRICK = 512
BRICKS = 8
COEFS = MODES * FIELDS
PART = SNAPS // 2
PART_ROWS = PART * FIELDS
WIRE = PART_ROWS + 16
TOP = 32767.0
STEPS = 8 / math.log(2)
SPLIT = 128
TAIL = SNAPS - SPLIT
LANES = CW // 128
F32 = jnp.float32
BF16 = jnp.bfloat16
NT = (((1,), (1,)), ((), ()))
TN = (((0,), (0,)), ((), ()))


def params(mib):
    return pltpu.CompilerParams(vmem_limit_bytes=mib * 1024 * 1024)


def dot_nt(a, b):
    return lax.dot_general(a, b, NT, preferred_element_type=F32)


def dot(a, b):
    return jnp.dot(a, b, preferred_element_type=F32)


def exact_dot(a, b):
    return jnp.dot(a, b, precision=lax.Precision.HIGHEST, preferred_element_type=F32)


def cell_hot(cells, brick, keep=None):
    ids = lax.broadcasted_iota(jnp.int32, (CW, 128), 0)
    tiles = []
    for t in range(LANES):
        row = cells[brick * LANES + t : brick * LANES + t + 1, :]
        if keep is not None:
            row = jnp.where(keep, row, -1)
        tiles.append((ids == row).astype(F32).astype(BF16))
    return jnp.concatenate(tiles, axis=1)


def halves(x):
    head = x.astype(BF16)
    return head, (x - head.astype(F32)).astype(BF16)


def one_field(total, field):
    rows = pl.ds(field, total.shape[1] // FIELDS, stride=FIELDS)
    return jnp.concatenate([total[t, rows, :] for t in range(LANES)], axis=1)


def brick_copy(values_hbm, held, sems, brick, slot):
    source = values_hbm.at[:, :, pl.ds(brick * PER_BRICK, PER_BRICK)]
    return pltpu.make_async_copy(source, held.at[slot], sems.at[slot])


def encode(total, out_ref):
    for t in range(LANES):
        lanes = slice(t * 128, (t + 1) * 128)
        most = jnp.max(jnp.abs(total[t]), axis=0, keepdims=True)
        code = jnp.ceil(jnp.log(jnp.maximum(most, 1e-30)) * STEPS)
        scale = jnp.exp(code * (-1 / STEPS)) * TOP
        for f in range(FIELDS):
            steps = jnp.round(total[t, pl.ds(f, PART, stride=FIELDS), :] * scale)
            out_ref[f * PART : (f + 1) * PART, lanes] = jnp.clip(steps, -TOP, TOP).astype(jnp.int32).astype(jnp.int16)
        out_ref[PART_ROWS:, lanes] = jnp.broadcast_to(code, (WIRE - PART_ROWS, 128)).astype(jnp.int32).astype(jnp.int16)


def wire_steps(wire, rows):
    return wire[rows, :].astype(jnp.int32).astype(F32)


def wire_scale(wire):
    return jnp.exp(wire_steps(wire, slice(PART_ROWS, WIRE))[:1] * (1 / STEPS)) * (1 / TOP)


HBM = pl.BlockSpec(memory_space=pltpu.HBM)
VMEM = pl.BlockSpec(memory_space=pltpu.VMEM)
SMEM = pl.BlockSpec(memory_space=pltpu.SMEM)


def faces_kernel(part, values_hbm, cells_hbm, column_hbm, low_ref, high_ref, cells, columns, total, held, sems, small):
    bricks = (0, 1, BRICKS - 2, BRICKS - 1)
    targets = ((0, low_ref), (EXT - 1, high_ref))
    inputs = [
        pltpu.make_async_copy(cells_hbm, cells, small.at[0]),
        pltpu.make_async_copy(column_hbm, columns, small.at[1]),
    ]
    copies = []
    for slot, brick in enumerate(bricks):
        source = values_hbm.at[pl.ds(part * PART, PART), :, pl.ds(brick * PER_BRICK, PER_BRICK)]
        copies.append(pltpu.make_async_copy(source, held.at[slot], sems.at[slot]))
    for copy in inputs + copies:
        copy.start()
    for copy in inputs:
        copy.wait()
    hots = [
        cell_hot(cells, brick, columns[:, brick : brick + 1] == targets[slot // 2][0]) for slot, brick in enumerate(bricks)
    ]
    for i in range(2):
        sums = None
        for slot in (2 * i, 2 * i + 1):
            copies[slot].wait()
            part_sums = dot_nt(held[slot].reshape(PART_ROWS, PER_BRICK), hots[slot])
            sums = part_sums if sums is None else sums + part_sums
        for t in range(LANES):
            total[i, t] = sums[:, t * 128 : (t + 1) * 128]
        encode(total.at[i], targets[i][1])


def face_sums(part, values, cells, columns):
    shape = jax.ShapeDtypeStruct((WIRE, CW), jnp.int16)
    return pl.pallas_call(
        functools.partial(faces_kernel, part),
        in_specs=[HBM] * 3,
        out_specs=[VMEM] * 5,
        scratch_shapes=[
            pltpu.VMEM((4, PART, FIELDS, PER_BRICK), BF16),
            pltpu.SemaphoreType.DMA((4,)),
            pltpu.SemaphoreType.DMA((2,)),
        ],
        out_shape=[
            shape,
            shape,
            jax.ShapeDtypeStruct((BRICKS * LANES, 128), jnp.int32),
            jax.ShapeDtypeStruct((1, BRICKS), jnp.int32),
            jax.ShapeDtypeStruct((2, LANES, PART_ROWS, 128), F32),
        ],
        compiler_params=params((51, 50)[part]),
        cost_estimate=pl.CostEstimate(flops=1_400_000_000, bytes_accessed=4_000_000, transcendentals=0),
        name="faces",
    )(values, cells, columns)


def local_kernel(column_ref, values_hbm, cells, early, late, heads, rests, hots, gram_ref, held, total, sems):
    copies = [brick_copy(values_hbm, held, sems, brick, brick - 1) for brick in range(1, BRICKS - 1)]
    for copy in copies:
        copy.start()
    total[...] = jnp.zeros_like(total)
    for brick in range(BRICKS):
        hot = cell_hot(cells, brick)
        hots[brick] = hot
        if brick in (0, BRICKS - 1):
            continue
        copies[brick - 1].wait()
        sums = dot_nt(held[brick - 1].reshape(ROWS, PER_BRICK), hot)
        column = column_ref[brick]
        place = jnp.where(column == EXT - 1, 0, column)
        for t in range(LANES):
            total[place, t] += sums[:, t * 128 : (t + 1) * 128]
    same = jnp.zeros((SNAPS, SNAPS), F32)
    mixed = jnp.zeros((SNAPS, SNAPS), F32)
    for k in range(EXT):
        for f in range(FIELDS):
            rows = slice(f * SNAPS, (f + 1) * SNAPS)
            if k in (0, EXT - 1):
                sums = jnp.concatenate([one_field(early.at[k // CX], f), one_field(late.at[k // CX], f)], axis=0)
            else:
                sums = one_field(total.at[k], f)
            head, rest = halves(sums)
            heads[k, rows, :] = head
            rests[k, rows, :] = rest
            same += dot_nt(head, head)
            mixed += dot_nt(head, rest)
    gram_ref[...] = same + mixed + mixed.T


def local_sums(values, cells, columns, early, late):
    half = jax.ShapeDtypeStruct((EXT, ROWS, CW), BF16)
    return pl.pallas_call(
        local_kernel,
        in_specs=[SMEM, HBM, VMEM, VMEM, VMEM],
        out_specs=[VMEM] * 4,
        scratch_shapes=[
            pltpu.VMEM((BRICKS - 2, SNAPS, FIELDS, PER_BRICK), BF16),
            pltpu.VMEM((CX + 1, LANES, ROWS, 128), F32),
            pltpu.SemaphoreType.DMA((BRICKS - 2,)),
        ],
        out_shape=[
            half,
            half,
            jax.ShapeDtypeStruct((BRICKS, CW, PER_BRICK), BF16),
            jax.ShapeDtypeStruct((SNAPS, SNAPS), F32),
        ],
        compiler_params=params(39),
        cost_estimate=pl.CostEstimate(flops=6_000_000_000, bytes_accessed=14_000_000, transcendentals=0),
        name="local",
    )(columns, values, cells, early, late)


def pack(gram):
    body = gram[:SPLIT, :SPLIT]
    side = gram[:SPLIT, SPLIT:]
    corner = gram[SPLIT:, SPLIT:]
    t = TAIL
    rows = [
        body[:t],
        jnp.concatenate([side[:t], body[t : 2 * t, t:]], axis=1),
        jnp.concatenate([side[t : 2 * t], side[2 * t : 3 * t], body[2 * t : 3 * t, 2 * t :]], axis=1),
        jnp.concatenate([side[3 * t :], corner, corner, body[3 * t :, 3 * t :]], axis=1),
    ]
    return jnp.concatenate(rows, axis=0)


def unpack(packed):
    t = TAIL
    row = lax.broadcasted_iota(jnp.int32, (SPLIT, SPLIT), 0) // t
    col = lax.broadcasted_iota(jnp.int32, (SPLIT, SPLIT), 1) // t
    above = jnp.where(col > row, packed, 0.0)
    body = jnp.where(col == row, packed, 0.0) + above + above.T
    side = jnp.concatenate(
        [packed[t : 2 * t, :t], packed[2 * t : 3 * t, :t], packed[2 * t : 3 * t, t : 2 * t], packed[3 * t :, :t]], axis=0
    )
    corner = packed[3 * t :, t : 2 * t]
    top = jnp.concatenate([body, side], axis=1)
    padded = jnp.concatenate([side, jnp.zeros((SPLIT, SPLIT - t), F32)], axis=1)
    bottom = jnp.concatenate([padded.T[:t], corner], axis=1)
    return jnp.concatenate([top, bottom], axis=0)


def cross_terms(gram, heads, rests, early, late):
    cross = jnp.zeros((SNAPS, SNAPS), F32)
    scales = [wire_scale(wire) for wire in (early, late)]
    for f in range(FIELDS):
        part = slice(f * PART, (f + 1) * PART)
        steps = [wire_steps(wire, part) * scale for wire, scale in zip((early, late), scales)]
        head, rest = halves(jnp.concatenate(steps, axis=0))
        rows = slice(f * SNAPS, (f + 1) * SNAPS)
        own = heads[rows, :]
        cross += dot_nt(own, head) + dot_nt(own, rest) + dot_nt(rests[rows, :], head)
    return gram + cross + cross.T


def below_kernel(gram_ref, heads, rests, early, late, out_ref):
    out_ref[...] = cross_terms(gram_ref[...], heads.at[1], rests.at[1], early, late)


def above_kernel(gram_ref, heads, rests, early, late, mine_ref, other_ref):
    packed = pack(cross_terms(gram_ref[...], heads.at[CX], rests.at[CX], early, late))
    first = on_first_core()
    mine_ref[...] = jnp.where(first, packed[: SPLIT // 2], packed[SPLIT // 2 :])
    other_ref[...] = jnp.where(first, packed[SPLIT // 2 :], packed[: SPLIT // 2])


def packed_gram(gram, heads, rests, below, above):
    common = dict(compiler_params=params(16), cost_estimate=pl.CostEstimate(flops=400_000_000, bytes_accessed=3_000_000, transcendentals=0))
    gram = pl.pallas_call(
        below_kernel,
        in_specs=[VMEM] * 5,
        out_specs=VMEM,
        out_shape=jax.ShapeDtypeStruct((SNAPS, SNAPS), F32),
        name="below",
        **common,
    )(gram, heads, rests, *below)
    return pl.pallas_call(
        above_kernel,
        in_specs=[VMEM] * 5,
        out_specs=[VMEM] * 2,
        out_shape=[jax.ShapeDtypeStruct((SPLIT // 2, SPLIT), F32)] * 2,
        name="above",
        **common,
    )(gram, heads, rests, *above)


def on_first_core():
    return lax.rem(lax.axis_index("gz"), 2) == 0


def tree_sum(terms):
    while len(terms) > 1:
        terms = [a + b for a, b in zip(terms[::2], terms[1::2])]
    return terms[0]


def terms_kernel(*refs):
    out_ref = refs[-1]
    out_ref[...] = jnp.broadcast_to(tree_sum([ref[...] for ref in refs[:-1]]), out_ref.shape)


def parts_kernel(parts, out_ref):
    out_ref[...] = tree_sum([parts[i] for i in range(parts.shape[0])])


def small_sum(kernel, terms, shape):
    return pl.pallas_call(
        kernel,
        in_specs=[VMEM] * len(terms),
        out_specs=VMEM,
        out_shape=jax.ShapeDtypeStruct(shape, F32),
        compiler_params=params(4),
        name="sum",
    )(*terms)


def add_over_devices(mine, other):
    axes = ("gx", "gz")
    depth = 8
    places = [(a, z, y, c) for a in range(4) for z in range(depth) for y in range(4) for c in range(2)]
    number = {place: i for i, place in enumerate(places)}
    lines = [[number[a, z, y, c] for z in range(depth)] for a in range(4) for y in range(4) for c in range(2)]

    def move(x, target):
        return lax.ppermute(x, axes, [(number[place], number[target(*place)]) for place in places])

    def swap(x):
        return move(x, lambda a, z, y, c: (a, z, y, 1 - c))

    shape = mine.shape
    mine = small_sum(terms_kernel, [mine, swap(other)], shape)
    others = [move(mine, lambda a, z, y, c, k=k: (a ^ k, z, y, c)) for k in (1, 2, 3)]
    mine = small_sum(terms_kernel, [mine] + others, shape)
    others = [move(mine, lambda a, z, y, c, k=k: (a, z, y ^ k, c)) for k in (1, 2, 3)]
    copies = small_sum(terms_kernel, [mine] + others, (depth,) + shape)
    parts = lax.all_to_all(copies, axes, 0, 0, axis_index_groups=lines, tiled=True)
    mine = small_sum(parts_kernel, [parts], shape)
    return mine, swap(mine)


def orthonormal(basis):
    inner = lax.dot_general(basis, basis, NT, precision=lax.Precision.HIGHEST, preferred_element_type=F32)
    row = lax.broadcasted_iota(jnp.int32, (MODES, 1), 0)
    columns = [jnp.broadcast_to(inner[:, j : j + 1], (MODES, 128)) for j in range(MODES)]
    wide = jnp.concatenate([basis, jnp.zeros((MODES, 256 - SNAPS), F32)], axis=1)
    parts = [wide[:, :128], wide[:, 128:]]
    scale = jnp.zeros((MODES, 128), F32)
    for j in range(MODES):
        pivot = columns[j][j : j + 1, :]
        scale = jnp.where(row == j, lax.rsqrt(pivot), scale)
        factor = jnp.where(row > j, columns[j] * (1.0 / pivot), 0.0)
        for k in range(j + 1, MODES):
            columns[k] = columns[k] - factor * columns[k][j : j + 1, :]
        parts = [part - factor * part[j : j + 1, :] for part in parts]
    return jnp.concatenate([part * scale for part in parts], axis=1)[:, :SNAPS]


def spread_matrix(basis):
    snap = lax.broadcasted_iota(jnp.int32, (SNAPS, ROWS), 0)
    column = lax.broadcasted_iota(jnp.int32, (SNAPS, ROWS), 1)
    repeat = (snap == column // FIELDS).astype(F32).astype(BF16)
    both = dot(jnp.concatenate(halves(basis), axis=0), repeat)
    field = lax.broadcasted_iota(jnp.int32, (COEFS, ROWS), 0) // MODES
    mine = field == lax.broadcasted_iota(jnp.int32, (COEFS, ROWS), 1) % FIELDS
    head = jnp.where(mine, jnp.concatenate([both[:MODES]] * FIELDS, axis=0), 0.0)
    rest = jnp.where(mine, jnp.concatenate([both[MODES:]] * FIELDS, axis=0), 0.0)
    return jnp.concatenate([head, head, rest, jnp.zeros_like(rest)], axis=0).T.astype(BF16)


def start(copies):
    for copy in copies:
        copy.start()
    return copies


def wait(copies):
    for copy in copies:
        copy.wait()


def by_field(basis):
    snaps = basis.shape[1]
    tall = jnp.concatenate([jnp.concatenate([basis] * FIELDS, axis=1)] * FIELDS, axis=0)
    row_field = lax.broadcasted_iota(jnp.int32, tall.shape, 0) // MODES
    col_field = lax.broadcasted_iota(jnp.int32, tall.shape, 1) // snaps
    return jnp.concatenate(halves(jnp.where(row_field == col_field, tall, 0.0)), axis=0)


def coefficients(both, head, rest):
    pair = dot(both, head)
    return pair[:COEFS] + pair[COEFS:] + dot(both[:COEFS], rest)


def basis_kernel(mine_ref, other_ref, heads, rests, basis_ref, down_ref, up_ref):
    first = on_first_core()
    mine, other = mine_ref[...], other_ref[...]
    gram = unpack(jnp.concatenate([jnp.where(first, mine, other), jnp.where(first, other, mine)], axis=0))
    basis = gram[:MODES, :]
    for _ in range(SWEEPS):
        basis = orthonormal(exact_dot(basis, gram))
    basis_ref[...] = basis
    both = by_field(basis)
    down_ref[...] = coefficients(both, heads[1], rests[1])
    up_ref[...] = coefficients(both, heads[CX], rests[CX])


def basis_and_faces(mine, other, heads, rests):
    side = jax.ShapeDtypeStruct((COEFS, CW), F32)
    return pl.pallas_call(
        basis_kernel,
        in_specs=[VMEM] * 4,
        out_specs=[VMEM] * 3,
        out_shape=[jax.ShapeDtypeStruct((MODES, SNAPS), F32), side, side],
        compiler_params=params(16),
        name="basis",
    )(mine, other, heads, rests)


def column_of(columns, brick, whole):
    mine = whole[0]
    for k in range(1, EXT):
        mine = jnp.where(columns[:, brick : brick + 1] == k, whole[k], mine)
    return mine


def write_brick(brick, column, hot, spread, held, out_hbm, sem):
    picked = dot(column, hot).astype(BF16)
    blank = jnp.zeros((COEFS, PER_BRICK), BF16)
    stacked = jnp.concatenate([picked, picked[:COEFS], blank], axis=0)
    held[...] = dot(spread, stacked).astype(BF16).reshape(SNAPS, FIELDS, PER_BRICK)
    copy = pltpu.make_async_copy(held, out_hbm.at[:, :, pl.ds(brick * PER_BRICK, PER_BRICK)], sem)
    copy.start()
    return copy


INNER = range(2, BRICKS - 2)
OUTER = (0, 1, BRICKS - 2, BRICKS - 1)


def inner_kernel(
    basis_ref, down_ref, up_ref, below_early, below_late, above_early, above_late, columns, heads, rests, hots,
    out_hbm, whole_ref, ends_ref, spread_ref, held, out_sems
):
    both = by_field(basis_ref[...])
    spread_ref[...] = spread_matrix(basis_ref[...])
    whole = [jnp.zeros((2 * COEFS, CW), BF16)] * EXT
    parts = [by_field(basis_ref[...][:, h * PART : (h + 1) * PART]) for h in range(2)]
    for k, mine, wires in ((1, down_ref, (below_early, below_late)), (CX, up_ref, (above_early, above_late))):
        value = mine[...]
        for part, wire in zip(parts, wires):
            value += coefficients(part, *halves(wire_steps(wire, slice(0, PART_ROWS)))) * wire_scale(wire)
        whole[k] = jnp.concatenate(halves(value), axis=0)
    for k in (2, 3):
        whole[k] = jnp.concatenate(halves(coefficients(both, heads[k], rests[k])), axis=0)
    outputs = []
    for i, brick in enumerate(INNER):
        column = column_of(columns, brick, whole)
        outputs.append(write_brick(brick, column, hots[brick], spread_ref[...], held.at[i], out_hbm, out_sems.at[i]))
    for k in range(EXT):
        whole_ref[k] = whole[k]
    for i, k in enumerate((0, EXT - 1)):
        ends_ref[i] = coefficients(both, heads[k], rests[k])
    wait(outputs)


def inner_fields(basis, down, up, below, above, columns, heads, rests, hots):
    return pl.pallas_call(
        inner_kernel,
        in_specs=[VMEM] * 11,
        out_specs=[HBM] + [VMEM] * 3,
        scratch_shapes=[
            pltpu.VMEM((4, SNAPS, FIELDS, PER_BRICK), BF16),
            pltpu.SemaphoreType.DMA((4,)),
        ],
        out_shape=[
            jax.ShapeDtypeStruct((SNAPS, FIELDS, BRICKS * PER_BRICK), BF16),
            jax.ShapeDtypeStruct((EXT, 2 * COEFS, CW), BF16),
            jax.ShapeDtypeStruct((2, COEFS, CW), F32),
            jax.ShapeDtypeStruct((ROWS, 4 * COEFS), BF16),
        ],
        compiler_params=params(24),
        cost_estimate=pl.CostEstimate(flops=4_000_000_000, bytes_accessed=14_000_000, transcendentals=0),
        name="inner",
    )(basis, down, up, *below, *above, columns, heads, rests, hots)


def outer_kernel(filled_hbm, whole_ref, ends_ref, below, above, spread_ref, hots, columns, out_hbm, held, out_sems):
    del filled_hbm
    whole = [whole_ref[k] for k in range(EXT)]
    for k, received in ((0, below), (EXT - 1, above)):
        whole[k] = jnp.concatenate(halves(ends_ref[k // CX] + received[...]), axis=0)
    outputs = []
    for i, brick in enumerate(OUTER):
        column = column_of(columns, brick, whole)
        outputs.append(write_brick(brick, column, hots[brick], spread_ref[...], held.at[i], out_hbm, out_sems.at[i]))
    wait(outputs)


def outer_fields(filled, whole, ends, below, above, spread, hots, columns):
    return pl.pallas_call(
        outer_kernel,
        in_specs=[HBM] + [VMEM] * 7,
        out_specs=HBM,
        scratch_shapes=[
            pltpu.VMEM((4, SNAPS, FIELDS, PER_BRICK), BF16),
            pltpu.SemaphoreType.DMA((4,)),
        ],
        out_shape=jax.ShapeDtypeStruct(filled.shape, BF16),
        input_output_aliases={0: 0},
        compiler_params=params(32),
        name="outer",
    )(filled, whole, ends, below, above, spread, hots, columns)


def on_device(atom_values, atom_cell, brick_column):
    count = lax.axis_size("gx")
    to_lower = [((i + 1) % count, i) for i in range(count)]
    to_upper = [(i, (i + 1) % count) for i in range(count)]
    cells = atom_cell.reshape(BRICKS * LANES, 128)
    columns = brick_column.reshape(1, BRICKS)
    below, above, totals = [], [], []
    for part in range(2):
        low, high, cells, columns, total = face_sums(part, atom_values, cells, columns)
        above.append(lax.ppermute(low, "gx", to_lower))
        below.append(lax.ppermute(high, "gx", to_upper))
        totals.append(total)
    heads, rests, hots, gram = local_sums(atom_values, cells, brick_column, *totals)
    mine, other = add_over_devices(*packed_gram(gram, heads, rests, below, above))
    basis, down, up = basis_and_faces(mine, other, heads, rests)
    end_above = lax.ppermute(down, "gx", to_lower)
    end_below = lax.ppermute(up, "gx", to_upper)
    filled, whole, ends, spread = inner_fields(basis, down, up, below, above, columns, heads, rests, hots)
    return outer_fields(filled, whole, ends, end_below, end_above, spread, hots, columns)


def solution(mesh):
    in_specs = (P(None, None, ("gx", "gz")), P(("gx", "gz")), P(("gx", "gz")))
    out_specs = P(None, None, ("gx", "gz"))
    return jax.shard_map(on_device, mesh=mesh, in_specs=in_specs, out_specs=out_specs, check_vma=False)
```

```python
import functools
import math

import jax
import jax.numpy as jnp
from jax import lax
from jax.experimental import pallas as pl
from jax.experimental.pallas import tpu as pltpu
from jax.sharding import PartitionSpec as P

SNAPS = 160
FIELDS = 4
ROWS = SNAPS * FIELDS
MODES = 8
SWEEPS = 3
CX = 4
EXT = CX + 2
CW = 512
PER_BRICK = 512
BRICKS = 8
COEFS = MODES * FIELDS
PART = SNAPS // 2
PART_ROWS = PART * FIELDS
WIRE = PART_ROWS + 16
TOP = 32767.0
STEPS = 8 / math.log(2)
SPLIT = 128
TAIL = SNAPS - SPLIT
LANES = CW // 128
F32 = jnp.float32
BF16 = jnp.bfloat16
NT = (((1,), (1,)), ((), ()))
TN = (((0,), (0,)), ((), ()))


def params(mib):
    return pltpu.CompilerParams(vmem_limit_bytes=mib * 1024 * 1024)


def dot_nt(a, b):
    return lax.dot_general(a, b, NT, preferred_element_type=F32)


def dot(a, b):
    return jnp.dot(a, b, preferred_element_type=F32)


def exact_dot(a, b):
    return jnp.dot(a, b, precision=lax.Precision.HIGHEST, preferred_element_type=F32)


def cell_hot(cells, brick, keep=None):
    ids = lax.broadcasted_iota(jnp.int32, (CW, 128), 0)
    tiles = []
    for t in range(LANES):
        row = cells[brick * LANES + t : brick * LANES + t + 1, :]
        if keep is not None:
            row = jnp.where(keep, row, -1)
        tiles.append((ids == row).astype(F32).astype(BF16))
    return jnp.concatenate(tiles, axis=1)


def halves(x):
    head = x.astype(BF16)
    return head, (x - head.astype(F32)).astype(BF16)


def one_field(total, field):
    rows = pl.ds(field, total.shape[1] // FIELDS, stride=FIELDS)
    return jnp.concatenate([total[t, rows, :] for t in range(LANES)], axis=1)


def brick_copy(values_hbm, held, sems, brick, slot):
    source = values_hbm.at[:, :, pl.ds(brick * PER_BRICK, PER_BRICK)]
    return pltpu.make_async_copy(source, held.at[slot], sems.at[slot])


def encode(total, out_ref):
    for t in range(LANES):
        lanes = slice(t * 128, (t + 1) * 128)
        most = jnp.max(jnp.abs(total[t]), axis=0, keepdims=True)
        code = jnp.ceil(jnp.log(jnp.maximum(most, 1e-30)) * STEPS)
        scale = jnp.exp(code * (-1 / STEPS)) * TOP
        for f in range(FIELDS):
            steps = jnp.round(total[t, pl.ds(f, PART, stride=FIELDS), :] * scale)
            out_ref[f * PART : (f + 1) * PART, lanes] = jnp.clip(steps, -TOP, TOP).astype(jnp.int32).astype(jnp.int16)
        out_ref[PART_ROWS:, lanes] = jnp.broadcast_to(code, (WIRE - PART_ROWS, 128)).astype(jnp.int32).astype(jnp.int16)


def wire_steps(wire, rows):
    return wire[rows, :].astype(jnp.int32).astype(F32)


def wire_scale(wire):
    return jnp.exp(wire_steps(wire, slice(PART_ROWS, WIRE))[:1] * (1 / STEPS)) * (1 / TOP)


def start(copies):
    for copy in copies:
        copy.start()


def wait(copies):
    for copy in copies:
        copy.wait()


def column_id(ids, brick):
    return ids[BRICKS * LANES : BRICKS * LANES + 1, brick : brick + 1]


INNER = range(2, BRICKS - 2)
OUTER = (0, 1, BRICKS - 2, BRICKS - 1)
HBM = pl.BlockSpec(memory_space=pltpu.HBM)
VMEM = pl.BlockSpec(memory_space=pltpu.VMEM)
SMEM = pl.BlockSpec(memory_space=pltpu.SMEM)


def faces_kernel(part, values_hbm, ids_ref, low_ref, high_ref, total, *rest):
    bricks = (0, 1, BRICKS - 2, BRICKS - 1)
    targets = ((0, low_ref), (EXT - 1, high_ref))
    held, sems = rest[-2:]
    copies = []
    for slot, brick in enumerate(bricks):
        source = values_hbm.at[pl.ds(part * PART, PART), :, pl.ds(brick * PER_BRICK, PER_BRICK)]
        copies.append(pltpu.make_async_copy(source, held.at[slot], sems.at[slot]))
    start(copies)
    later = []
    if part:
        passed, outer_hots, later_sems = rest[:3]
        later = [brick_copy(values_hbm, passed, later_sems, brick, i) for i, brick in enumerate(INNER)]
        start(later)
    hots = [
        cell_hot(ids_ref, brick, column_id(ids_ref, brick) == targets[slot // 2][0]) for slot, brick in enumerate(bricks)
    ]
    if part:
        outer_hots[0] = hots[0]
        outer_hots[1] = hots[3]
    for i in range(2):
        sums = None
        for slot in (2 * i, 2 * i + 1):
            copies[slot].wait()
            part_sums = dot_nt(held[slot].reshape(PART_ROWS, PER_BRICK), hots[slot])
            sums = part_sums if sums is None else sums + part_sums
        for t in range(LANES):
            total[i, t] = sums[:, t * 128 : (t + 1) * 128]
        encode(total.at[i], targets[i][1])
    wait(later)


def face_sums(part, values, ids):
    shape = jax.ShapeDtypeStruct((WIRE, CW), jnp.int16)
    later_shapes = [
        jax.ShapeDtypeStruct((len(INNER), SNAPS, FIELDS, PER_BRICK), BF16),
        jax.ShapeDtypeStruct((2, CW, PER_BRICK), BF16),
    ]
    later_scratch = [pltpu.SemaphoreType.DMA((len(INNER),))]
    return pl.pallas_call(
        functools.partial(faces_kernel, part),
        in_specs=[HBM, VMEM],
        out_specs=[VMEM] * (3 + 2 * part),
        scratch_shapes=later_scratch * part
        + [
            pltpu.VMEM((4, PART, FIELDS, PER_BRICK), BF16),
            pltpu.SemaphoreType.DMA((4,)),
        ],
        out_shape=[shape, shape, jax.ShapeDtypeStruct((2, LANES, PART_ROWS, 128), F32)] + later_shapes * part,
        compiler_params=params((51, 46)[part]),
        cost_estimate=pl.CostEstimate(flops=1_400_000_000, bytes_accessed=4_000_000, transcendentals=0),
        name="faces",
    )(values, ids)


def local_kernel(
    column_ref, values_hbm, ids_ref, early, late, inner, outer_hots, heads, rests, hots, gram_ref, held, total, sems
):
    edges = (1, BRICKS - 2)
    copies = [brick_copy(values_hbm, held, sems, brick, i) for i, brick in enumerate(edges)]
    start(copies)
    total[...] = jnp.zeros_like(total)
    hots[0] = outer_hots[0]
    hots[BRICKS - 1] = outer_hots[1]
    for brick in tuple(INNER) + edges:
        hot = cell_hot(ids_ref, brick)
        hots[brick] = hot
        if brick in INNER:
            values = inner[brick - 2]
        else:
            copies[edges.index(brick)].wait()
            values = held[edges.index(brick)]
        sums = dot_nt(values.reshape(ROWS, PER_BRICK), hot)
        column = column_ref[brick]
        place = jnp.where(column == EXT - 1, 0, column)
        for t in range(LANES):
            total[place, t] += sums[:, t * 128 : (t + 1) * 128]
    both = jnp.zeros((2 * SNAPS, SNAPS), F32)
    for k in range(EXT):
        for f in range(FIELDS):
            rows = slice(f * SNAPS, (f + 1) * SNAPS)
            if k in (0, EXT - 1):
                sums = jnp.concatenate([one_field(early.at[k // CX], f), one_field(late.at[k // CX], f)], axis=0)
            else:
                sums = one_field(total.at[k], f)
            head, rest = halves(sums)
            heads[k, rows, :] = head
            rests[k, rows, :] = rest
            both += dot_nt(jnp.concatenate([head, rest], axis=0), head)
    mixed = both[SNAPS:]
    gram_ref[...] = both[:SNAPS] + mixed + mixed.T


def local_sums(values, ids, columns, early, late, inner, outer_hots):
    half = jax.ShapeDtypeStruct((EXT, ROWS, CW), BF16)
    return pl.pallas_call(
        local_kernel,
        in_specs=[SMEM, HBM] + [VMEM] * 5,
        out_specs=[VMEM] * 4,
        scratch_shapes=[
            pltpu.VMEM((2, SNAPS, FIELDS, PER_BRICK), BF16),
            pltpu.VMEM((CX + 1, LANES, ROWS, 128), F32),
            pltpu.SemaphoreType.DMA((2,)),
        ],
        out_shape=[
            half,
            half,
            jax.ShapeDtypeStruct((BRICKS, CW, PER_BRICK), BF16),
            jax.ShapeDtypeStruct((SNAPS, SNAPS), F32),
        ],
        compiler_params=params(36),
        cost_estimate=pl.CostEstimate(flops=6_000_000_000, bytes_accessed=14_000_000, transcendentals=0),
        name="local",
    )(columns, values, ids, early, late, inner, outer_hots)


def pack(gram):
    body = gram[:SPLIT, :SPLIT]
    side = gram[:SPLIT, SPLIT:]
    corner = gram[SPLIT:, SPLIT:]
    t = TAIL
    rows = [
        body[:t],
        jnp.concatenate([side[:t], body[t : 2 * t, t:]], axis=1),
        jnp.concatenate([side[t : 2 * t], side[2 * t : 3 * t], body[2 * t : 3 * t, 2 * t :]], axis=1),
        jnp.concatenate([side[3 * t :], corner, corner, body[3 * t :, 3 * t :]], axis=1),
    ]
    return jnp.concatenate(rows, axis=0)


def unpack(packed):
    t = TAIL
    row = lax.broadcasted_iota(jnp.int32, (SPLIT, SPLIT), 0) // t
    col = lax.broadcasted_iota(jnp.int32, (SPLIT, SPLIT), 1) // t
    above = jnp.where(col > row, packed, 0.0)
    body = jnp.where(col == row, packed, 0.0) + above + above.T
    side = jnp.concatenate(
        [packed[t : 2 * t, :t], packed[2 * t : 3 * t, :t], packed[2 * t : 3 * t, t : 2 * t], packed[3 * t :, :t]], axis=0
    )
    corner = packed[3 * t :, t : 2 * t]
    top = jnp.concatenate([body, side], axis=1)
    padded = jnp.concatenate([side, jnp.zeros((SPLIT, SPLIT - t), F32)], axis=1)
    bottom = jnp.concatenate([padded.T[:t], corner], axis=1)
    return jnp.concatenate([top, bottom], axis=0)


def cross_terms(gram, heads, rests, early, late):
    cross = jnp.zeros((SNAPS, SNAPS), F32)
    scales = [wire_scale(wire) for wire in (early, late)]
    for f in range(FIELDS):
        part = slice(f * PART, (f + 1) * PART)
        steps = [wire_steps(wire, part) * scale for wire, scale in zip((early, late), scales)]
        head, rest = halves(jnp.concatenate(steps, axis=0))
        rows = slice(f * SNAPS, (f + 1) * SNAPS)
        own = heads[rows, :]
        pair = dot_nt(jnp.concatenate([own, rests[rows, :]], axis=0), head)
        cross += pair[:SNAPS] + pair[SNAPS:] + dot_nt(own, rest)
    return gram + cross + cross.T


def below_kernel(gram_ref, heads, rests, early, late, out_ref):
    out_ref[...] = cross_terms(gram_ref[...], heads.at[1], rests.at[1], early, late)


def above_kernel(gram_ref, heads, rests, early, late, mine_ref, other_ref):
    packed = pack(cross_terms(gram_ref[...], heads.at[CX], rests.at[CX], early, late))
    first = on_first_core()
    mine_ref[...] = jnp.where(first, packed[: SPLIT // 2], packed[SPLIT // 2 :])
    other_ref[...] = jnp.where(first, packed[SPLIT // 2 :], packed[: SPLIT // 2])


def packed_gram(gram, heads, rests, below, above):
    common = dict(compiler_params=params(16), cost_estimate=pl.CostEstimate(flops=400_000_000, bytes_accessed=3_000_000, transcendentals=0))
    gram = pl.pallas_call(
        below_kernel,
        in_specs=[VMEM] * 5,
        out_specs=VMEM,
        out_shape=jax.ShapeDtypeStruct((SNAPS, SNAPS), F32),
        name="below",
        **common,
    )(gram, heads, rests, *below)
    return pl.pallas_call(
        above_kernel,
        in_specs=[VMEM] * 5,
        out_specs=[VMEM] * 2,
        out_shape=[jax.ShapeDtypeStruct((SPLIT // 2, SPLIT), F32)] * 2,
        name="above",
        **common,
    )(gram, heads, rests, *above)


def on_first_core():
    return lax.rem(lax.axis_index("gz"), 2) == 0


def tree_sum(terms):
    while len(terms) > 1:
        terms = [a + b for a, b in zip(terms[::2], terms[1::2])]
    return terms[0]


def terms_kernel(*refs):
    out_ref = refs[-1]
    out_ref[...] = jnp.broadcast_to(tree_sum([ref[...] for ref in refs[:-1]]), out_ref.shape)


def parts_kernel(parts, out_ref):
    out_ref[...] = tree_sum([parts[i] for i in range(parts.shape[0])])


def small_sum(kernel, terms, shape):
    return pl.pallas_call(
        kernel,
        in_specs=[VMEM] * len(terms),
        out_specs=VMEM,
        out_shape=jax.ShapeDtypeStruct(shape, F32),
        compiler_params=params(4),
        name="sum",
    )(*terms)


def add_over_devices(mine, other):
    axes = ("gx", "gz")
    depth = 8
    places = [(a, z, y, c) for a in range(4) for z in range(depth) for y in range(4) for c in range(2)]
    number = {place: i for i, place in enumerate(places)}
    lines = [[number[a, z, y, c] for z in range(depth)] for a in range(4) for y in range(4) for c in range(2)]

    def move(x, target):
        return lax.ppermute(x, axes, [(number[place], number[target(*place)]) for place in places])

    def swap(x):
        return move(x, lambda a, z, y, c: (a, z, y, 1 - c))

    shape = mine.shape
    mine = small_sum(terms_kernel, [mine, swap(other)], shape)
    others = [move(mine, lambda a, z, y, c, k=k: (a ^ k, z, y, c)) for k in (1, 2, 3)]
    mine = small_sum(terms_kernel, [mine] + others, shape)
    others = [move(mine, lambda a, z, y, c, k=k: (a, z, y ^ k, c)) for k in (1, 2, 3)]
    copies = small_sum(terms_kernel, [mine] + others, (depth,) + shape)
    parts = lax.all_to_all(copies, axes, 0, 0, axis_index_groups=lines, tiled=True)
    mine = small_sum(parts_kernel, [parts], shape)
    return mine, swap(mine)


def orthonormal(basis):
    inner = lax.dot_general(basis, basis, NT, precision=lax.Precision.HIGHEST, preferred_element_type=F32)
    row = lax.broadcasted_iota(jnp.int32, (MODES, 1), 0)
    columns = [jnp.broadcast_to(inner[:, j : j + 1], (MODES, 128)) for j in range(MODES)]
    wide = jnp.concatenate([basis, jnp.zeros((MODES, 256 - SNAPS), F32)], axis=1)
    parts = [wide[:, :128], wide[:, 128:]]
    scale = jnp.zeros((MODES, 128), F32)
    for j in range(MODES):
        pivot = columns[j][j : j + 1, :]
        scale = jnp.where(row == j, lax.rsqrt(pivot), scale)
        factor = jnp.where(row > j, columns[j] * (1.0 / pivot), 0.0)
        for k in range(j + 1, MODES):
            columns[k] = columns[k] - factor * columns[k][j : j + 1, :]
        parts = [part - factor * part[j : j + 1, :] for part in parts]
    return jnp.concatenate([part * scale for part in parts], axis=1)[:, :SNAPS]


def spread_matrix(basis):
    snap = lax.broadcasted_iota(jnp.int32, (SNAPS, ROWS), 0)
    column = lax.broadcasted_iota(jnp.int32, (SNAPS, ROWS), 1)
    repeat = (snap == column // FIELDS).astype(F32).astype(BF16)
    both = dot(jnp.concatenate(halves(basis), axis=0), repeat)
    field = lax.broadcasted_iota(jnp.int32, (COEFS, ROWS), 0) // MODES
    mine = field == lax.broadcasted_iota(jnp.int32, (COEFS, ROWS), 1) % FIELDS
    head = jnp.where(mine, jnp.concatenate([both[:MODES]] * FIELDS, axis=0), 0.0)
    rest = jnp.where(mine, jnp.concatenate([both[MODES:]] * FIELDS, axis=0), 0.0)
    return jnp.concatenate([head, head, rest, jnp.zeros_like(rest)], axis=0).T.astype(BF16)


def by_field(basis):
    snaps = basis.shape[1]
    tall = jnp.concatenate([jnp.concatenate([basis] * FIELDS, axis=1)] * FIELDS, axis=0)
    row_field = lax.broadcasted_iota(jnp.int32, tall.shape, 0) // MODES
    col_field = lax.broadcasted_iota(jnp.int32, tall.shape, 1) // snaps
    return jnp.concatenate(halves(jnp.where(row_field == col_field, tall, 0.0)), axis=0)


def coefficients(both, head, rest):
    pair = dot(both, head)
    return pair[:COEFS] + pair[COEFS:] + dot(both[:COEFS], rest)


def basis_kernel(mine_ref, other_ref, heads, rests, basis_ref, down_ref, up_ref):
    first = on_first_core()
    mine, other = mine_ref[...], other_ref[...]
    gram = unpack(jnp.concatenate([jnp.where(first, mine, other), jnp.where(first, other, mine)], axis=0))
    basis = gram[:MODES, :]
    for _ in range(SWEEPS):
        basis = orthonormal(exact_dot(basis, gram))
    basis_ref[...] = basis
    both = by_field(basis)
    down_ref[...] = coefficients(both, heads[1], rests[1])
    up_ref[...] = coefficients(both, heads[CX], rests[CX])


def basis_and_faces(mine, other, heads, rests):
    side = jax.ShapeDtypeStruct((COEFS, CW), F32)
    return pl.pallas_call(
        basis_kernel,
        in_specs=[VMEM] * 4,
        out_specs=[VMEM] * 3,
        out_shape=[jax.ShapeDtypeStruct((MODES, SNAPS), F32), side, side],
        compiler_params=params(16),
        name="basis",
    )(mine, other, heads, rests)


def column_of(ids, brick, whole):
    mine = whole[0]
    for k in range(1, EXT):
        mine = jnp.where(column_id(ids, brick) == k, whole[k], mine)
    return mine


def write_brick(brick, column, hot, spread, held, out_hbm, sem):
    picked = dot(column, hot).astype(BF16)
    blank = jnp.zeros((COEFS, PER_BRICK), BF16)
    stacked = jnp.concatenate([picked, picked[:COEFS], blank], axis=0)
    held[...] = dot(spread, stacked).astype(BF16).reshape(SNAPS, FIELDS, PER_BRICK)
    copy = pltpu.make_async_copy(held, out_hbm.at[:, :, pl.ds(brick * PER_BRICK, PER_BRICK)], sem)
    copy.start()
    return copy


def inner_kernel(
    basis_ref, down_ref, up_ref, below_early, below_late, above_early, above_late, ids, heads, rests, hots,
    out_hbm, whole_ref, ends_ref, spread_ref, held, out_sems
):
    both = by_field(basis_ref[...])
    spread_ref[...] = spread_matrix(basis_ref[...])
    whole = [jnp.zeros((2 * COEFS, CW), BF16)] * EXT
    parts = [by_field(basis_ref[...][:, h * PART : (h + 1) * PART]) for h in range(2)]
    for k, mine, wires in ((1, down_ref, (below_early, below_late)), (CX, up_ref, (above_early, above_late))):
        value = mine[...]
        for part, wire in zip(parts, wires):
            value += coefficients(part, *halves(wire_steps(wire, slice(0, PART_ROWS)))) * wire_scale(wire)
        whole[k] = jnp.concatenate(halves(value), axis=0)
    for k in (2, 3):
        whole[k] = jnp.concatenate(halves(coefficients(both, heads[k], rests[k])), axis=0)
    outputs = []
    for i, brick in enumerate(INNER):
        column = column_of(ids, brick, whole)
        outputs.append(write_brick(brick, column, hots[brick], spread_ref[...], held.at[i], out_hbm, out_sems.at[i]))
    for k in range(EXT):
        whole_ref[k] = whole[k]
    for i, k in enumerate((0, EXT - 1)):
        ends_ref[i] = coefficients(both, heads[k], rests[k])
    wait(outputs)


def inner_fields(basis, down, up, below, above, ids, heads, rests, hots):
    return pl.pallas_call(
        inner_kernel,
        in_specs=[VMEM] * 11,
        out_specs=[HBM] + [VMEM] * 3,
        scratch_shapes=[
            pltpu.VMEM((4, SNAPS, FIELDS, PER_BRICK), BF16),
            pltpu.SemaphoreType.DMA((4,)),
        ],
        out_shape=[
            jax.ShapeDtypeStruct((SNAPS, FIELDS, BRICKS * PER_BRICK), BF16),
            jax.ShapeDtypeStruct((EXT, 2 * COEFS, CW), BF16),
            jax.ShapeDtypeStruct((2, COEFS, CW), F32),
            jax.ShapeDtypeStruct((ROWS, 4 * COEFS), BF16),
        ],
        compiler_params=params(24),
        cost_estimate=pl.CostEstimate(flops=4_000_000_000, bytes_accessed=14_000_000, transcendentals=0),
        name="inner",
    )(basis, down, up, *below, *above, ids, heads, rests, hots)


def outer_kernel(filled_hbm, whole_ref, ends_ref, below, above, spread_ref, hots, ids, out_hbm, held, out_sems):
    del filled_hbm
    whole = [whole_ref[k] for k in range(EXT)]
    for k, received in ((0, below), (EXT - 1, above)):
        whole[k] = jnp.concatenate(halves(ends_ref[k // CX] + received[...]), axis=0)
    outputs = []
    for i, brick in enumerate(OUTER):
        column = column_of(ids, brick, whole)
        outputs.append(write_brick(brick, column, hots[brick], spread_ref[...], held.at[i], out_hbm, out_sems.at[i]))
    wait(outputs)


def outer_fields(filled, whole, ends, below, above, spread, hots, ids):
    return pl.pallas_call(
        outer_kernel,
        in_specs=[HBM] + [VMEM] * 7,
        out_specs=HBM,
        scratch_shapes=[
            pltpu.VMEM((4, SNAPS, FIELDS, PER_BRICK), BF16),
            pltpu.SemaphoreType.DMA((4,)),
        ],
        out_shape=jax.ShapeDtypeStruct(filled.shape, BF16),
        input_output_aliases={0: 0},
        compiler_params=params(32),
        name="outer",
    )(filled, whole, ends, below, above, spread, hots, ids)


def on_device(atom_values, atom_cell, brick_column):
    count = lax.axis_size("gx")
    to_lower = [((i + 1) % count, i) for i in range(count)]
    to_upper = [(i, (i + 1) % count) for i in range(count)]
    columns = jnp.pad(brick_column.reshape(1, BRICKS), ((0, 7), (0, 128 - BRICKS)))
    ids = jnp.concatenate([atom_cell.reshape(BRICKS * LANES, 128), columns], axis=0)
    below, above, totals, extra = [], [], [], []
    for part in range(2):
        low, high, total, *extra = face_sums(part, atom_values, ids)
        above.append(lax.ppermute(low, "gx", to_lower))
        below.append(lax.ppermute(high, "gx", to_upper))
        totals.append(total)
    heads, rests, hots, gram = local_sums(atom_values, ids, brick_column, *totals, *extra)
    mine, other = add_over_devices(*packed_gram(gram, heads, rests, below, above))
    basis, down, up = basis_and_faces(mine, other, heads, rests)
    end_above = lax.ppermute(down, "gx", to_lower)
    end_below = lax.ppermute(up, "gx", to_upper)
    filled, whole, ends, spread = inner_fields(basis, down, up, below, above, ids, heads, rests, hots)
    return outer_fields(filled, whole, ends, end_below, end_above, spread, hots, ids)


def solution(mesh):
    in_specs = (P(None, None, ("gx", "gz")), P(("gx", "gz")), P(("gx", "gz")))
    out_specs = P(None, None, ("gx", "gz"))
    return jax.shard_map(on_device, mesh=mesh, in_specs=in_specs, out_specs=out_specs, check_vma=False)
```

```python
import functools
import math

import jax
import jax.numpy as jnp
from jax import lax
from jax.experimental import pallas as pl
from jax.experimental.pallas import tpu as pltpu
from jax.sharding import PartitionSpec as P

SNAPS = 160
FIELDS = 4
ROWS = SNAPS * FIELDS
MODES = 8
SWEEPS = 3
CX = 4
EXT = CX + 2
CW = 512
PER_BRICK = 512
BRICKS = 8
COEFS = MODES * FIELDS
PART = SNAPS // 2
PART_ROWS = PART * FIELDS
WIRE = PART_ROWS + 16
TOP = 32767.0
STEPS = 8 / math.log(2)
SPLIT = 128
TAIL = SNAPS - SPLIT
LANES = CW // 128
F32 = jnp.float32
BF16 = jnp.bfloat16
NT = (((1,), (1,)), ((), ()))
TN = (((0,), (0,)), ((), ()))


def params(mib):
    return pltpu.CompilerParams(vmem_limit_bytes=mib * 1024 * 1024)


def dot_nt(a, b):
    return lax.dot_general(a, b, NT, preferred_element_type=F32)


def dot(a, b):
    return jnp.dot(a, b, preferred_element_type=F32)


def exact_dot(a, b):
    return jnp.dot(a, b, precision=lax.Precision.HIGHEST, preferred_element_type=F32)


def cell_hot(cells, brick, keep=None):
    ids = lax.broadcasted_iota(jnp.int32, (CW, 128), 0)
    tiles = []
    for t in range(LANES):
        row = cells[brick * LANES + t : brick * LANES + t + 1, :]
        if keep is not None:
            row = jnp.where(keep, row, -1)
        tiles.append((ids == row).astype(F32).astype(BF16))
    return jnp.concatenate(tiles, axis=1)


def halves(x):
    head = x.astype(BF16)
    return head, (x - head.astype(F32)).astype(BF16)


def one_field(total, field):
    rows = pl.ds(field, total.shape[1] // FIELDS, stride=FIELDS)
    return jnp.concatenate([total[t, rows, :] for t in range(LANES)], axis=1)


def brick_copy(values_hbm, held, sems, brick, slot):
    source = values_hbm.at[:, :, pl.ds(brick * PER_BRICK, PER_BRICK)]
    return pltpu.make_async_copy(source, held.at[slot], sems.at[slot])


def encode(total, out_ref):
    for t in range(LANES):
        lanes = slice(t * 128, (t + 1) * 128)
        most = jnp.max(jnp.abs(total[t]), axis=0, keepdims=True)
        code = jnp.ceil(jnp.log(jnp.maximum(most, 1e-30)) * STEPS)
        scale = jnp.exp(code * (-1 / STEPS)) * TOP
        for f in range(FIELDS):
            steps = jnp.round(total[t, pl.ds(f, PART, stride=FIELDS), :] * scale)
            out_ref[f * PART : (f + 1) * PART, lanes] = jnp.clip(steps, -TOP, TOP).astype(jnp.int32).astype(jnp.int16)
        out_ref[PART_ROWS:, lanes] = jnp.broadcast_to(code, (WIRE - PART_ROWS, 128)).astype(jnp.int32).astype(jnp.int16)


def wire_steps(wire, rows):
    return wire[rows, :].astype(jnp.int32).astype(F32)


def wire_scale(wire):
    return jnp.exp(wire_steps(wire, slice(PART_ROWS, WIRE))[:1] * (1 / STEPS)) * (1 / TOP)


def start(copies):
    for copy in copies:
        copy.start()


def wait(copies):
    for copy in copies:
        copy.wait()


def column_id(ids, brick):
    return ids[BRICKS * LANES : BRICKS * LANES + 1, brick : brick + 1]


INNER = range(2, BRICKS - 2)
OUTER = (0, 1, BRICKS - 2, BRICKS - 1)
HBM = pl.BlockSpec(memory_space=pltpu.HBM)
VMEM = pl.BlockSpec(memory_space=pltpu.VMEM)
SMEM = pl.BlockSpec(memory_space=pltpu.SMEM)


def faces_kernel(part, values_hbm, ids_ref, low_ref, high_ref, total, *rest):
    bricks = (0, 1, BRICKS - 2, BRICKS - 1)
    targets = ((0, low_ref), (EXT - 1, high_ref))
    held, sems = rest[-2:]
    copies = []
    for slot, brick in enumerate(bricks):
        source = values_hbm.at[pl.ds(part * PART, PART), :, pl.ds(brick * PER_BRICK, PER_BRICK)]
        copies.append(pltpu.make_async_copy(source, held.at[slot], sems.at[slot]))
    start(copies)
    later = []
    if part:
        passed, outer_hots, later_sems = rest[:3]
        later = [brick_copy(values_hbm, passed, later_sems, brick, i) for i, brick in enumerate(INNER)]
        start(later)
    hots = [
        cell_hot(ids_ref, brick, column_id(ids_ref, brick) == targets[slot // 2][0]) for slot, brick in enumerate(bricks)
    ]
    if part:
        outer_hots[0] = hots[0]
        outer_hots[1] = hots[3]
    for i in range(2):
        sums = None
        for slot in (2 * i, 2 * i + 1):
            copies[slot].wait()
            part_sums = dot_nt(held[slot].reshape(PART_ROWS, PER_BRICK), hots[slot])
            sums = part_sums if sums is None else sums + part_sums
        for t in range(LANES):
            total[i, t] = sums[:, t * 128 : (t + 1) * 128]
        encode(total.at[i], targets[i][1])
    wait(later)


def face_sums(part, values, ids):
    shape = jax.ShapeDtypeStruct((WIRE, CW), jnp.int16)
    later_shapes = [
        jax.ShapeDtypeStruct((len(INNER), SNAPS, FIELDS, PER_BRICK), BF16),
        jax.ShapeDtypeStruct((2, CW, PER_BRICK), BF16),
    ]
    later_scratch = [pltpu.SemaphoreType.DMA((len(INNER),))]
    return pl.pallas_call(
        functools.partial(faces_kernel, part),
        in_specs=[HBM, VMEM],
        out_specs=[VMEM] * (3 + 2 * part),
        scratch_shapes=later_scratch * part
        + [
            pltpu.VMEM((4, PART, FIELDS, PER_BRICK), BF16),
            pltpu.SemaphoreType.DMA((4,)),
        ],
        out_shape=[shape, shape, jax.ShapeDtypeStruct((2, LANES, PART_ROWS, 128), F32)] + later_shapes * part,
        compiler_params=params((51, 46)[part]),
        cost_estimate=pl.CostEstimate(flops=1_400_000_000, bytes_accessed=4_000_000, transcendentals=0),
        name="faces",
    )(values, ids)


def local_kernel(
    column_ref, values_hbm, ids_ref, early, late, inner, outer_hots, heads, rests, hots, gram_ref, held, total, sems
):
    edges = (1, BRICKS - 2)
    copies = [brick_copy(values_hbm, held, sems, brick, i) for i, brick in enumerate(edges)]
    start(copies)
    total[...] = jnp.zeros_like(total)
    hots[0] = outer_hots[0]
    hots[BRICKS - 1] = outer_hots[1]
    for brick in tuple(INNER) + edges:
        hot = cell_hot(ids_ref, brick)
        hots[brick] = hot
        if brick in INNER:
            values = inner[brick - 2]
        else:
            copies[edges.index(brick)].wait()
            values = held[edges.index(brick)]
        sums = dot_nt(values.reshape(ROWS, PER_BRICK), hot)
        column = column_ref[brick]
        place = jnp.where(column == EXT - 1, 0, column)
        for t in range(LANES):
            total[place, t] += sums[:, t * 128 : (t + 1) * 128]
    same = jnp.zeros((SNAPS, SNAPS), F32)
    mixed = jnp.zeros((SNAPS, SNAPS), F32)
    for k in range(EXT):
        for f in range(FIELDS):
            rows = slice(f * SNAPS, (f + 1) * SNAPS)
            if k in (0, EXT - 1):
                sums = jnp.concatenate([one_field(early.at[k // CX], f), one_field(late.at[k // CX], f)], axis=0)
            else:
                sums = one_field(total.at[k], f)
            head, rest = halves(sums)
            heads[k, rows, :] = head
            rests[k, rows, :] = rest
        for f in range(FIELDS):
            rows = slice(f * SNAPS, (f + 1) * SNAPS)
            same += dot_nt(heads[k, rows, :], heads[k, rows, :])
            mixed += dot_nt(heads[k, rows, :], rests[k, rows, :])
    gram_ref[...] = same + mixed + mixed.T


def local_sums(values, ids, columns, early, late, inner, outer_hots):
    half = jax.ShapeDtypeStruct((EXT, ROWS, CW), BF16)
    return pl.pallas_call(
        local_kernel,
        in_specs=[SMEM, HBM] + [VMEM] * 5,
        out_specs=[VMEM] * 4,
        scratch_shapes=[
            pltpu.VMEM((2, SNAPS, FIELDS, PER_BRICK), BF16),
            pltpu.VMEM((CX + 1, LANES, ROWS, 128), F32),
            pltpu.SemaphoreType.DMA((2,)),
        ],
        out_shape=[
            half,
            half,
            jax.ShapeDtypeStruct((BRICKS, CW, PER_BRICK), BF16),
            jax.ShapeDtypeStruct((SNAPS, SNAPS), F32),
        ],
        compiler_params=params(36),
        cost_estimate=pl.CostEstimate(flops=6_000_000_000, bytes_accessed=14_000_000, transcendentals=0),
        name="local",
    )(columns, values, ids, early, late, inner, outer_hots)


def pack(gram):
    body = gram[:SPLIT, :SPLIT]
    side = gram[:SPLIT, SPLIT:]
    corner = gram[SPLIT:, SPLIT:]
    t = TAIL
    rows = [
        body[:t],
        jnp.concatenate([side[:t], body[t : 2 * t, t:]], axis=1),
        jnp.concatenate([side[t : 2 * t], side[2 * t : 3 * t], body[2 * t : 3 * t, 2 * t :]], axis=1),
        jnp.concatenate([side[3 * t :], corner, corner, body[3 * t :, 3 * t :]], axis=1),
    ]
    return jnp.concatenate(rows, axis=0)


def unpack(packed):
    t = TAIL
    row = lax.broadcasted_iota(jnp.int32, (SPLIT, SPLIT), 0) // t
    col = lax.broadcasted_iota(jnp.int32, (SPLIT, SPLIT), 1) // t
    above = jnp.where(col > row, packed, 0.0)
    body = jnp.where(col == row, packed, 0.0) + above + above.T
    side = jnp.concatenate(
        [packed[t : 2 * t, :t], packed[2 * t : 3 * t, :t], packed[2 * t : 3 * t, t : 2 * t], packed[3 * t :, :t]], axis=0
    )
    corner = packed[3 * t :, t : 2 * t]
    top = jnp.concatenate([body, side], axis=1)
    padded = jnp.concatenate([side, jnp.zeros((SPLIT, SPLIT - t), F32)], axis=1)
    bottom = jnp.concatenate([padded.T[:t], corner], axis=1)
    return jnp.concatenate([top, bottom], axis=0)


def cross_terms(gram, heads, rests, early, late):
    cross = jnp.zeros((SNAPS, SNAPS), F32)
    scales = [wire_scale(wire) for wire in (early, late)]
    for f in range(FIELDS):
        part = slice(f * PART, (f + 1) * PART)
        steps = [wire_steps(wire, part) * scale for wire, scale in zip((early, late), scales)]
        head, rest = halves(jnp.concatenate(steps, axis=0))
        rows = slice(f * SNAPS, (f + 1) * SNAPS)
        own = heads[rows, :]
        pair = dot_nt(jnp.concatenate([own, rests[rows, :]], axis=0), head)
        cross += pair[:SNAPS] + pair[SNAPS:] + dot_nt(own, rest)
    return gram + cross + cross.T


def below_kernel(gram_ref, heads, rests, early, late, out_ref):
    out_ref[...] = cross_terms(gram_ref[...], heads.at[1], rests.at[1], early, late)


def above_kernel(gram_ref, heads, rests, early, late, mine_ref, other_ref):
    packed = pack(cross_terms(gram_ref[...], heads.at[CX], rests.at[CX], early, late))
    first = on_first_core()
    mine_ref[...] = jnp.where(first, packed[: SPLIT // 2], packed[SPLIT // 2 :])
    other_ref[...] = jnp.where(first, packed[SPLIT // 2 :], packed[: SPLIT // 2])


def packed_gram(gram, heads, rests, below, above):
    common = dict(compiler_params=params(16), cost_estimate=pl.CostEstimate(flops=400_000_000, bytes_accessed=3_000_000, transcendentals=0))
    gram = pl.pallas_call(
        below_kernel,
        in_specs=[VMEM] * 5,
        out_specs=VMEM,
        out_shape=jax.ShapeDtypeStruct((SNAPS, SNAPS), F32),
        name="below",
        **common,
    )(gram, heads, rests, *below)
    return pl.pallas_call(
        above_kernel,
        in_specs=[VMEM] * 5,
        out_specs=[VMEM] * 2,
        out_shape=[jax.ShapeDtypeStruct((SPLIT // 2, SPLIT), F32)] * 2,
        name="above",
        **common,
    )(gram, heads, rests, *above)


def on_first_core():
    return lax.rem(lax.axis_index("gz"), 2) == 0


def tree_sum(terms):
    while len(terms) > 1:
        terms = [a + b for a, b in zip(terms[::2], terms[1::2])]
    return terms[0]


def terms_kernel(*refs):
    out_ref = refs[-1]
    out_ref[...] = jnp.broadcast_to(tree_sum([ref[...] for ref in refs[:-1]]), out_ref.shape)


def parts_kernel(parts, out_ref):
    out_ref[...] = tree_sum([parts[i] for i in range(parts.shape[0])])


def small_sum(kernel, terms, shape):
    return pl.pallas_call(
        kernel,
        in_specs=[VMEM] * len(terms),
        out_specs=VMEM,
        out_shape=jax.ShapeDtypeStruct(shape, F32),
        compiler_params=params(4),
        name="sum",
    )(*terms)


def add_over_devices(mine, other):
    axes = ("gx", "gz")
    depth = 8
    places = [(a, z, y, c) for a in range(4) for z in range(depth) for y in range(4) for c in range(2)]
    number = {place: i for i, place in enumerate(places)}
    lines = [[number[a, z, y, c] for z in range(depth)] for a in range(4) for y in range(4) for c in range(2)]

    def move(x, target):
        return lax.ppermute(x, axes, [(number[place], number[target(*place)]) for place in places])

    def swap(x):
        return move(x, lambda a, z, y, c: (a, z, y, 1 - c))

    shape = mine.shape
    mine = small_sum(terms_kernel, [mine, swap(other)], shape)
    one, three, two = [move(mine, lambda a, z, y, c, k=k: (a ^ k, z, y, c)) for k in (1, 3, 2)]
    mine = small_sum(terms_kernel, [mine, one, three, two], shape)
    one, three, two = [move(mine, lambda a, z, y, c, k=k: (a, z, y ^ k, c)) for k in (1, 3, 2)]
    copies = small_sum(terms_kernel, [mine, one, three, two], (depth,) + shape)
    parts = lax.all_to_all(copies, axes, 0, 0, axis_index_groups=lines, tiled=True)
    mine = small_sum(parts_kernel, [parts], shape)
    return mine, swap(mine)


def orthonormal(basis):
    inner = lax.dot_general(basis, basis, NT, precision=lax.Precision.HIGHEST, preferred_element_type=F32)
    row = lax.broadcasted_iota(jnp.int32, (MODES, 1), 0)
    columns = [jnp.broadcast_to(inner[:, j : j + 1], (MODES, 128)) for j in range(MODES)]
    wide = jnp.concatenate([basis, jnp.zeros((MODES, 256 - SNAPS), F32)], axis=1)
    parts = [wide[:, :128], wide[:, 128:]]
    scale = jnp.zeros((MODES, 128), F32)
    for j in range(MODES):
        pivot = columns[j][j : j + 1, :]
        scale = jnp.where(row == j, lax.rsqrt(pivot), scale)
        factor = jnp.where(row > j, columns[j] * (1.0 / pivot), 0.0)
        for k in range(j + 1, MODES):
            columns[k] = columns[k] - factor * columns[k][j : j + 1, :]
        parts = [part - factor * part[j : j + 1, :] for part in parts]
    return jnp.concatenate([part * scale for part in parts], axis=1)[:, :SNAPS]


def spread_matrix(basis):
    snap = lax.broadcasted_iota(jnp.int32, (SNAPS, ROWS), 0)
    column = lax.broadcasted_iota(jnp.int32, (SNAPS, ROWS), 1)
    repeat = (snap == column // FIELDS).astype(F32).astype(BF16)
    both = dot(jnp.concatenate(halves(basis), axis=0), repeat)
    field = lax.broadcasted_iota(jnp.int32, (COEFS, ROWS), 0) // MODES
    mine = field == lax.broadcasted_iota(jnp.int32, (COEFS, ROWS), 1) % FIELDS
    head = jnp.where(mine, jnp.concatenate([both[:MODES]] * FIELDS, axis=0), 0.0)
    rest = jnp.where(mine, jnp.concatenate([both[MODES:]] * FIELDS, axis=0), 0.0)
    return jnp.concatenate([head, head, rest, jnp.zeros_like(rest)], axis=0).T.astype(BF16)


def by_field(basis):
    snaps = basis.shape[1]
    tall = jnp.concatenate([jnp.concatenate([basis] * FIELDS, axis=1)] * FIELDS, axis=0)
    row_field = lax.broadcasted_iota(jnp.int32, tall.shape, 0) // MODES
    col_field = lax.broadcasted_iota(jnp.int32, tall.shape, 1) // snaps
    return jnp.concatenate(halves(jnp.where(row_field == col_field, tall, 0.0)), axis=0)


def coefficients(both, head, rest):
    pair = dot(both, head)
    return pair[:COEFS] + pair[COEFS:] + dot(both[:COEFS], rest)


def basis_kernel(mine_ref, other_ref, heads, rests, basis_ref, down_ref, up_ref):
    first = on_first_core()
    mine, other = mine_ref[...], other_ref[...]
    gram = unpack(jnp.concatenate([jnp.where(first, mine, other), jnp.where(first, other, mine)], axis=0))
    basis = gram[:MODES, :]
    for _ in range(SWEEPS):
        basis = orthonormal(exact_dot(basis, gram))
    basis_ref[...] = basis
    both = by_field(basis)
    down_ref[...] = coefficients(both, heads[1], rests[1])
    up_ref[...] = coefficients(both, heads[CX], rests[CX])


def basis_and_faces(mine, other, heads, rests):
    side = jax.ShapeDtypeStruct((COEFS, CW), F32)
    return pl.pallas_call(
        basis_kernel,
        in_specs=[VMEM] * 4,
        out_specs=[VMEM] * 3,
        out_shape=[jax.ShapeDtypeStruct((MODES, SNAPS), F32), side, side],
        compiler_params=params(16),
        name="basis",
    )(mine, other, heads, rests)


def column_of(ids, brick, whole):
    mine = whole[0]
    for k in range(1, EXT):
        mine = jnp.where(column_id(ids, brick) == k, whole[k], mine)
    return mine


def write_brick(brick, column, hot, spread, held, out_hbm, sem):
    picked = dot(column, hot).astype(BF16)
    blank = jnp.zeros((COEFS, PER_BRICK), BF16)
    stacked = jnp.concatenate([picked, picked[:COEFS], blank], axis=0)
    held[...] = dot(spread, stacked).astype(BF16).reshape(SNAPS, FIELDS, PER_BRICK)
    copy = pltpu.make_async_copy(held, out_hbm.at[:, :, pl.ds(brick * PER_BRICK, PER_BRICK)], sem)
    copy.start()
    return copy


def inner_kernel(
    basis_ref, down_ref, up_ref, below_early, below_late, above_early, above_late, ids, heads, rests, hots,
    out_hbm, whole_ref, ends_ref, spread_ref, held, out_sems
):
    both = by_field(basis_ref[...])
    spread_ref[...] = spread_matrix(basis_ref[...])
    whole = [jnp.zeros((2 * COEFS, CW), BF16)] * EXT
    parts = [by_field(basis_ref[...][:, h * PART : (h + 1) * PART]) for h in range(2)]
    for k, mine, wires in ((1, down_ref, (below_early, below_late)), (CX, up_ref, (above_early, above_late))):
        value = mine[...]
        for part, wire in zip(parts, wires):
            value += coefficients(part, *halves(wire_steps(wire, slice(0, PART_ROWS)))) * wire_scale(wire)
        whole[k] = jnp.concatenate(halves(value), axis=0)
    for k in (2, 3):
        whole[k] = jnp.concatenate(halves(coefficients(both, heads[k], rests[k])), axis=0)
    outputs = []
    for i, brick in enumerate(INNER):
        column = column_of(ids, brick, whole)
        outputs.append(write_brick(brick, column, hots[brick], spread_ref[...], held.at[i], out_hbm, out_sems.at[i]))
    for k in range(EXT):
        whole_ref[k] = whole[k]
    for i, k in enumerate((0, EXT - 1)):
        ends_ref[i] = coefficients(both, heads[k], rests[k])
    wait(outputs)


def inner_fields(basis, down, up, below, above, ids, heads, rests, hots):
    return pl.pallas_call(
        inner_kernel,
        in_specs=[VMEM] * 11,
        out_specs=[HBM] + [VMEM] * 3,
        scratch_shapes=[
            pltpu.VMEM((4, SNAPS, FIELDS, PER_BRICK), BF16),
            pltpu.SemaphoreType.DMA((4,)),
        ],
        out_shape=[
            jax.ShapeDtypeStruct((SNAPS, FIELDS, BRICKS * PER_BRICK), BF16),
            jax.ShapeDtypeStruct((EXT, 2 * COEFS, CW), BF16),
            jax.ShapeDtypeStruct((2, COEFS, CW), F32),
            jax.ShapeDtypeStruct((ROWS, 4 * COEFS), BF16),
        ],
        compiler_params=params(24),
        cost_estimate=pl.CostEstimate(flops=4_000_000_000, bytes_accessed=14_000_000, transcendentals=0),
        name="inner",
    )(basis, down, up, *below, *above, ids, heads, rests, hots)


def outer_kernel(filled_hbm, whole_ref, ends_ref, below, above, spread_ref, hots, ids, out_hbm, held, out_sems):
    del filled_hbm
    whole = [whole_ref[k] for k in range(EXT)]
    for k, received in ((0, below), (EXT - 1, above)):
        whole[k] = jnp.concatenate(halves(ends_ref[k // CX] + received[...]), axis=0)
    outputs = []
    for i, brick in enumerate(OUTER):
        column = column_of(ids, brick, whole)
        outputs.append(write_brick(brick, column, hots[brick], spread_ref[...], held.at[i], out_hbm, out_sems.at[i]))
    wait(outputs)


def outer_fields(filled, whole, ends, below, above, spread, hots, ids):
    return pl.pallas_call(
        outer_kernel,
        in_specs=[HBM] + [VMEM] * 7,
        out_specs=HBM,
        scratch_shapes=[
            pltpu.VMEM((4, SNAPS, FIELDS, PER_BRICK), BF16),
            pltpu.SemaphoreType.DMA((4,)),
        ],
        out_shape=jax.ShapeDtypeStruct(filled.shape, BF16),
        input_output_aliases={0: 0},
        compiler_params=params(32),
        name="outer",
    )(filled, whole, ends, below, above, spread, hots, ids)


def on_device(atom_values, atom_cell, brick_column):
    count = lax.axis_size("gx")
    to_lower = [((i + 1) % count, i) for i in range(count)]
    to_upper = [(i, (i + 1) % count) for i in range(count)]
    columns = jnp.pad(brick_column.reshape(1, BRICKS), ((0, 7), (0, 128 - BRICKS)))
    ids = jnp.concatenate([atom_cell.reshape(BRICKS * LANES, 128), columns], axis=0)
    below, above, totals, extra = [], [], [], []
    for part in range(2):
        low, high, total, *extra = face_sums(part, atom_values, ids)
        above.append(lax.ppermute(low, "gx", to_lower))
        below.append(lax.ppermute(high, "gx", to_upper))
        totals.append(total)
    heads, rests, hots, gram = local_sums(atom_values, ids, brick_column, *totals, *extra)
    mine, other = add_over_devices(*packed_gram(gram, heads, rests, below, above))
    basis, down, up = basis_and_faces(mine, other, heads, rests)
    end_above = lax.ppermute(down, "gx", to_lower)
    end_below = lax.ppermute(up, "gx", to_upper)
    filled, whole, ends, spread = inner_fields(basis, down, up, below, above, ids, heads, rests, hots)
    return outer_fields(filled, whole, ends, end_below, end_above, spread, hots, ids)


def solution(mesh):
    in_specs = (P(None, None, ("gx", "gz")), P(("gx", "gz")), P(("gx", "gz")))
    out_specs = P(None, None, ("gx", "gz"))
    return jax.shard_map(on_device, mesh=mesh, in_specs=in_specs, out_specs=out_specs, check_vma=False)
```

```python
import functools
import math

import jax
import jax.numpy as jnp
from jax import lax
from jax.experimental import pallas as pl
from jax.experimental.pallas import tpu as pltpu
from jax.sharding import PartitionSpec as P

SNAPS = 160
FIELDS = 4
ROWS = SNAPS * FIELDS
MODES = 8
SWEEPS = 3
CX = 4
EXT = CX + 2
CW = 512
PER_BRICK = 512
BRICKS = 8
COEFS = MODES * FIELDS
PART = SNAPS // 2
PART_ROWS = PART * FIELDS
WIRE = PART_ROWS + 16
TOP = 32767.0
STEPS = 8 / math.log(2)
SPLIT = 128
TAIL = SNAPS - SPLIT
LANES = CW // 128
F32 = jnp.float32
BF16 = jnp.bfloat16
NT = (((1,), (1,)), ((), ()))
TN = (((0,), (0,)), ((), ()))


def params(mib):
    return pltpu.CompilerParams(vmem_limit_bytes=mib * 1024 * 1024)


def dot_nt(a, b):
    return lax.dot_general(a, b, NT, preferred_element_type=F32)


def dot(a, b):
    return jnp.dot(a, b, preferred_element_type=F32)


def exact_dot(a, b):
    return jnp.dot(a, b, precision=lax.Precision.HIGHEST, preferred_element_type=F32)


def cell_hot(cells, brick, keep=None):
    ids = lax.broadcasted_iota(jnp.int32, (CW, 128), 0)
    tiles = []
    for t in range(LANES):
        row = cells[brick * LANES + t : brick * LANES + t + 1, :]
        if keep is not None:
            row = jnp.where(keep, row, -1)
        tiles.append((ids == row).astype(F32).astype(BF16))
    return jnp.concatenate(tiles, axis=1)


def halves(x):
    head = x.astype(BF16)
    return head, (x - head.astype(F32)).astype(BF16)


def one_field(total, field):
    rows = pl.ds(field, total.shape[1] // FIELDS, stride=FIELDS)
    return jnp.concatenate([total[t, rows, :] for t in range(LANES)], axis=1)


def brick_copy(values_hbm, held, sems, brick, slot):
    source = values_hbm.at[:, :, pl.ds(brick * PER_BRICK, PER_BRICK)]
    return pltpu.make_async_copy(source, held.at[slot], sems.at[slot])


def encode(total, out_ref):
    for t in range(LANES):
        lanes = slice(t * 128, (t + 1) * 128)
        most = jnp.max(jnp.abs(total[t]), axis=0, keepdims=True)
        code = jnp.ceil(jnp.log(jnp.maximum(most, 1e-30)) * STEPS)
        scale = jnp.exp(code * (-1 / STEPS)) * TOP
        for f in range(FIELDS):
            steps = jnp.round(total[t, pl.ds(f, PART, stride=FIELDS), :] * scale)
            out_ref[f * PART : (f + 1) * PART, lanes] = jnp.clip(steps, -TOP, TOP).astype(jnp.int32).astype(jnp.int16)
        out_ref[PART_ROWS:, lanes] = jnp.broadcast_to(code, (WIRE - PART_ROWS, 128)).astype(jnp.int32).astype(jnp.int16)


def wire_steps(wire, rows):
    return wire[rows, :].astype(jnp.int32).astype(F32)


def wire_scale(wire):
    return jnp.exp(wire_steps(wire, slice(PART_ROWS, WIRE))[:1] * (1 / STEPS)) * (1 / TOP)


def start(copies):
    for copy in copies:
        copy.start()


def wait(copies):
    for copy in copies:
        copy.wait()


def column_id(ids, brick):
    return ids[BRICKS * LANES : BRICKS * LANES + 1, brick : brick + 1]


INNER = range(2, BRICKS - 2)
OUTER = (0, 1, BRICKS - 2, BRICKS - 1)
HBM = pl.BlockSpec(memory_space=pltpu.HBM)
VMEM = pl.BlockSpec(memory_space=pltpu.VMEM)
SMEM = pl.BlockSpec(memory_space=pltpu.SMEM)


def faces_kernel(part, values_hbm, ids_ref, low_ref, high_ref, total, *rest):
    bricks = (0, 1, BRICKS - 2, BRICKS - 1)
    targets = ((0, low_ref), (EXT - 1, high_ref))
    held, sems = rest[-2:]
    copies = []
    for slot, brick in enumerate(bricks):
        source = values_hbm.at[pl.ds(part * PART, PART), :, pl.ds(brick * PER_BRICK, PER_BRICK)]
        copies.append(pltpu.make_async_copy(source, held.at[slot], sems.at[slot]))
    start(copies)
    later = []
    if part:
        passed, outer_hots, later_sems = rest[:3]
        later = [brick_copy(values_hbm, passed, later_sems, brick, i) for i, brick in enumerate(INNER)]
        start(later)
    hots = [
        cell_hot(ids_ref, brick, column_id(ids_ref, brick) == targets[slot // 2][0]) for slot, brick in enumerate(bricks)
    ]
    if part:
        outer_hots[0] = hots[0]
        outer_hots[1] = hots[3]
    for i in range(2):
        sums = None
        for slot in (2 * i, 2 * i + 1):
            copies[slot].wait()
            part_sums = dot_nt(held[slot].reshape(PART_ROWS, PER_BRICK), hots[slot])
            sums = part_sums if sums is None else sums + part_sums
        for t in range(LANES):
            total[i, t] = sums[:, t * 128 : (t + 1) * 128]
        encode(total.at[i], targets[i][1])
    wait(later)


def face_sums(part, values, ids):
    shape = jax.ShapeDtypeStruct((WIRE, CW), jnp.int16)
    later_shapes = [
        jax.ShapeDtypeStruct((len(INNER), SNAPS, FIELDS, PER_BRICK), BF16),
        jax.ShapeDtypeStruct((2, CW, PER_BRICK), BF16),
    ]
    later_scratch = [pltpu.SemaphoreType.DMA((len(INNER),))]
    return pl.pallas_call(
        functools.partial(faces_kernel, part),
        in_specs=[HBM, VMEM],
        out_specs=[VMEM] * (3 + 2 * part),
        scratch_shapes=later_scratch * part
        + [
            pltpu.VMEM((4, PART, FIELDS, PER_BRICK), BF16),
            pltpu.SemaphoreType.DMA((4,)),
        ],
        out_shape=[shape, shape, jax.ShapeDtypeStruct((2, LANES, PART_ROWS, 128), F32)] + later_shapes * part,
        compiler_params=params((51, 46)[part]),
        cost_estimate=pl.CostEstimate(flops=1_400_000_000, bytes_accessed=4_000_000, transcendentals=0),
        name="faces",
    )(values, ids)


def local_kernel(
    column_ref, values_hbm, ids_ref, early, late, inner, outer_hots, heads, rests, hots, gram_ref, held, total, sems
):
    edges = (1, BRICKS - 2)
    copies = [brick_copy(values_hbm, held, sems, brick, i) for i, brick in enumerate(edges)]
    start(copies)
    total[...] = jnp.zeros_like(total)
    hots[0] = outer_hots[0]
    hots[BRICKS - 1] = outer_hots[1]
    for brick in tuple(INNER) + edges:
        hot = cell_hot(ids_ref, brick)
        hots[brick] = hot
        if brick in INNER:
            values = inner[brick - 2]
        else:
            copies[edges.index(brick)].wait()
            values = held[edges.index(brick)]
        sums = dot_nt(values.reshape(ROWS, PER_BRICK), hot)
        column = column_ref[brick]
        place = jnp.where(column == EXT - 1, 0, column)
        for t in range(LANES):
            total[place, t] += sums[:, t * 128 : (t + 1) * 128]
    same = jnp.zeros((SNAPS, SNAPS), F32)
    mixed = jnp.zeros((SNAPS, SNAPS), F32)
    for k in range(EXT):
        for f in range(FIELDS):
            rows = slice(f * SNAPS, (f + 1) * SNAPS)
            if k in (0, EXT - 1):
                sums = jnp.concatenate([one_field(early.at[k // CX], f), one_field(late.at[k // CX], f)], axis=0)
            else:
                sums = one_field(total.at[k], f)
            head, rest = halves(sums)
            heads[k, rows, :] = head
            rests[k, rows, :] = rest
        for f in range(FIELDS):
            rows = slice(f * SNAPS, (f + 1) * SNAPS)
            same += dot_nt(heads[k, rows, :], heads[k, rows, :])
            mixed += dot_nt(heads[k, rows, :], rests[k, rows, :])
    gram_ref[...] = same + mixed + mixed.T


def local_sums(values, ids, columns, early, late, inner, outer_hots):
    half = jax.ShapeDtypeStruct((EXT, ROWS, CW), BF16)
    return pl.pallas_call(
        local_kernel,
        in_specs=[SMEM, HBM] + [VMEM] * 5,
        out_specs=[VMEM] * 4,
        scratch_shapes=[
            pltpu.VMEM((2, SNAPS, FIELDS, PER_BRICK), BF16),
            pltpu.VMEM((CX + 1, LANES, ROWS, 128), F32),
            pltpu.SemaphoreType.DMA((2,)),
        ],
        out_shape=[
            half,
            half,
            jax.ShapeDtypeStruct((BRICKS, CW, PER_BRICK), BF16),
            jax.ShapeDtypeStruct((SNAPS, SNAPS), F32),
        ],
        compiler_params=params(36),
        cost_estimate=pl.CostEstimate(flops=6_000_000_000, bytes_accessed=14_000_000, transcendentals=0),
        name="local",
    )(columns, values, ids, early, late, inner, outer_hots)


def pack(gram):
    body = gram[:SPLIT, :SPLIT]
    side = gram[:SPLIT, SPLIT:]
    corner = gram[SPLIT:, SPLIT:]
    t = TAIL
    rows = [
        body[:t],
        jnp.concatenate([side[:t], body[t : 2 * t, t:]], axis=1),
        jnp.concatenate([side[t : 2 * t], side[2 * t : 3 * t], body[2 * t : 3 * t, 2 * t :]], axis=1),
        jnp.concatenate([side[3 * t :], corner, corner, body[3 * t :, 3 * t :]], axis=1),
    ]
    return jnp.concatenate(rows, axis=0)


def unpack(packed):
    t = TAIL
    row = lax.broadcasted_iota(jnp.int32, (SPLIT, SPLIT), 0) // t
    col = lax.broadcasted_iota(jnp.int32, (SPLIT, SPLIT), 1) // t
    above = jnp.where(col > row, packed, 0.0)
    body = jnp.where(col == row, packed, 0.0) + above + above.T
    side = jnp.concatenate(
        [packed[t : 2 * t, :t], packed[2 * t : 3 * t, :t], packed[2 * t : 3 * t, t : 2 * t], packed[3 * t :, :t]], axis=0
    )
    corner = packed[3 * t :, t : 2 * t]
    top = jnp.concatenate([body, side], axis=1)
    padded = jnp.concatenate([side, jnp.zeros((SPLIT, SPLIT - t), F32)], axis=1)
    bottom = jnp.concatenate([padded.T[:t], corner], axis=1)
    return jnp.concatenate([top, bottom], axis=0)


def cross_terms(heads, rests, below, above):
    cross = jnp.zeros((SNAPS, PART), F32)
    for k, wire in ((1, below), (CX, above)):
        scale = wire_scale(wire)
        for f in range(FIELDS):
            head, rest = halves(wire_steps(wire, slice(f * PART, (f + 1) * PART)) * scale)
            rows = slice(f * SNAPS, (f + 1) * SNAPS)
            own = heads[k, rows, :]
            pair = dot_nt(jnp.concatenate([own, rests[k, rows, :]], axis=0), head)
            cross += pair[:SNAPS] + pair[SNAPS:] + dot_nt(own, rest)
    return cross


def early_kernel(heads, rests, below, above, cross_ref):
    cross_ref[...] = cross_terms(heads, rests, below, above)


def late_kernel(gram_ref, early_ref, heads, rests, below, above, mine_ref, other_ref):
    cross = jnp.concatenate([early_ref[...], cross_terms(heads, rests, below, above)], axis=1)
    packed = pack(gram_ref[...] + cross + cross.T)
    first = on_first_core()
    mine_ref[...] = jnp.where(first, packed[: SPLIT // 2], packed[SPLIT // 2 :])
    other_ref[...] = jnp.where(first, packed[SPLIT // 2 :], packed[: SPLIT // 2])


def packed_gram(gram, heads, rests, below, above):
    common = dict(compiler_params=params(16), cost_estimate=pl.CostEstimate(flops=400_000_000, bytes_accessed=3_000_000, transcendentals=0))
    early = pl.pallas_call(
        early_kernel,
        in_specs=[VMEM] * 4,
        out_specs=VMEM,
        out_shape=jax.ShapeDtypeStruct((SNAPS, PART), F32),
        name="early",
        **common,
    )(heads, rests, below[0], above[0])
    return pl.pallas_call(
        late_kernel,
        in_specs=[VMEM] * 6,
        out_specs=[VMEM] * 2,
        out_shape=[jax.ShapeDtypeStruct((SPLIT // 2, SPLIT), F32)] * 2,
        name="late",
        **common,
    )(gram, early, heads, rests, below[1], above[1])


def on_first_core():
    return lax.rem(lax.axis_index("gz"), 2) == 0


def tree_sum(terms):
    while len(terms) > 1:
        terms = [a + b for a, b in zip(terms[::2], terms[1::2])]
    return terms[0]


def terms_kernel(*refs):
    out_ref = refs[-1]
    out_ref[...] = jnp.broadcast_to(tree_sum([ref[...] for ref in refs[:-1]]), out_ref.shape)


def parts_kernel(parts, out_ref):
    out_ref[...] = tree_sum([parts[i] for i in range(parts.shape[0])])


def small_sum(kernel, terms, shape):
    return pl.pallas_call(
        kernel,
        in_specs=[VMEM] * len(terms),
        out_specs=VMEM,
        out_shape=jax.ShapeDtypeStruct(shape, F32),
        compiler_params=params(4),
        name="sum",
    )(*terms)


def add_over_devices(mine, other):
    axes = ("gx", "gz")
    depth = 8
    places = [(a, z, y, c) for a in range(4) for z in range(depth) for y in range(4) for c in range(2)]
    number = {place: i for i, place in enumerate(places)}
    lines = [[number[a, z, y, c] for z in range(depth)] for a in range(4) for y in range(4) for c in range(2)]

    def move(x, target):
        return lax.ppermute(x, axes, [(number[place], number[target(*place)]) for place in places])

    def swap(x):
        return move(x, lambda a, z, y, c: (a, z, y, 1 - c))

    shape = mine.shape
    mine = small_sum(terms_kernel, [mine, swap(other)], shape)
    one, three, two = [move(mine, lambda a, z, y, c, k=k: (a ^ k, z, y, c)) for k in (1, 3, 2)]
    mine = small_sum(terms_kernel, [mine, one, three, two], shape)
    one, three, two = [move(mine, lambda a, z, y, c, k=k: (a, z, y ^ k, c)) for k in (1, 3, 2)]
    copies = small_sum(terms_kernel, [mine, one, three, two], (depth,) + shape)
    parts = lax.all_to_all(copies, axes, 0, 0, axis_index_groups=lines, tiled=True)
    mine = small_sum(parts_kernel, [parts], shape)
    return mine, swap(mine)


def orthonormal(basis):
    inner = lax.dot_general(basis, basis, NT, precision=lax.Precision.HIGHEST, preferred_element_type=F32)
    row = lax.broadcasted_iota(jnp.int32, (MODES, 1), 0)
    columns = [jnp.broadcast_to(inner[:, j : j + 1], (MODES, 128)) for j in range(MODES)]
    wide = jnp.concatenate([basis, jnp.zeros((MODES, 256 - SNAPS), F32)], axis=1)
    parts = [wide[:, :128], wide[:, 128:]]
    scale = jnp.zeros((MODES, 128), F32)
    for j in range(MODES):
        pivot = columns[j][j : j + 1, :]
        scale = jnp.where(row == j, lax.rsqrt(pivot), scale)
        factor = jnp.where(row > j, columns[j] * (1.0 / pivot), 0.0)
        for k in range(j + 1, MODES):
            columns[k] = columns[k] - factor * columns[k][j : j + 1, :]
        parts = [part - factor * part[j : j + 1, :] for part in parts]
    return jnp.concatenate([part * scale for part in parts], axis=1)[:, :SNAPS]


def spread_matrix(basis):
    snap = lax.broadcasted_iota(jnp.int32, (SNAPS, ROWS), 0)
    column = lax.broadcasted_iota(jnp.int32, (SNAPS, ROWS), 1)
    repeat = (snap == column // FIELDS).astype(F32).astype(BF16)
    both = dot(jnp.concatenate(halves(basis), axis=0), repeat)
    field = lax.broadcasted_iota(jnp.int32, (COEFS, ROWS), 0) // MODES
    mine = field == lax.broadcasted_iota(jnp.int32, (COEFS, ROWS), 1) % FIELDS
    head = jnp.where(mine, jnp.concatenate([both[:MODES]] * FIELDS, axis=0), 0.0)
    rest = jnp.where(mine, jnp.concatenate([both[MODES:]] * FIELDS, axis=0), 0.0)
    return jnp.concatenate([head, head, rest, jnp.zeros_like(rest)], axis=0).T.astype(BF16)


def by_field(basis):
    snaps = basis.shape[1]
    tall = jnp.concatenate([jnp.concatenate([basis] * FIELDS, axis=1)] * FIELDS, axis=0)
    row_field = lax.broadcasted_iota(jnp.int32, tall.shape, 0) // MODES
    col_field = lax.broadcasted_iota(jnp.int32, tall.shape, 1) // snaps
    return jnp.concatenate(halves(jnp.where(row_field == col_field, tall, 0.0)), axis=0)


def coefficients(both, head, rest):
    pair = dot(both, head)
    return pair[:COEFS] + pair[COEFS:] + dot(both[:COEFS], rest)


def basis_kernel(mine_ref, other_ref, heads, rests, basis_ref, down_ref, up_ref):
    first = on_first_core()
    mine, other = mine_ref[...], other_ref[...]
    gram = unpack(jnp.concatenate([jnp.where(first, mine, other), jnp.where(first, other, mine)], axis=0))
    basis = gram[:MODES, :]
    for _ in range(SWEEPS):
        basis = orthonormal(exact_dot(basis, gram))
    basis_ref[...] = basis
    both = by_field(basis)
    down_ref[...] = coefficients(both, heads[1], rests[1])
    up_ref[...] = coefficients(both, heads[CX], rests[CX])


def basis_and_faces(mine, other, heads, rests):
    side = jax.ShapeDtypeStruct((COEFS, CW), F32)
    return pl.pallas_call(
        basis_kernel,
        in_specs=[VMEM] * 4,
        out_specs=[VMEM] * 3,
        out_shape=[jax.ShapeDtypeStruct((MODES, SNAPS), F32), side, side],
        compiler_params=params(16),
        name="basis",
    )(mine, other, heads, rests)


def column_of(ids, brick, whole):
    mine = whole[0]
    for k in range(1, EXT):
        mine = jnp.where(column_id(ids, brick) == k, whole[k], mine)
    return mine


def write_brick(brick, column, hot, spread, held, out_hbm, sem):
    picked = dot(column, hot).astype(BF16)
    blank = jnp.zeros((COEFS, PER_BRICK), BF16)
    stacked = jnp.concatenate([picked, picked[:COEFS], blank], axis=0)
    held[...] = dot(spread, stacked).astype(BF16).reshape(SNAPS, FIELDS, PER_BRICK)
    copy = pltpu.make_async_copy(held, out_hbm.at[:, :, pl.ds(brick * PER_BRICK, PER_BRICK)], sem)
    copy.start()
    return copy


def inner_kernel(
    basis_ref, down_ref, up_ref, below_early, below_late, above_early, above_late, ids, heads, rests, hots,
    out_hbm, whole_ref, ends_ref, spread_ref, held, out_sems
):
    both = by_field(basis_ref[...])
    spread_ref[...] = spread_matrix(basis_ref[...])
    whole = [jnp.zeros((2 * COEFS, CW), BF16)] * EXT
    parts = [by_field(basis_ref[...][:, h * PART : (h + 1) * PART]) for h in range(2)]
    for k, mine, wires in ((1, down_ref, (below_early, below_late)), (CX, up_ref, (above_early, above_late))):
        value = mine[...]
        for part, wire in zip(parts, wires):
            value += coefficients(part, *halves(wire_steps(wire, slice(0, PART_ROWS)))) * wire_scale(wire)
        whole[k] = jnp.concatenate(halves(value), axis=0)
    for k in (2, 3):
        whole[k] = jnp.concatenate(halves(coefficients(both, heads[k], rests[k])), axis=0)
    outputs = []
    for i, brick in enumerate(INNER):
        column = column_of(ids, brick, whole)
        outputs.append(write_brick(brick, column, hots[brick], spread_ref[...], held.at[i], out_hbm, out_sems.at[i]))
    for k in range(EXT):
        whole_ref[k] = whole[k]
    for i, k in enumerate((0, EXT - 1)):
        ends_ref[i] = coefficients(both, heads[k], rests[k])
    wait(outputs)


def inner_fields(basis, down, up, below, above, ids, heads, rests, hots):
    return pl.pallas_call(
        inner_kernel,
        in_specs=[VMEM] * 11,
        out_specs=[HBM] + [VMEM] * 3,
        scratch_shapes=[
            pltpu.VMEM((4, SNAPS, FIELDS, PER_BRICK), BF16),
            pltpu.SemaphoreType.DMA((4,)),
        ],
        out_shape=[
            jax.ShapeDtypeStruct((SNAPS, FIELDS, BRICKS * PER_BRICK), BF16),
            jax.ShapeDtypeStruct((EXT, 2 * COEFS, CW), BF16),
            jax.ShapeDtypeStruct((2, COEFS, CW), F32),
            jax.ShapeDtypeStruct((ROWS, 4 * COEFS), BF16),
        ],
        compiler_params=params(24),
        cost_estimate=pl.CostEstimate(flops=4_000_000_000, bytes_accessed=14_000_000, transcendentals=0),
        name="inner",
    )(basis, down, up, *below, *above, ids, heads, rests, hots)


def outer_kernel(filled_hbm, whole_ref, ends_ref, below, above, spread_ref, hots, ids, out_hbm, held, out_sems):
    del filled_hbm
    whole = [whole_ref[k] for k in range(EXT)]
    for k, received in ((0, below), (EXT - 1, above)):
        whole[k] = jnp.concatenate(halves(ends_ref[k // CX] + received[...]), axis=0)
    outputs = []
    for i, brick in enumerate(OUTER):
        column = column_of(ids, brick, whole)
        outputs.append(write_brick(brick, column, hots[brick], spread_ref[...], held.at[i], out_hbm, out_sems.at[i]))
    wait(outputs)


def outer_fields(filled, whole, ends, below, above, spread, hots, ids):
    return pl.pallas_call(
        outer_kernel,
        in_specs=[HBM] + [VMEM] * 7,
        out_specs=HBM,
        scratch_shapes=[
            pltpu.VMEM((4, SNAPS, FIELDS, PER_BRICK), BF16),
            pltpu.SemaphoreType.DMA((4,)),
        ],
        out_shape=jax.ShapeDtypeStruct(filled.shape, BF16),
        input_output_aliases={0: 0},
        compiler_params=params(32),
        name="outer",
    )(filled, whole, ends, below, above, spread, hots, ids)


def on_device(atom_values, atom_cell, brick_column):
    count = lax.axis_size("gx")
    to_lower = [((i + 1) % count, i) for i in range(count)]
    to_upper = [(i, (i + 1) % count) for i in range(count)]
    columns = jnp.pad(brick_column.reshape(1, BRICKS), ((0, 7), (0, 128 - BRICKS)))
    ids = jnp.concatenate([atom_cell.reshape(BRICKS * LANES, 128), columns], axis=0)
    below, above, totals, extra = [], [], [], []
    for part in range(2):
        low, high, total, *extra = face_sums(part, atom_values, ids)
        above.append(lax.ppermute(low, "gx", to_lower))
        below.append(lax.ppermute(high, "gx", to_upper))
        totals.append(total)
    heads, rests, hots, gram = local_sums(atom_values, ids, brick_column, *totals, *extra)
    mine, other = add_over_devices(*packed_gram(gram, heads, rests, below, above))
    basis, down, up = basis_and_faces(mine, other, heads, rests)
    end_above = lax.ppermute(down, "gx", to_lower)
    end_below = lax.ppermute(up, "gx", to_upper)
    filled, whole, ends, spread = inner_fields(basis, down, up, below, above, ids, heads, rests, hots)
    return outer_fields(filled, whole, ends, end_below, end_above, spread, hots, ids)


def solution(mesh):
    in_specs = (P(None, None, ("gx", "gz")), P(("gx", "gz")), P(("gx", "gz")))
    out_specs = P(None, None, ("gx", "gz"))
    return jax.shard_map(on_device, mesh=mesh, in_specs=in_specs, out_specs=out_specs, check_vma=False)
```

```python
import functools
import math

import jax
import jax.numpy as jnp
from jax import lax
from jax.experimental import pallas as pl
from jax.experimental.pallas import tpu as pltpu
from jax.sharding import PartitionSpec as P

SNAPS = 160
FIELDS = 4
ROWS = SNAPS * FIELDS
MODES = 8
SWEEPS = 3
CX = 4
EXT = CX + 2
CW = 512
PER_BRICK = 512
BRICKS = 8
COEFS = MODES * FIELDS
PART = SNAPS // 2
PART_ROWS = PART * FIELDS
WIRE = PART_ROWS + 16
TOP = 32767.0
STEPS = 8 / math.log(2)
SPLIT = 128
TAIL = SNAPS - SPLIT
LANES = CW // 128
F32 = jnp.float32
BF16 = jnp.bfloat16
NT = (((1,), (1,)), ((), ()))
TN = (((0,), (0,)), ((), ()))


def params(mib):
    return pltpu.CompilerParams(vmem_limit_bytes=mib * 1024 * 1024)


def dot_nt(a, b):
    return lax.dot_general(a, b, NT, preferred_element_type=F32)


def dot(a, b):
    return jnp.dot(a, b, preferred_element_type=F32)


def exact_dot(a, b):
    return jnp.dot(a, b, precision=lax.Precision.HIGHEST, preferred_element_type=F32)


def cell_hot(cells, brick, keep=None):
    ids = lax.broadcasted_iota(jnp.int32, (CW, 128), 0)
    tiles = []
    for t in range(LANES):
        row = cells[brick * LANES + t : brick * LANES + t + 1, :]
        if keep is not None:
            row = jnp.where(keep, row, -1)
        tiles.append((ids == row).astype(F32).astype(BF16))
    return jnp.concatenate(tiles, axis=1)


def halves(x):
    head = x.astype(BF16)
    return head, (x - head.astype(F32)).astype(BF16)


def one_field(total, field):
    rows = pl.ds(field, total.shape[1] // FIELDS, stride=FIELDS)
    return jnp.concatenate([total[t, rows, :] for t in range(LANES)], axis=1)


def brick_copy(values_hbm, held, sems, brick, slot):
    source = values_hbm.at[:, :, pl.ds(brick * PER_BRICK, PER_BRICK)]
    return pltpu.make_async_copy(source, held.at[slot], sems.at[slot])


def encode(total, out_ref):
    for t in range(LANES):
        lanes = slice(t * 128, (t + 1) * 128)
        most = jnp.max(jnp.abs(total[t]), axis=0, keepdims=True)
        code = jnp.ceil(jnp.log(jnp.maximum(most, 1e-30)) * STEPS)
        scale = jnp.exp(code * (-1 / STEPS)) * TOP
        for f in range(FIELDS):
            steps = jnp.round(total[t, pl.ds(f, PART, stride=FIELDS), :] * scale)
            out_ref[f * PART : (f + 1) * PART, lanes] = jnp.clip(steps, -TOP, TOP).astype(jnp.int32).astype(jnp.int16)
        out_ref[PART_ROWS:, lanes] = jnp.broadcast_to(code, (WIRE - PART_ROWS, 128)).astype(jnp.int32).astype(jnp.int16)


def wire_steps(wire, rows):
    return wire[rows, :].astype(jnp.int32).astype(F32)


def wire_scale(wire):
    return jnp.exp(wire_steps(wire, slice(PART_ROWS, WIRE))[:1] * (1 / STEPS)) * (1 / TOP)


def start(copies):
    for copy in copies:
        copy.start()


def wait(copies):
    for copy in copies:
        copy.wait()


def column_id(ids, brick):
    return ids[BRICKS * LANES : BRICKS * LANES + 1, brick : brick + 1]


INNER = range(2, BRICKS - 2)
OUTER = (0, 1, BRICKS - 2, BRICKS - 1)
HBM = pl.BlockSpec(memory_space=pltpu.HBM)
VMEM = pl.BlockSpec(memory_space=pltpu.VMEM)
SMEM = pl.BlockSpec(memory_space=pltpu.SMEM)


def faces_kernel(part, values_hbm, ids_ref, low_ref, high_ref, total, *rest):
    bricks = (0, 1, BRICKS - 2, BRICKS - 1)
    targets = ((0, low_ref), (EXT - 1, high_ref))
    held, sems = rest[-2:]
    copies = []
    for slot, brick in enumerate(bricks):
        source = values_hbm.at[pl.ds(part * PART, PART), :, pl.ds(brick * PER_BRICK, PER_BRICK)]
        copies.append(pltpu.make_async_copy(source, held.at[slot], sems.at[slot]))
    start(copies)
    later = []
    if part:
        passed, outer_hots, later_sems = rest[:3]
        later = [brick_copy(values_hbm, passed, later_sems, brick, i) for i, brick in enumerate(INNER)]
        start(later)
    hots = [
        cell_hot(ids_ref, brick, column_id(ids_ref, brick) == targets[slot // 2][0]) for slot, brick in enumerate(bricks)
    ]
    if part:
        outer_hots[0] = hots[0]
        outer_hots[1] = hots[3]
    for i in range(2):
        sums = None
        for slot in (2 * i, 2 * i + 1):
            copies[slot].wait()
            part_sums = dot_nt(held[slot].reshape(PART_ROWS, PER_BRICK), hots[slot])
            sums = part_sums if sums is None else sums + part_sums
        for t in range(LANES):
            total[i, t] = sums[:, t * 128 : (t + 1) * 128]
        encode(total.at[i], targets[i][1])
    wait(later)


def face_sums(part, values, ids):
    shape = jax.ShapeDtypeStruct((WIRE, CW), jnp.int16)
    later_shapes = [
        jax.ShapeDtypeStruct((len(INNER), SNAPS, FIELDS, PER_BRICK), BF16),
        jax.ShapeDtypeStruct((2, CW, PER_BRICK), BF16),
    ]
    later_scratch = [pltpu.SemaphoreType.DMA((len(INNER),))]
    return pl.pallas_call(
        functools.partial(faces_kernel, part),
        in_specs=[HBM, VMEM],
        out_specs=[VMEM] * (3 + 2 * part),
        scratch_shapes=later_scratch * part
        + [
            pltpu.VMEM((4, PART, FIELDS, PER_BRICK), BF16),
            pltpu.SemaphoreType.DMA((4,)),
        ],
        out_shape=[shape, shape, jax.ShapeDtypeStruct((2, LANES, PART_ROWS, 128), F32)] + later_shapes * part,
        compiler_params=params((51, 46)[part]),
        cost_estimate=pl.CostEstimate(flops=1_400_000_000, bytes_accessed=4_000_000, transcendentals=0),
        name="faces",
    )(values, ids)


def local_kernel(
    column_ref, values_hbm, ids_ref, early, late, inner, outer_hots, heads, rests, hots, gram_ref, held, total, sems
):
    edges = (1, BRICKS - 2)
    copies = [brick_copy(values_hbm, held, sems, brick, i) for i, brick in enumerate(edges)]
    start(copies)
    total[...] = jnp.zeros_like(total)
    hots[0] = outer_hots[0]
    hots[BRICKS - 1] = outer_hots[1]
    for brick in tuple(INNER) + edges:
        hot = cell_hot(ids_ref, brick)
        hots[brick] = hot
        if brick in INNER:
            values = inner[brick - 2]
        else:
            copies[edges.index(brick)].wait()
            values = held[edges.index(brick)]
        sums = dot_nt(values.reshape(ROWS, PER_BRICK), hot)
        column = column_ref[brick]
        place = jnp.where(column == EXT - 1, 0, column)
        for t in range(LANES):
            total[place, t] += sums[:, t * 128 : (t + 1) * 128]
    same = jnp.zeros((SNAPS, SNAPS), F32)
    mixed = jnp.zeros((SNAPS, SNAPS), F32)
    for k in range(EXT):
        for f in range(FIELDS):
            rows = slice(f * SNAPS, (f + 1) * SNAPS)
            if k in (0, EXT - 1):
                sums = jnp.concatenate([one_field(early.at[k // CX], f), one_field(late.at[k // CX], f)], axis=0)
            else:
                sums = one_field(total.at[k], f)
            head, rest = halves(sums)
            heads[k, rows, :] = head
            rests[k, rows, :] = rest
        for f in range(FIELDS):
            rows = slice(f * SNAPS, (f + 1) * SNAPS)
            same += dot_nt(heads[k, rows, :], heads[k, rows, :])
            mixed += dot_nt(heads[k, rows, :], rests[k, rows, :])
    gram_ref[...] = same + mixed + mixed.T


def local_sums(values, ids, columns, early, late, inner, outer_hots):
    half = jax.ShapeDtypeStruct((EXT, ROWS, CW), BF16)
    return pl.pallas_call(
        local_kernel,
        in_specs=[SMEM, HBM] + [VMEM] * 5,
        out_specs=[VMEM] * 4,
        scratch_shapes=[
            pltpu.VMEM((2, SNAPS, FIELDS, PER_BRICK), BF16),
            pltpu.VMEM((CX + 1, LANES, ROWS, 128), F32),
            pltpu.SemaphoreType.DMA((2,)),
        ],
        out_shape=[
            half,
            half,
            jax.ShapeDtypeStruct((BRICKS, CW, PER_BRICK), BF16),
            jax.ShapeDtypeStruct((SNAPS, SNAPS), F32),
        ],
        compiler_params=params(36),
        cost_estimate=pl.CostEstimate(flops=6_000_000_000, bytes_accessed=14_000_000, transcendentals=0),
        name="local",
    )(columns, values, ids, early, late, inner, outer_hots)


def pack(gram):
    body = gram[:SPLIT, :SPLIT]
    side = gram[:SPLIT, SPLIT:]
    corner = gram[SPLIT:, SPLIT:]
    t = TAIL
    rows = [
        body[:t],
        jnp.concatenate([side[:t], body[t : 2 * t, t:]], axis=1),
        jnp.concatenate([side[t : 2 * t], side[2 * t : 3 * t], body[2 * t : 3 * t, 2 * t :]], axis=1),
        jnp.concatenate([side[3 * t :], corner, corner, body[3 * t :, 3 * t :]], axis=1),
    ]
    return jnp.concatenate(rows, axis=0)


def unpack(packed):
    t = TAIL
    row = lax.broadcasted_iota(jnp.int32, (SPLIT, SPLIT), 0) // t
    col = lax.broadcasted_iota(jnp.int32, (SPLIT, SPLIT), 1) // t
    above = jnp.where(col > row, packed, 0.0)
    body = jnp.where(col == row, packed, 0.0) + above + above.T
    side = jnp.concatenate(
        [packed[t : 2 * t, :t], packed[2 * t : 3 * t, :t], packed[2 * t : 3 * t, t : 2 * t], packed[3 * t :, :t]], axis=0
    )
    corner = packed[3 * t :, t : 2 * t]
    top = jnp.concatenate([body, side], axis=1)
    padded = jnp.concatenate([side, jnp.zeros((SPLIT, SPLIT - t), F32)], axis=1)
    bottom = jnp.concatenate([padded.T[:t], corner], axis=1)
    return jnp.concatenate([top, bottom], axis=0)


def cross_terms(gram, heads, rests, early, late):
    cross = jnp.zeros((SNAPS, SNAPS), F32)
    scales = [wire_scale(wire) for wire in (early, late)]
    for f in range(FIELDS):
        part = slice(f * PART, (f + 1) * PART)
        steps = [wire_steps(wire, part) * scale for wire, scale in zip((early, late), scales)]
        head, rest = halves(jnp.concatenate(steps, axis=0))
        rows = slice(f * SNAPS, (f + 1) * SNAPS)
        own = heads[rows, :]
        pair = dot_nt(jnp.concatenate([own, rests[rows, :]], axis=0), head)
        cross += pair[:SNAPS] + pair[SNAPS:] + dot_nt(own, rest)
    return gram + cross + cross.T


def below_kernel(gram_ref, heads, rests, early, late, out_ref):
    out_ref[...] = cross_terms(gram_ref[...], heads.at[1], rests.at[1], early, late)


def above_kernel(gram_ref, heads, rests, early, late, mine_ref, other_ref):
    packed = pack(cross_terms(gram_ref[...], heads.at[CX], rests.at[CX], early, late))
    first = on_first_core()
    mine_ref[...] = jnp.where(first, packed[: SPLIT // 2], packed[SPLIT // 2 :])
    other_ref[...] = jnp.where(first, packed[SPLIT // 2 :], packed[: SPLIT // 2])


def packed_gram(gram, heads, rests, below, above):
    common = dict(compiler_params=params(16), cost_estimate=pl.CostEstimate(flops=400_000_000, bytes_accessed=3_000_000, transcendentals=0))
    gram = pl.pallas_call(
        below_kernel,
        in_specs=[VMEM] * 5,
        out_specs=VMEM,
        out_shape=jax.ShapeDtypeStruct((SNAPS, SNAPS), F32),
        name="below",
        **common,
    )(gram, heads, rests, *below)
    return pl.pallas_call(
        above_kernel,
        in_specs=[VMEM] * 5,
        out_specs=[VMEM] * 2,
        out_shape=[jax.ShapeDtypeStruct((SPLIT // 2, SPLIT), F32)] * 2,
        name="above",
        **common,
    )(gram, heads, rests, *above)


def on_first_core():
    return lax.rem(lax.axis_index("gz"), 2) == 0


def tree_sum(terms):
    while len(terms) > 1:
        terms = [a + b for a, b in zip(terms[::2], terms[1::2])]
    return terms[0]


def terms_kernel(*refs):
    out_ref = refs[-1]
    out_ref[...] = jnp.broadcast_to(tree_sum([ref[...] for ref in refs[:-1]]), out_ref.shape)


def parts_kernel(parts, out_ref):
    out_ref[...] = tree_sum([parts[i] for i in range(parts.shape[0])])


def small_sum(kernel, terms, shape):
    return pl.pallas_call(
        kernel,
        in_specs=[VMEM] * len(terms),
        out_specs=VMEM,
        out_shape=jax.ShapeDtypeStruct(shape, F32),
        compiler_params=params(4),
        name="sum",
    )(*terms)


def add_over_devices(mine, other):
    axes = ("gx", "gz")
    depth = 8
    places = [(a, z, y, c) for a in range(4) for z in range(depth) for y in range(4) for c in range(2)]
    number = {place: i for i, place in enumerate(places)}
    lines = [[number[a, z, y, c] for z in range(depth)] for a in range(4) for y in range(4) for c in range(2)]

    def move(x, target):
        return lax.ppermute(x, axes, [(number[place], number[target(*place)]) for place in places])

    def swap(x):
        return move(x, lambda a, z, y, c: (a, z, y, 1 - c))

    shape = mine.shape
    mine = small_sum(terms_kernel, [mine, swap(other)], shape)
    one, three, two = [move(mine, lambda a, z, y, c, k=k: (a ^ k, z, y, c)) for k in (1, 3, 2)]
    mine = small_sum(terms_kernel, [mine, one, three, two], shape)
    one, three, two = [move(mine, lambda a, z, y, c, k=k: (a, z, y ^ k, c)) for k in (1, 3, 2)]
    copies = small_sum(terms_kernel, [mine, one, three, two], (depth,) + shape)
    parts = lax.all_to_all(copies, axes, 0, 0, axis_index_groups=lines, tiled=True)
    mine = small_sum(parts_kernel, [parts], shape)
    return mine, swap(mine)


def orthonormal(basis):
    inner = lax.dot_general(basis, basis, NT, precision=lax.Precision.HIGHEST, preferred_element_type=F32)
    row = lax.broadcasted_iota(jnp.int32, (MODES, 1), 0)
    columns = [jnp.broadcast_to(inner[:, j : j + 1], (MODES, 128)) for j in range(MODES)]
    wide = jnp.concatenate([basis, jnp.zeros((MODES, 256 - SNAPS), F32)], axis=1)
    parts = [wide[:, :128], wide[:, 128:]]
    scale = jnp.zeros((MODES, 128), F32)
    for j in range(MODES):
        pivot = columns[j][j : j + 1, :]
        scale = jnp.where(row == j, lax.rsqrt(pivot), scale)
        factor = jnp.where(row > j, columns[j] * (1.0 / pivot), 0.0)
        for k in range(j + 1, MODES):
            columns[k] = columns[k] - factor * columns[k][j : j + 1, :]
        parts = [part - factor * part[j : j + 1, :] for part in parts]
    return jnp.concatenate([part * scale for part in parts], axis=1)[:, :SNAPS]


def spread_matrix(basis):
    snap = lax.broadcasted_iota(jnp.int32, (SNAPS, ROWS), 0)
    column = lax.broadcasted_iota(jnp.int32, (SNAPS, ROWS), 1)
    repeat = (snap == column // FIELDS).astype(F32).astype(BF16)
    both = dot(jnp.concatenate(halves(basis), axis=0), repeat)
    field = lax.broadcasted_iota(jnp.int32, (COEFS, ROWS), 0) // MODES
    mine = field == lax.broadcasted_iota(jnp.int32, (COEFS, ROWS), 1) % FIELDS
    head = jnp.where(mine, jnp.concatenate([both[:MODES]] * FIELDS, axis=0), 0.0)
    rest = jnp.where(mine, jnp.concatenate([both[MODES:]] * FIELDS, axis=0), 0.0)
    return jnp.concatenate([head, head, rest, jnp.zeros_like(rest)], axis=0).T.astype(BF16)


def by_field(basis):
    snaps = basis.shape[1]
    tall = jnp.concatenate([jnp.concatenate([basis] * FIELDS, axis=1)] * FIELDS, axis=0)
    row_field = lax.broadcasted_iota(jnp.int32, tall.shape, 0) // MODES
    col_field = lax.broadcasted_iota(jnp.int32, tall.shape, 1) // snaps
    return jnp.concatenate(halves(jnp.where(row_field == col_field, tall, 0.0)), axis=0)


def coefficients(both, head, rest):
    pair = dot(both, head)
    return pair[:COEFS] + pair[COEFS:] + dot(both[:COEFS], rest)


def basis_kernel(mine_ref, other_ref, heads, rests, basis_ref, down_ref, up_ref):
    first = on_first_core()
    mine, other = mine_ref[...], other_ref[...]
    gram = unpack(jnp.concatenate([jnp.where(first, mine, other), jnp.where(first, other, mine)], axis=0))
    basis = gram[:MODES, :]
    for _ in range(SWEEPS):
        basis = orthonormal(exact_dot(basis, gram))
    basis_ref[...] = basis
    both = by_field(basis)
    down_ref[...] = coefficients(both, heads[1], rests[1])
    up_ref[...] = coefficients(both, heads[CX], rests[CX])


def basis_and_faces(mine, other, heads, rests):
    side = jax.ShapeDtypeStruct((COEFS, CW), F32)
    return pl.pallas_call(
        basis_kernel,
        in_specs=[VMEM] * 4,
        out_specs=[VMEM] * 3,
        out_shape=[jax.ShapeDtypeStruct((MODES, SNAPS), F32), side, side],
        compiler_params=params(16),
        name="basis",
    )(mine, other, heads, rests)


def column_of(ids, brick, whole):
    first = {0: 0, 1: 0, BRICKS - 1: EXT - 1}.get(brick, 1)
    last = {0: 0, BRICKS - 2: EXT - 1, BRICKS - 1: EXT - 1}.get(brick, CX)
    mine = whole[first]
    for k in range(first + 1, last + 1):
        mine = jnp.where(column_id(ids, brick) == k, whole[k], mine)
    return mine


def write_brick(brick, column, hot, spread, held, out_hbm, sem):
    picked = dot(column, hot).astype(BF16)
    blank = jnp.zeros((COEFS, PER_BRICK), BF16)
    stacked = jnp.concatenate([picked, picked[:COEFS], blank], axis=0)
    held[...] = dot(spread, stacked).astype(BF16).reshape(SNAPS, FIELDS, PER_BRICK)
    copy = pltpu.make_async_copy(held, out_hbm.at[:, :, pl.ds(brick * PER_BRICK, PER_BRICK)], sem)
    copy.start()
    return copy


def inner_kernel(
    basis_ref, down_ref, up_ref, below_early, below_late, above_early, above_late, ids, heads, rests, hots,
    out_hbm, whole_ref, ends_ref, spread_ref, held, out_sems
):
    both = by_field(basis_ref[...])
    spread_ref[...] = spread_matrix(basis_ref[...])
    whole = [jnp.zeros((2 * COEFS, CW), BF16)] * EXT
    parts = [by_field(basis_ref[...][:, h * PART : (h + 1) * PART]) for h in range(2)]
    for k, mine, wires in ((1, down_ref, (below_early, below_late)), (CX, up_ref, (above_early, above_late))):
        value = mine[...]
        for part, wire in zip(parts, wires):
            value += coefficients(part, *halves(wire_steps(wire, slice(0, PART_ROWS)))) * wire_scale(wire)
        whole[k] = jnp.concatenate(halves(value), axis=0)
    for k in (2, 3):
        whole[k] = jnp.concatenate(halves(coefficients(both, heads[k], rests[k])), axis=0)
    outputs = []
    for i, brick in enumerate(INNER):
        column = column_of(ids, brick, whole)
        outputs.append(write_brick(brick, column, hots[brick], spread_ref[...], held.at[i], out_hbm, out_sems.at[i]))
    for k in range(EXT):
        whole_ref[k] = whole[k]
    for i, k in enumerate((0, EXT - 1)):
        ends_ref[i] = coefficients(both, heads[k], rests[k])
    wait(outputs)


def inner_fields(basis, down, up, below, above, ids, heads, rests, hots):
    return pl.pallas_call(
        inner_kernel,
        in_specs=[VMEM] * 11,
        out_specs=[HBM] + [VMEM] * 3,
        scratch_shapes=[
            pltpu.VMEM((4, SNAPS, FIELDS, PER_BRICK), BF16),
            pltpu.SemaphoreType.DMA((4,)),
        ],
        out_shape=[
            jax.ShapeDtypeStruct((SNAPS, FIELDS, BRICKS * PER_BRICK), BF16),
            jax.ShapeDtypeStruct((EXT, 2 * COEFS, CW), BF16),
            jax.ShapeDtypeStruct((2, COEFS, CW), F32),
            jax.ShapeDtypeStruct((ROWS, 4 * COEFS), BF16),
        ],
        compiler_params=params(24),
        cost_estimate=pl.CostEstimate(flops=4_000_000_000, bytes_accessed=14_000_000, transcendentals=0),
        name="inner",
    )(basis, down, up, *below, *above, ids, heads, rests, hots)


def outer_kernel(filled_hbm, whole_ref, ends_ref, below, above, spread_ref, hots, ids, out_hbm, held, out_sems):
    del filled_hbm
    whole = [whole_ref[k] for k in range(EXT)]
    for k, received in ((0, below), (EXT - 1, above)):
        whole[k] = jnp.concatenate(halves(ends_ref[k // CX] + received[...]), axis=0)
    outputs = []
    for i, brick in enumerate(OUTER):
        column = column_of(ids, brick, whole)
        outputs.append(write_brick(brick, column, hots[brick], spread_ref[...], held.at[i], out_hbm, out_sems.at[i]))
    wait(outputs)


def outer_fields(filled, whole, ends, below, above, spread, hots, ids):
    return pl.pallas_call(
        outer_kernel,
        in_specs=[HBM] + [VMEM] * 7,
        out_specs=HBM,
        scratch_shapes=[
            pltpu.VMEM((4, SNAPS, FIELDS, PER_BRICK), BF16),
            pltpu.SemaphoreType.DMA((4,)),
        ],
        out_shape=jax.ShapeDtypeStruct(filled.shape, BF16),
        input_output_aliases={0: 0},
        compiler_params=params(32),
        name="outer",
    )(filled, whole, ends, below, above, spread, hots, ids)


def on_device(atom_values, atom_cell, brick_column):
    count = lax.axis_size("gx")
    to_lower = [((i + 1) % count, i) for i in range(count)]
    to_upper = [(i, (i + 1) % count) for i in range(count)]
    columns = jnp.pad(brick_column.reshape(1, BRICKS), ((0, 7), (0, 128 - BRICKS)))
    ids = jnp.concatenate([atom_cell.reshape(BRICKS * LANES, 128), columns], axis=0)
    below, above, totals, extra = [], [], [], []
    for part in range(2):
        low, high, total, *extra = face_sums(part, atom_values, ids)
        above.append(lax.ppermute(low, "gx", to_lower))
        below.append(lax.ppermute(high, "gx", to_upper))
        totals.append(total)
    heads, rests, hots, gram = local_sums(atom_values, ids, brick_column, *totals, *extra)
    mine, other = add_over_devices(*packed_gram(gram, heads, rests, below, above))
    basis, down, up = basis_and_faces(mine, other, heads, rests)
    end_above = lax.ppermute(down, "gx", to_lower)
    end_below = lax.ppermute(up, "gx", to_upper)
    filled, whole, ends, spread = inner_fields(basis, down, up, below, above, ids, heads, rests, hots)
    return outer_fields(filled, whole, ends, end_below, end_above, spread, hots, ids)


def solution(mesh):
    in_specs = (P(None, None, ("gx", "gz")), P(("gx", "gz")), P(("gx", "gz")))
    out_specs = P(None, None, ("gx", "gz"))
    return jax.shard_map(on_device, mesh=mesh, in_specs=in_specs, out_specs=out_specs, check_vma=False)
```
